32 devices in a mesh: row: 16 (over z, x, core), col: 2 (over y).
Axes of the slice: x: 2, y: 2, z: 4, core: 2. Of those that a mesh axis runs over, the one named last changes fastest.
Arguments:
- vectors: bfloat16 [8, 32768], P(None, ('row', 'col')), may hold values from -6 to 6
- energies: float32 [32768], P(('row', 'col')), may hold values from 0.5 to 6
- tiles: bfloat16 [32768, 4096], P(('row', 'col')), may hold values from -0.25 to 0.25
- tile_rows: int32 [32768], P(('row', 'col')), may hold values from 0 to 31, as said below
- tile_cols: int32 [32768], P(('row', 'col')), may hold values from 0 to 255
- tile_count: int32 [32], P(('row', 'col')), may hold values from 128 to 1024, as said below
Outputs:
- product: bfloat16 [8, 32768], P(None, ('row', 'col'))
- residual: float32 [8, 32768], P(None, ('row', 'col'))
The draws below stay inside these ranges and needn't reach their ends.
Inputs may be any that keep to these rules, and one draw needn't show every extreme that they name: `tile_count`: every count is at least 128, and some device uses all 1024 slots in every draw; a few devices are full while most use far fewer. `tile_rows`: slots may name the same row and column block more than once; such tiles add.
All inputs are finite; a program needn't handle non-finite values.
Results may differ from the reference program's by a relative error of at most 0.008.
Values may be sent and summed in bfloat16 or wider, within the bound.
No kernel may reach another device: no remote copies, remote signals or barrier semaphores. Data moves between devices by JAX's collectives and lax.ppermute only.
A program may use at most 64 MiB of HBM per device.

```python
import jax
import jax.numpy as jnp
from jax import lax

K = 8
BLK_DEV = 16
TILE_DEV = 1024
NBLK = 512
NBASIS = 32768
SLOTS = 32768
N_ROW = 16
N_COL = 2


def draw_energies(key, part):
    base = 1.0 + 2.0 * jnp.arange(NBASIS, dtype=jnp.float32) / NBASIS
    factor = jnp.exp(jax.random.uniform(key, (NBASIS,), jnp.float32, -0.6, 0.6))
    return jnp.clip(base * factor, 0.5, 6.0)


def draw_tile_count(key, part):
    first = jax.random.fold_in(key, 11)
    second = jax.random.fold_in(key, 23)
    counts = jax.random.randint(first, (N_ROW * N_COL,), TILE_DEV // 8, TILE_DEV // 2 + 1)
    heavy = jax.random.randint(second, (4,), 0, N_ROW * N_COL)
    return counts.at[heavy].set(TILE_DEV).astype(jnp.int32)


def tile_layout(key):
    devices = N_ROW * N_COL
    key_rows = jax.random.fold_in(key, 41)
    key_cols = jax.random.fold_in(key, 43)
    key_own = jax.random.fold_in(key, 47)
    key_pick = jax.random.fold_in(key, 53)
    rows = jax.random.randint(key_rows, (devices, TILE_DEV), 0, N_COL * BLK_DEV)
    cols = jax.random.randint(key_cols, (devices, TILE_DEV), 0, N_ROW * BLK_DEV)
    own_block = jax.random.randint(key_own, (devices, TILE_DEV), 0, BLK_DEV)
    picked = jax.random.randint(key_pick, (devices, TILE_DEV), 0, 4) == 0
    device = jnp.arange(devices, dtype=jnp.int32)[:, None]
    row_index = device // N_COL
    col_index = device % N_COL
    rows = jnp.where(picked, col_index * BLK_DEV + own_block, rows)
    cols = jnp.where(picked, row_index * BLK_DEV + own_block, cols)
    return (rows.reshape(-1).astype(jnp.int32), cols.reshape(-1).astype(jnp.int32))


def draw_tile_rows(key, part):
    rows, cols = tile_layout(key)
    return rows


def draw_tile_cols(key, part):
    rows, cols = tile_layout(key)
    return cols


def draw_tiles(key, part):
    scale = (64.0 * TILE_DEV / BLK_DEV) ** (-0.5)
    key_base = jax.random.fold_in(key, 61)
    key_bias = jax.random.fold_in(key, 67)
    base = jnp.clip(jax.random.normal(key_base, (SLOTS, 64, 64), jnp.float32), -6.0, 6.0)
    bias = jax.random.uniform(key_bias, (SLOTS, 1, 1), jnp.float32, 0.03, 0.08)
    diagonal_mask = (jnp.arange(64)[:, None] == jnp.arange(64)[None, :]).astype(jnp.float32)
    return jnp.clip(scale * base + bias * diagonal_mask[None, :, :], -0.25, 0.25).reshape(SLOTS, 4096).astype(jnp.bfloat16)


def block_scale(stream_key, extent, cuts, least, largest):
    factor_of, own = 1.0, jax.random.fold_in(stream_key, 6)
    for axis_at, parts in cuts:
        draws = jnp.exp(jax.random.uniform(jax.random.fold_in(own, axis_at), (parts,), jnp.float32, least / len(cuts), largest / len(cuts)))
        factor_of = factor_of * jnp.repeat(draws, extent[axis_at] // parts).reshape([-1 if axis == axis_at else 1 for axis in range(len(extent))])
    return factor_of


def normal_values(rng, dims, scale, bound, cuts=(), kind=jnp.bfloat16):
    result = jax.random.normal(rng, dims, jnp.float32) * scale
    if len(cuts) > 0:
        result = block_scale(rng, dims, cuts, -0.22, 0.18) * result
    return jnp.clip(result, min=-bound, max=bound).astype(kind)


def setup_inputs(seed: int = 0) -> dict:
    seeds = jax.random.split(jax.random.key(seed), 7)
    return {
        "vectors": normal_values(seeds[0], (K, NBASIS), 1.0, 6.0, ((1, 32),)),
        "energies": draw_energies(jax.random.fold_in(seeds[6], 71), 0),
        "tiles": draw_tiles(jax.random.fold_in(seeds[6], 71), 0),
        "tile_rows": draw_tile_rows(jax.random.fold_in(seeds[6], 71), 0),
        "tile_cols": draw_tile_cols(jax.random.fold_in(seeds[6], 71), 0),
        "tile_count": draw_tile_count(jax.random.fold_in(seeds[6], 71), 0),
    }


def reference(vectors, energies, tiles, tile_rows, tile_cols, tile_count):
    kvec = vectors.shape[0]
    blocks = vectors.reshape(kvec, NBLK, 64).astype(jnp.float32)
    tiles_dev = tiles.reshape(N_ROW * N_COL, TILE_DEV, 64, 64)
    rows_dev = tile_rows.reshape(N_ROW * N_COL, TILE_DEV)
    cols_dev = tile_cols.reshape(N_ROW * N_COL, TILE_DEV)
    device_ids = jnp.arange(N_ROW * N_COL, dtype=jnp.int32)
    slot_ids = jnp.arange(TILE_DEV, dtype=jnp.int32)

    def one_device(accum, item):
        tile, local_rows, local_cols, count, device = item
        row_index = device // N_COL
        col_index = device % N_COL
        grow = (row_index * N_COL * BLK_DEV + local_rows).astype(jnp.int32)
        gcol = (((local_cols // BLK_DEV) * N_COL + col_index) * BLK_DEV + local_cols % BLK_DEV).astype(jnp.int32)
        gathered = blocks[:, gcol, :]
        prod = jnp.einsum("tji,kti->ktj", tile.astype(jnp.float32), gathered, precision=lax.Precision.HIGHEST)
        live = (slot_ids < count).astype(jnp.float32)
        prod = prod * live[None, :, None]
        return accum.at[:, grow, :].add(prod), None

    start = jnp.zeros((kvec, NBLK, 64), jnp.float32)
    off, _ = lax.scan(one_device, start, (tiles_dev, rows_dev, cols_dev, tile_count, device_ids))
    vec32 = vectors.astype(jnp.float32)
    whole = energies[None, :] * vec32 + off.reshape(kvec, NBASIS)
    gram = jnp.einsum("an,bn->ab", vec32, whole, precision=lax.Precision.HIGHEST) / NBASIS
    residual = whole - jnp.einsum("ab,an->bn", gram, vec32, precision=lax.Precision.HIGHEST)
    return whole.astype(jnp.bfloat16), residual
```

```python
import functools
import math

import jax
import jax.numpy as jnp
from jax import lax
from jax.experimental import pallas as pl
from jax.experimental.pallas import tpu as pltpu
from jax.sharding import PartitionSpec as P

LANES = 128
SUB = 8
CHUNK = 64

NT = (((1,), (1,)), ((), ()))


def tile_kernel(
    n_col, side, rows_s, cols_s, info_s, gath, seg, ener, tiles,
    own_ref, send_ref, terms_ref, buf, table, picked, part, sems, *acc,
):
    n_row, kvec, own = gath.shape
    slots = tiles.shape[0]
    blk_own = own // side
    per = LANES // side
    chunks = slots // CHUNK
    n_chunk = tiles.shape[1] // LANES
    count = info_s[0]
    my_col = info_s[1]

    def tile_copy(ch):
        span = pl.ds(pl.multiple_of(ch * CHUNK, CHUNK), CHUNK)
        return pltpu.make_async_copy(tiles.at[span], buf.at[span], sems.at[ch])

    used = (count + CHUNK - 1) // CHUNK

    def start(ch, carry):
        tile_copy(ch).start()
        return carry

    lax.fori_loop(0, used, start, 0)

    lane = lax.broadcasted_iota(jnp.int32, (kvec, LANES), 1)
    low = lane < side
    zero = jnp.zeros((kvec, LANES), jnp.float32)

    def fill(r, carry):
        for p in range(own // LANES):
            x = gath[r, :, p * LANES:(p + 1) * LANES].astype(jnp.float32)
            y = pltpu.roll(x, side, 1)
            at = r * blk_own + p * per
            even = jnp.concatenate([jnp.where(low, x, zero), jnp.where(low, zero, y)], axis=0)
            odd = jnp.concatenate([jnp.where(low, y, zero), jnp.where(low, zero, x)], axis=0)
            table[at] = even.astype(jnp.bfloat16)
            table[at + 1] = odd.astype(jnp.bfloat16)
        return carry

    lax.fori_loop(0, n_row, fill, 0)
    table[n_row * blk_own] = jnp.zeros((per * kvec, LANES), jnp.bfloat16)

    n_seg = acc[0].shape[0]

    def clear(r, carry):
        for a in acc:
            a[r] = jnp.zeros(a.shape[1:], jnp.float32)
        return carry

    lax.fori_loop(0, n_seg, clear, 0)

    rows_of = per * kvec

    def one_chunk(ch, carry):
        tile_copy(ch).wait()

        def pair(q, inner):
            base = pl.multiple_of(ch * CHUNK + q * 2 * SUB, 2 * SUB)
            x = buf[pl.ds(base, 2 * SUB), :].astype(jnp.float32)
            for h in range(2):
                xh = x[h * SUB:(h + 1) * SUB]
                w = jnp.concatenate(
                    [xh[:, c * LANES:(c + 1) * LANES] for c in range(n_chunk)], axis=0
                ).astype(jnp.bfloat16)
                left = jnp.concatenate(
                    [table[cols_s[base + h * SUB + t]] for t in range(SUB)], axis=0
                )
                out = lax.dot_general(left, w, NT, preferred_element_type=jnp.float32)
                for t in range(SUB):
                    r = rows_s[base + h * SUB + t]
                    acc[t][r] += out[t * rows_of:(t + 1) * rows_of]
            return inner

        lax.fori_loop(0, CHUNK // (2 * SUB), pair, 0)
        return carry

    lax.fori_loop(0, used, one_chunk, 0)

    width = n_chunk * SUB
    lane_w = lax.broadcasted_iota(jnp.int32, (rows_of, width), 1)

    def pick(m, carry):
        pieces = []
        for par in range(per):
            total = jnp.zeros((rows_of, width), jnp.float32)
            for t in range(SUB):
                total = jnp.where(lane_w % SUB == t, acc[t][m * per + par], total)
            for jp in range(per):
                pieces.append(total[jp * kvec:(jp + 1) * kvec])
        a = jnp.concatenate(pieces, axis=1)
        hi = a.astype(jnp.bfloat16).astype(jnp.float32)
        both = jnp.concatenate([hi, a - hi], axis=0).astype(jnp.bfloat16)
        picked[pl.ds(pl.multiple_of(m * 2 * kvec, 2 * kvec), 2 * kvec), :] = both
        return carry

    pairs = n_seg // per
    lax.fori_loop(0, pairs, pick, 0)

    depth = per * per * width
    k_id = lax.broadcasted_iota(jnp.int32, (depth, LANES), 0)
    n_id = lax.broadcasted_iota(jnp.int32, (depth, LANES), 1)
    par_id = k_id // (per * width)
    jp_id = (k_id // width) % per
    c_id = (k_id % width) // SUB
    select = (n_id == side * par_id + per * c_id + jp_id).astype(jnp.float32).astype(jnp.bfloat16)
    spread = jnp.dot(picked[...], select, preferred_element_type=jnp.float32)
    for m in range(pairs):
        at = m * 2 * kvec
        row = spread[at:at + kvec] + spread[at + kvec:at + 2 * kvec]
        c, lane0 = divmod(m * LANES, own)
        part[c, :, lane0:lane0 + LANES] = row

    mine = seg[my_col].astype(jnp.float32)
    base = part[my_col] + ener[...] * mine
    part[my_col] = base
    own_ref[...] = base
    for s in range(1, n_col):
        send_ref[s - 1] = part[(my_col + s) % n_col].astype(jnp.bfloat16)
    terms = jnp.zeros((kvec, kvec), jnp.float32)
    for c in range(n_col):
        terms = terms + lax.dot_general(
            seg[c].astype(jnp.float32), part[c], NT,
            precision=lax.Precision.HIGHEST, preferred_element_type=jnp.float32,
        )
    terms_ref[...] = terms


def tile_work(n_col, rows, cols, info, gath, seg, ener, tiles):
    n_row, kvec, own = gath.shape
    slots, area = tiles.shape
    side = math.isqrt(area)
    per = LANES // side
    blk_own = own // side
    n_seg = n_col * blk_own
    width = area // LANES * SUB
    vmem = pl.BlockSpec(memory_space=pltpu.VMEM)
    smem = pl.BlockSpec(memory_space=pltpu.SMEM)
    return pl.pallas_call(
        functools.partial(tile_kernel, n_col, side),
        out_shape=(
            jax.ShapeDtypeStruct((kvec, own), jnp.float32),
            jax.ShapeDtypeStruct((n_col - 1, kvec, own), jnp.bfloat16),
            jax.ShapeDtypeStruct((kvec, kvec), jnp.float32),
        ),
        in_specs=[smem, smem, smem, vmem, vmem, vmem, pl.BlockSpec(memory_space=pl.ANY)],
        out_specs=(vmem, vmem, vmem),
        scratch_shapes=[
            pltpu.VMEM((slots, area), jnp.bfloat16),
            pltpu.VMEM((n_row * blk_own + 1, per * kvec, LANES), jnp.bfloat16),
            pltpu.VMEM((n_seg // per * 2 * kvec, per * per * width), jnp.bfloat16),
            pltpu.VMEM((n_col, kvec, own), jnp.float32),
            pltpu.SemaphoreType.DMA((slots // CHUNK,)),
        ] + [pltpu.VMEM((n_seg, per * kvec, width), jnp.float32)] * SUB,
        compiler_params=pltpu.CompilerParams(vmem_limit_bytes=48 * 2**20),
        cost_estimate=pl.CostEstimate(
            flops=2 * slots * area * kvec, bytes_accessed=2 * slots * area, transcendentals=0
        ),
        name="tile_work",
    )(rows, cols, info, gath, seg, ener, tiles)


def sum_everywhere(x, axes, size):
    if size & (size - 1):
        return lax.psum(x, axes)
    step = 1
    while step < size:
        x = x + lax.ppermute(x, axes, [(i, i ^ step) for i in range(size)])
        step *= 2
    return x


def per_device(vectors, energies, tiles, tile_rows, tile_cols, tile_count):
    kvec, own = vectors.shape
    n_row = lax.axis_size("row")
    n_col = lax.axis_size("col")
    slots, area = tiles.shape
    side = math.isqrt(area)
    n_blocks = n_row * (own // side)
    gath = lax.all_gather(vectors, "row", axis=0)
    seg = lax.all_gather(vectors, "col", axis=0)
    live = jnp.arange(slots, dtype=jnp.int32) < tile_count[0]
    cols = jnp.where(live, tile_cols, n_blocks)
    info = jnp.stack([tile_count[0], lax.axis_index("col").astype(jnp.int32)])
    base, send, terms = tile_work(n_col, tile_rows, cols, info, gath, seg, energies[None, :], tiles)
    gram = sum_everywhere(terms, ("row", "col"), n_row * n_col) / (n_row * n_col * own)
    whole = base
    for s in range(1, n_col):
        got = lax.ppermute(send[s - 1], "col", [(c, (c + s) % n_col) for c in range(n_col)])
        whole = whole + got.astype(jnp.float32)
    vec32 = vectors.astype(jnp.float32)
    residual = whole - jnp.einsum("ab,an->bn", gram, vec32, precision=lax.Precision.HIGHEST)
    return (whole.astype(jnp.bfloat16), residual)


def solution(mesh):
    in_specs = (
        P(None, ("row", "col")),
        P(("row", "col")),
        P(("row", "col"), None),
        P(("row", "col")),
        P(("row", "col")),
        P(("row", "col")),
    )
    out_specs = (P(None, ("row", "col")), P(None, ("row", "col")))
    return jax.shard_map(
        per_device, mesh=mesh, in_specs=in_specs, out_specs=out_specs, check_vma=False
    )
```

```python
import functools
import math

import jax
import jax.numpy as jnp
from jax import lax
from jax.experimental import pallas as pl
from jax.experimental.pallas import tpu as pltpu
from jax.sharding import PartitionSpec as P

LANES = 128
SUB = 8
CHUNK = 64
WIDEST = 32

NT = (((1,), (1,)), ((), ()))


def tile_kernel(
    n_row, n_col, side, rows_s, cols_s, count_s, ener, tiles, *refs,
):
    gath, refs = refs[:n_row], refs[n_row:]
    seg, refs = refs[:n_col], refs[n_col:]
    own_ref, send_ref, terms_ref, buf, table, picked, select, part, sems, *acc = refs
    kvec, own = gath[0].shape
    slots = tiles.shape[0]
    blk_own = own // side
    per = LANES // side
    n_chunk = tiles.shape[1] // LANES
    count = count_s[0]
    my_row = lax.axis_index("row")
    my_col = lax.axis_index("col")

    def tile_copy(ch):
        span = pl.ds(pl.multiple_of(ch * CHUNK, CHUNK), CHUNK)
        return pltpu.make_async_copy(tiles.at[span], buf.at[span], sems.at[ch])

    used = (count + CHUNK - 1) // CHUNK

    def start(ch, carry):
        tile_copy(ch).start()
        return carry

    lax.fori_loop(0, used, start, 0)

    lane = lax.broadcasted_iota(jnp.int32, (kvec, LANES), 1)
    low = lane < side
    zero = jnp.zeros((kvec, LANES), jnp.float32)

    for s in range(n_row):
        first = lax.rem(my_row + (n_row - s), n_row) * blk_own
        for p in range(own // LANES):
            x = gath[s][:, p * LANES:(p + 1) * LANES].astype(jnp.float32)
            y = pltpu.roll(x, side, 1)
            at = first + p * per
            even = jnp.concatenate([jnp.where(low, x, zero), jnp.where(low, zero, y)], axis=0)
            odd = jnp.concatenate([jnp.where(low, y, zero), jnp.where(low, zero, x)], axis=0)
            table[at] = even.astype(jnp.bfloat16)
            table[at + 1] = odd.astype(jnp.bfloat16)
    n_blocks = n_row * blk_own
    table[n_blocks] = jnp.zeros((per * kvec, LANES), jnp.bfloat16)

    n_seg = acc[0].shape[0]
    width = n_chunk * SUB
    depth = per * per * width

    def clear(r, carry):
        for a in acc:
            a[r] = jnp.zeros(a.shape[1:], jnp.float32)
        return carry

    lax.fori_loop(0, n_seg, clear, 0)

    k_id = lax.broadcasted_iota(jnp.int32, (width, LANES), 0)
    n_id = lax.broadcasted_iota(jnp.int32, (width, LANES), 1)
    base_id = n_id - per * (k_id // SUB)
    for par in range(per):
        for jp in range(per):
            at = (par * per + jp) * width
            hit = (base_id == side * par + jp).astype(jnp.float32)
            select[at:at + width, :] = hit.astype(jnp.bfloat16)

    rows_of = per * kvec

    def product(base, half, x):
        xh = x[half * SUB:(half + 1) * SUB]
        w = jnp.concatenate(
            [xh[:, c * LANES:(c + 1) * LANES] for c in range(n_chunk)], axis=0
        ).astype(jnp.bfloat16)
        entries = []
        for t in range(SUB):
            slot = base + half * SUB + t
            entries.append(table[jnp.where(slot < count, cols_s[slot], n_blocks)])
        left = jnp.concatenate(entries, axis=0)
        return lax.dot_general(left, w, NT, preferred_element_type=jnp.float32)

    def accumulate(at, out):
        for t in range(SUB):
            r = rows_s[at + t]
            acc[t][r] += out[t * rows_of:(t + 1) * rows_of]

    def one_chunk(ch, carry):
        tile_copy(ch).wait()
        waiting = None
        for q in range(CHUNK // (2 * SUB)):
            base = pl.multiple_of(ch * CHUNK + q * 2 * SUB, 2 * SUB)
            x = buf[pl.ds(base, 2 * SUB), :].astype(jnp.float32)
            for half in range(2):
                out = product(base, half, x)
                if waiting is not None:
                    accumulate(*waiting)
                waiting = (base + half * SUB, out)
        accumulate(*waiting)
        return carry

    lax.fori_loop(0, used, one_chunk, 0)

    lane_w = lax.broadcasted_iota(jnp.int32, (rows_of, width), 1) % SUB
    pairs = n_seg // per

    def pick(m, carry):
        pieces = []
        for par in range(per):
            total = jnp.zeros((rows_of, width), jnp.float32)
            for t in range(SUB):
                total = jnp.where(lane_w == t, acc[t][m * per + par], total)
            for jp in range(per):
                pieces.append(total[jp * kvec:(jp + 1) * kvec])
        a = jnp.concatenate(pieces, axis=1)
        hi = a.astype(jnp.bfloat16).astype(jnp.float32)
        both = jnp.concatenate([hi, a - hi], axis=0).astype(jnp.bfloat16)
        picked[pl.ds(pl.multiple_of(m * 2 * kvec, 2 * kvec), 2 * kvec), :] = both
        return carry

    lax.fori_loop(0, pairs, pick, 0)

    spread = jnp.dot(picked[...], select[...], preferred_element_type=jnp.float32)
    for m in range(pairs):
        at = m * 2 * kvec
        row = spread[at:at + kvec] + spread[at + kvec:at + 2 * kvec]
        c, lane0 = divmod(m * LANES, own)
        part[c, :, lane0:lane0 + LANES] = row

    part[my_col] += ener[...] * seg[0][...].astype(jnp.float32)
    own_ref[...] = part[my_col]
    terms = jnp.zeros((kvec, kvec), jnp.float32)
    for s in range(n_col):
        share = part[lax.rem(my_col + s, n_col)]
        if s > 0:
            send_ref[s - 1] = share.astype(jnp.bfloat16)
        terms = terms + lax.dot_general(
            seg[(n_col - s) % n_col][...].astype(jnp.float32), share, NT,
            precision=lax.Precision.HIGHEST, preferred_element_type=jnp.float32,
        )
    terms_ref[...] = terms


def tile_work(rows, cols, count, gath, seg, ener, tiles):
    n_row, n_col = len(gath), len(seg)
    kvec, own = gath[0].shape
    slots, area = tiles.shape
    side = math.isqrt(area)
    per = LANES // side
    blk_own = own // side
    n_seg = n_col * blk_own
    width = area // LANES * SUB
    vmem = pl.BlockSpec(memory_space=pltpu.VMEM)
    smem = pl.BlockSpec(memory_space=pltpu.SMEM)
    return pl.pallas_call(
        functools.partial(tile_kernel, n_row, n_col, side),
        out_shape=(
            jax.ShapeDtypeStruct((kvec, own), jnp.float32),
            jax.ShapeDtypeStruct((n_col - 1, kvec, own), jnp.bfloat16),
            jax.ShapeDtypeStruct((kvec, kvec), jnp.float32),
        ),
        in_specs=[smem, smem, smem, vmem, pl.BlockSpec(memory_space=pl.ANY)]
        + [vmem] * (n_row + n_col),
        out_specs=(vmem, vmem, vmem),
        scratch_shapes=[
            pltpu.VMEM((slots, area), jnp.bfloat16),
            pltpu.VMEM((n_row * blk_own + 1, per * kvec, LANES), jnp.bfloat16),
            pltpu.VMEM((n_seg // per * 2 * kvec, per * per * width), jnp.bfloat16),
            pltpu.VMEM((per * per * width, LANES), jnp.bfloat16),
            pltpu.VMEM((n_col, kvec, own), jnp.float32),
            pltpu.SemaphoreType.DMA((slots // CHUNK,)),
        ] + [pltpu.VMEM((n_seg, per * kvec, width), jnp.float32)] * SUB,
        compiler_params=pltpu.CompilerParams(vmem_limit_bytes=48 * 2**20),
        cost_estimate=pl.CostEstimate(
            flops=2 * slots * area * kvec, bytes_accessed=2 * slots * area, transcendentals=0
        ),
        name="tile_work",
    )(rows, cols, count, ener, tiles, *gath, *seg)


def from_all(x, axes, size, group, stride):
    got = [x]
    for s in range(1, group):
        perm = []
        for i in range(size):
            place = i // stride % group
            perm.append((i, i + ((place + s) % group - place) * stride))
        got.append(lax.ppermute(x, axes, perm))
    return got


def sum_everywhere(x, axes, size):
    stride = 1
    while stride < size:
        group = math.gcd(size // stride, WIDEST)
        if group == 1:
            group = size // stride
        x = sum(from_all(x, axes, size, group, stride))
        stride *= group
    return x


def per_device(vectors, energies, tiles, tile_rows, tile_cols, tile_count):
    kvec, own = vectors.shape
    n_row = lax.axis_size("row")
    n_col = lax.axis_size("col")
    seg = from_all(vectors, "col", n_col, n_col, 1)
    gath = from_all(vectors, "row", n_row, n_row, 1)
    base, send, terms = tile_work(
        tile_rows, tile_cols, tile_count, gath, seg, energies[None, :], tiles
    )
    whole = base
    for s in range(1, n_col):
        got = lax.ppermute(send[s - 1], "col", [(c, (c + s) % n_col) for c in range(n_col)])
        whole = whole + got.astype(jnp.float32)
    gram = sum_everywhere(terms, ("row", "col"), n_row * n_col) / (n_row * n_col * own)
    vec32 = vectors.astype(jnp.float32)
    residual = whole - jnp.einsum("ab,an->bn", gram, vec32, precision=lax.Precision.HIGHEST)
    return (whole.astype(jnp.bfloat16), residual)


def solution(mesh):
    in_specs = (
        P(None, ("row", "col")),
        P(("row", "col")),
        P(("row", "col"), None),
        P(("row", "col")),
        P(("row", "col")),
        P(("row", "col")),
    )
    out_specs = (P(None, ("row", "col")), P(None, ("row", "col")))
    return jax.shard_map(
        per_device, mesh=mesh, in_specs=in_specs, out_specs=out_specs, check_vma=False
    )
```

```python
import functools
import math

import jax
import jax.numpy as jnp
from jax import lax
from jax.experimental import pallas as pl
from jax.experimental.pallas import tpu as pltpu
from jax.sharding import PartitionSpec as P

LANES = 128
SUB = 8
CHUNK = 64

NT = (((1,), (1,)), ((), ()))


def tile_kernel(
    n_col, side, rows_s, cols_s, count_s, ener, tiles, gath, *refs,
):
    seg, refs = refs[:n_col], refs[n_col:]
    own_ref, send_ref, terms_ref, buf, table, picked, select, part, sems, *acc = refs
    n_row, kvec, own = gath.shape
    slots = tiles.shape[0]
    blk_own = own // side
    per = LANES // side
    n_chunk = tiles.shape[1] // LANES
    count = count_s[0]
    my_col = lax.axis_index("col")

    def tile_copy(ch):
        span = pl.ds(pl.multiple_of(ch * CHUNK, CHUNK), CHUNK)
        return pltpu.make_async_copy(tiles.at[span], buf.at[span], sems.at[ch])

    used = (count + CHUNK - 1) // CHUNK

    def start(ch, carry):
        tile_copy(ch).start()
        return carry

    lax.fori_loop(0, used, start, 0)

    lane = lax.broadcasted_iota(jnp.int32, (kvec, LANES), 1)
    low = lane < side
    zero = jnp.zeros((kvec, LANES), jnp.float32)

    for r in range(n_row):
        for p in range(own // LANES):
            x = gath[r, :, p * LANES:(p + 1) * LANES].astype(jnp.float32)
            y = pltpu.roll(x, side, 1)
            at = r * blk_own + p * per
            even = jnp.concatenate([jnp.where(low, x, zero), jnp.where(low, zero, y)], axis=0)
            odd = jnp.concatenate([jnp.where(low, y, zero), jnp.where(low, zero, x)], axis=0)
            table[at] = even.astype(jnp.bfloat16)
            table[at + 1] = odd.astype(jnp.bfloat16)
    n_blocks = n_row * blk_own
    table[n_blocks] = jnp.zeros((per * kvec, LANES), jnp.bfloat16)

    n_seg = acc[0].shape[0]
    width = n_chunk * SUB
    depth = per * per * width

    def clear(r, carry):
        for a in acc:
            a[r] = jnp.zeros(a.shape[1:], jnp.float32)
        return carry

    lax.fori_loop(0, n_seg, clear, 0)

    k_id = lax.broadcasted_iota(jnp.int32, (width, LANES), 0)
    n_id = lax.broadcasted_iota(jnp.int32, (width, LANES), 1)
    base_id = n_id - per * (k_id // SUB)
    for par in range(per):
        for jp in range(per):
            at = (par * per + jp) * width
            hit = (base_id == side * par + jp).astype(jnp.float32)
            select[at:at + width, :] = hit.astype(jnp.bfloat16)

    rows_of = per * kvec

    def product(base, half, x):
        xh = x[half * SUB:(half + 1) * SUB]
        w = jnp.concatenate(
            [xh[:, c * LANES:(c + 1) * LANES] for c in range(n_chunk)], axis=0
        ).astype(jnp.bfloat16)
        entries = []
        for t in range(SUB):
            slot = base + half * SUB + t
            entries.append(table[jnp.where(slot < count, cols_s[slot], n_blocks)])
        left = jnp.concatenate(entries, axis=0)
        return lax.dot_general(left, w, NT, preferred_element_type=jnp.float32)

    def accumulate(at, out):
        for t in range(SUB):
            r = rows_s[at + t]
            acc[t][r] += out[t * rows_of:(t + 1) * rows_of]

    def one_chunk(ch, carry):
        tile_copy(ch).wait()
        waiting = None
        for q in range(CHUNK // (2 * SUB)):
            base = pl.multiple_of(ch * CHUNK + q * 2 * SUB, 2 * SUB)
            x = buf[pl.ds(base, 2 * SUB), :].astype(jnp.float32)
            for half in range(2):
                out = product(base, half, x)
                if waiting is not None:
                    accumulate(*waiting)
                waiting = (base + half * SUB, out)
        accumulate(*waiting)
        return carry

    lax.fori_loop(0, used, one_chunk, 0)

    lane_w = lax.broadcasted_iota(jnp.int32, (rows_of, width), 1) % SUB
    pairs = n_seg // per

    def pick(m, carry):
        pieces = []
        for par in range(per):
            total = jnp.zeros((rows_of, width), jnp.float32)
            for t in range(SUB):
                total = jnp.where(lane_w == t, acc[t][m * per + par], total)
            for jp in range(per):
                pieces.append(total[jp * kvec:(jp + 1) * kvec])
        a = jnp.concatenate(pieces, axis=1)
        hi = a.astype(jnp.bfloat16).astype(jnp.float32)
        both = jnp.concatenate([hi, a - hi], axis=0).astype(jnp.bfloat16)
        picked[pl.ds(pl.multiple_of(m * 2 * kvec, 2 * kvec), 2 * kvec), :] = both
        return carry

    lax.fori_loop(0, pairs, pick, 0)

    spread = jnp.dot(picked[...], select[...], preferred_element_type=jnp.float32)
    for m in range(pairs):
        at = m * 2 * kvec
        row = spread[at:at + kvec] + spread[at + kvec:at + 2 * kvec]
        c, lane0 = divmod(m * LANES, own)
        part[c, :, lane0:lane0 + LANES] = row

    part[my_col] += ener[...] * seg[0][...].astype(jnp.float32)
    own_ref[...] = part[my_col]
    terms = jnp.zeros((kvec, kvec), jnp.float32)
    for s in range(n_col):
        share = part[lax.rem(my_col + s, n_col)]
        if s > 0:
            send_ref[s - 1] = share.astype(jnp.bfloat16)
        terms = terms + lax.dot_general(
            seg[(n_col - s) % n_col][...].astype(jnp.float32), share, NT,
            precision=lax.Precision.HIGHEST, preferred_element_type=jnp.float32,
        )
    terms_ref[...] = terms


def tile_work(rows, cols, count, gath, seg, ener, tiles):
    n_col = len(seg)
    n_row, kvec, own = gath.shape
    slots, area = tiles.shape
    side = math.isqrt(area)
    per = LANES // side
    blk_own = own // side
    n_seg = n_col * blk_own
    width = area // LANES * SUB
    vmem = pl.BlockSpec(memory_space=pltpu.VMEM)
    smem = pl.BlockSpec(memory_space=pltpu.SMEM)
    return pl.pallas_call(
        functools.partial(tile_kernel, n_col, side),
        out_shape=(
            jax.ShapeDtypeStruct((kvec, own), jnp.float32),
            jax.ShapeDtypeStruct((n_col - 1, kvec, own), jnp.bfloat16),
            jax.ShapeDtypeStruct((kvec, kvec), jnp.float32),
        ),
        in_specs=[smem, smem, smem, vmem, pl.BlockSpec(memory_space=pl.ANY)]
        + [vmem] * (1 + n_col),
        out_specs=(vmem, vmem, vmem),
        scratch_shapes=[
            pltpu.VMEM((slots, area), jnp.bfloat16),
            pltpu.VMEM((n_row * blk_own + 1, per * kvec, LANES), jnp.bfloat16),
            pltpu.VMEM((n_seg // per * 2 * kvec, per * per * width), jnp.bfloat16),
            pltpu.VMEM((per * per * width, LANES), jnp.bfloat16),
            pltpu.VMEM((n_col, kvec, own), jnp.float32),
            pltpu.SemaphoreType.DMA((slots // CHUNK,)),
        ] + [pltpu.VMEM((n_seg, per * kvec, width), jnp.float32)] * SUB,
        compiler_params=pltpu.CompilerParams(vmem_limit_bytes=48 * 2**20),
        cost_estimate=pl.CostEstimate(
            flops=2 * slots * area * kvec, bytes_accessed=2 * slots * area, transcendentals=0
        ),
        name="tile_work",
    )(rows, cols, count, ener, tiles, gath, *seg)


def from_all(x, axis, size):
    got = [x]
    for s in range(1, size):
        got.append(lax.ppermute(x, axis, [(i, (i + s) % size) for i in range(size)]))
    return got


def exchange(x, axes, size):
    copies = jnp.broadcast_to(x[None], (size,) + x.shape)
    return lax.all_to_all(copies, axes, 0, 0)


def per_device(vectors, energies, tiles, tile_rows, tile_cols, tile_count):
    kvec, own = vectors.shape
    n_row = lax.axis_size("row")
    n_col = lax.axis_size("col")
    devices = n_row * n_col
    seg = from_all(vectors, "col", n_col)
    gath = exchange(vectors, "row", n_row)
    base, send, terms = tile_work(
        tile_rows, tile_cols, tile_count, gath, seg, energies[None, :], tiles
    )
    whole = base
    for s in range(1, n_col):
        got = lax.ppermute(send[s - 1], "col", [(c, (c + s) % n_col) for c in range(n_col)])
        whole = whole + got.astype(jnp.float32)
    gram = jnp.sum(exchange(terms, ("row", "col"), devices), axis=0) / (devices * own)
    vec32 = vectors.astype(jnp.float32)
    residual = whole - jnp.einsum("ab,an->bn", gram, vec32, precision=lax.Precision.HIGHEST)
    return (whole.astype(jnp.bfloat16), residual)


def solution(mesh):
    in_specs = (
        P(None, ("row", "col")),
        P(("row", "col")),
        P(("row", "col"), None),
        P(("row", "col")),
        P(("row", "col")),
        P(("row", "col")),
    )
    out_specs = (P(None, ("row", "col")), P(None, ("row", "col")))
    return jax.shard_map(
        per_device, mesh=mesh, in_specs=in_specs, out_specs=out_specs, check_vma=False
    )
```

```python
import functools
import math

import jax
import jax.numpy as jnp
from jax import lax
from jax.experimental import pallas as pl
from jax.experimental.pallas import tpu as pltpu
from jax.sharding import Mesh, PartitionSpec as P

LANES = 128
SUB = 8
CHUNK = 64
EARLY = 2

NT = (((1,), (1,)), ((), ()))


def tile_kernel(
    n_core, n_col, side, rows_h, cols_h, count_h, ener_h, tiles, *refs,
):
    gath, refs = refs[:n_core], refs[n_core:]
    seg, refs = refs[:n_col], refs[n_col:]
    (own_ref, send_ref, terms_ref, rows_s, cols_s, count_s, ener,
     buf, table, picked, select, part, sems, small, *acc) = refs
    n_far, kvec, own = gath[0].shape
    slots = tiles.shape[0]
    blk_own = own // side
    per = LANES // side
    n_chunk = tiles.shape[1] // LANES
    my_core = lax.axis_index("core")
    my_col = lax.axis_index("col")

    copies = [
        pltpu.make_async_copy(src, dst, small.at[i])
        for i, (src, dst) in enumerate(
            ((count_h, count_s), (cols_h, cols_s), (rows_h, rows_s), (ener_h, ener))
        )
    ]
    for copy in copies:
        copy.start()

    def tile_copy(ch):
        span = pl.ds(pl.multiple_of(ch * CHUNK, CHUNK), CHUNK)
        return pltpu.make_async_copy(tiles.at[span], buf.at[span], sems.at[ch])

    early = min(EARLY, slots // CHUNK)
    for ch in range(early):
        tile_copy(ch).start()

    lane = lax.broadcasted_iota(jnp.int32, (kvec, LANES), 1)
    low = lane < side
    zero = jnp.zeros((kvec, LANES), jnp.float32)

    for s in range(n_core):
        core = lax.rem(my_core + (n_core - s), n_core)
        for f in range(n_far):
            for p in range(own // LANES):
                x = gath[s][f, :, p * LANES:(p + 1) * LANES].astype(jnp.float32)
                y = pltpu.roll(x, side, 1)
                at = (f * n_core + core) * blk_own + p * per
                even = jnp.concatenate([jnp.where(low, x, zero), jnp.where(low, zero, y)], axis=0)
                odd = jnp.concatenate([jnp.where(low, y, zero), jnp.where(low, zero, x)], axis=0)
                table[at] = even.astype(jnp.bfloat16)
                table[at + 1] = odd.astype(jnp.bfloat16)
    n_blocks = n_far * n_core * blk_own
    table[n_blocks] = jnp.zeros((per * kvec, LANES), jnp.bfloat16)

    for copy in copies:
        copy.wait()
    count = count_s[0]
    used = jnp.maximum((count + CHUNK - 1) // CHUNK, early)

    def start(ch, carry):
        tile_copy(ch).start()
        return carry

    lax.fori_loop(early, used, start, 0)

    n_seg = acc[0].shape[0]
    width = n_chunk * SUB

    def clear(r, carry):
        for a in acc:
            a[r] = jnp.zeros(a.shape[1:], jnp.float32)
        return carry

    lax.fori_loop(0, n_seg, clear, 0)

    k_id = lax.broadcasted_iota(jnp.int32, (width, LANES), 0)
    n_id = lax.broadcasted_iota(jnp.int32, (width, LANES), 1)
    base_id = n_id - per * (k_id // SUB)
    for par in range(per):
        for jp in range(per):
            at = (par * per + jp) * width
            hit = (base_id == side * par + jp).astype(jnp.float32)
            select[at:at + width, :] = hit.astype(jnp.bfloat16)

    rows_of = per * kvec

    def product(base, half, x):
        xh = x[half * SUB:(half + 1) * SUB]
        w = jnp.concatenate(
            [xh[:, c * LANES:(c + 1) * LANES] for c in range(n_chunk)], axis=0
        ).astype(jnp.bfloat16)
        entries = []
        for t in range(SUB):
            slot = base + half * SUB + t
            entries.append(table[jnp.where(slot < count, cols_s[slot], n_blocks)])
        left = jnp.concatenate(entries, axis=0)
        return lax.dot_general(left, w, NT, preferred_element_type=jnp.float32)

    def accumulate(at, out):
        for t in range(SUB):
            r = rows_s[at + t]
            acc[t][r] += out[t * rows_of:(t + 1) * rows_of]

    def one_chunk(ch, carry):
        tile_copy(ch).wait()
        waiting = None
        for q in range(CHUNK // (2 * SUB)):
            base = pl.multiple_of(ch * CHUNK + q * 2 * SUB, 2 * SUB)
            x = buf[pl.ds(base, 2 * SUB), :].astype(jnp.float32)
            for half in range(2):
                out = product(base, half, x)
                if waiting is not None:
                    accumulate(*waiting)
                waiting = (base + half * SUB, out)
        accumulate(*waiting)
        return carry

    lax.fori_loop(0, used, one_chunk, 0)

    lane_w = lax.broadcasted_iota(jnp.int32, (rows_of, width), 1) % SUB
    pairs = n_seg // per

    def pick(m, carry):
        pieces = []
        for par in range(per):
            total = jnp.zeros((rows_of, width), jnp.float32)
            for t in range(SUB):
                total = jnp.where(lane_w == t, acc[t][m * per + par], total)
            for jp in range(per):
                pieces.append(total[jp * kvec:(jp + 1) * kvec])
        a = jnp.concatenate(pieces, axis=1)
        hi = a.astype(jnp.bfloat16).astype(jnp.float32)
        both = jnp.concatenate([hi, a - hi], axis=0).astype(jnp.bfloat16)
        picked[pl.ds(pl.multiple_of(m * 2 * kvec, 2 * kvec), 2 * kvec), :] = both
        return carry

    lax.fori_loop(0, pairs, pick, 0)

    spread = jnp.dot(picked[...], select[...], preferred_element_type=jnp.float32)
    for m in range(pairs):
        at = m * 2 * kvec
        row = spread[at:at + kvec] + spread[at + kvec:at + 2 * kvec]
        c, lane0 = divmod(m * LANES, own)
        part[c, :, lane0:lane0 + LANES] = row

    part[my_col] += ener[...] * seg[0][...].astype(jnp.float32)
    own_ref[...] = part[my_col]
    terms = jnp.zeros((kvec, kvec), jnp.float32)
    for s in range(n_col):
        share = part[lax.rem(my_col + s, n_col)]
        if s > 0:
            send_ref[s - 1] = share.astype(jnp.bfloat16)
        terms = terms + lax.dot_general(
            share, seg[(n_col - s) % n_col][...].astype(jnp.float32), NT,
            precision=lax.Precision.HIGHEST, preferred_element_type=jnp.float32,
        )
    terms_ref[...] = terms


def tile_work(rows, cols, count, gath, seg, ener, tiles):
    n_core, n_col = len(gath), len(seg)
    n_far, kvec, own = gath[0].shape
    slots, area = tiles.shape
    side = math.isqrt(area)
    per = LANES // side
    blk_own = own // side
    n_seg = n_col * blk_own
    width = area // LANES * SUB
    vmem = pl.BlockSpec(memory_space=pltpu.VMEM)
    far_away = pl.BlockSpec(memory_space=pltpu.HBM)
    return pl.pallas_call(
        functools.partial(tile_kernel, n_core, n_col, side),
        out_shape=(
            jax.ShapeDtypeStruct((kvec, own), jnp.float32),
            jax.ShapeDtypeStruct((n_col - 1, kvec, own), jnp.bfloat16),
            jax.ShapeDtypeStruct((kvec, kvec), jnp.float32),
        ),
        in_specs=[far_away] * 5 + [vmem] * (n_core + n_col),
        out_specs=(vmem, vmem, vmem),
        scratch_shapes=[
            pltpu.SMEM((slots,), jnp.int32),
            pltpu.SMEM((slots,), jnp.int32),
            pltpu.SMEM((1,), jnp.int32),
            pltpu.VMEM((1, own), jnp.float32),
            pltpu.VMEM((slots, area), jnp.bfloat16),
            pltpu.VMEM((n_far * n_core * blk_own + 1, per * kvec, LANES), jnp.bfloat16),
            pltpu.VMEM((n_seg // per * 2 * kvec, per * per * width), jnp.bfloat16),
            pltpu.VMEM((per * per * width, LANES), jnp.bfloat16),
            pltpu.VMEM((n_col, kvec, own), jnp.float32),
            pltpu.SemaphoreType.DMA((slots // CHUNK,)),
            pltpu.SemaphoreType.DMA((4,)),
        ] + [pltpu.VMEM((n_seg, per * kvec, width), jnp.float32)] * SUB,
        compiler_params=pltpu.CompilerParams(vmem_limit_bytes=48 * 2**20),
        cost_estimate=pl.CostEstimate(
            flops=2 * slots * area * kvec, bytes_accessed=2 * slots * area, transcendentals=0
        ),
        name="tile_work",
    )(rows, cols, count, ener, tiles, *gath, *seg)


def finish_kernel(scale, base, gram_parts, vec, *refs):
    got, (product, residual) = refs[:-2], refs[-2:]
    whole = base[...]
    for piece in got:
        whole = whole + piece[...].astype(jnp.float32)
    product[...] = whole.astype(jnp.bfloat16)
    gram = gram_parts[0]
    for i in range(1, gram_parts.shape[0]):
        gram = gram + gram_parts[i]
    gram = gram * scale
    vec32 = vec[...].astype(jnp.float32)
    for a in range(vec.shape[0]):
        whole = whole - gram[:, a:a + 1] * vec32[a:a + 1, :]
    residual[...] = whole


def finish(scale, base, gram_parts, vectors, got):
    vmem = pl.BlockSpec(memory_space=pltpu.VMEM)
    return pl.pallas_call(
        functools.partial(finish_kernel, scale),
        out_shape=(
            jax.ShapeDtypeStruct(vectors.shape, jnp.bfloat16),
            jax.ShapeDtypeStruct(vectors.shape, jnp.float32),
        ),
        in_specs=[vmem] * (3 + len(got)),
        out_specs=(vmem, vmem),
        name="finish",
    )(base, gram_parts, vectors, *got)


def from_all(x, axis):
    size = lax.axis_size(axis)
    got = [x]
    for s in range(1, size):
        got.append(lax.ppermute(x, axis, [(i, (i + s) % size) for i in range(size)]))
    return got


def exchange(x, axes):
    copies = jnp.broadcast_to(x[None], (lax.axis_size(axes),) + x.shape)
    return lax.all_to_all(copies, axes, 0, 0)


def per_device(vectors, energies, tiles, tile_rows, tile_cols, tile_count):
    kvec, own = vectors.shape
    n_col = lax.axis_size("col")
    gath = exchange(vectors, "far")
    seg = from_all(vectors, "col")
    gath = from_all(gath, "core")
    base, send, terms = tile_work(
        tile_rows, tile_cols, tile_count, gath, seg, energies[None, :], tiles
    )
    got = [
        lax.ppermute(send[s - 1], "col", [(c, (c + s) % n_col) for c in range(n_col)])
        for s in range(1, n_col)
    ]
    terms = jnp.sum(exchange(terms, ("core", "col")), axis=0)
    gram_parts = exchange(terms, "far")
    states = lax.axis_size(("far", "core", "col")) * own
    return finish(1.0 / states, base, gram_parts, vectors, got)


def solution(mesh):
    n_row, n_col = mesh.devices.shape
    n_core = 2 if n_row % 2 == 0 else 1
    chips = Mesh(
        mesh.devices.reshape(n_row // n_core, n_core, n_col), ("far", "core", "col")
    )
    split = ("far", "core", "col")
    in_specs = (P(None, split), P(split), P(split, None), P(split), P(split), P(split))
    out_specs = (P(None, split), P(None, split))
    return jax.shard_map(
        per_device, mesh=chips, in_specs=in_specs, out_specs=out_specs, check_vma=False
    )
```

```python
import functools
import math

import jax
import jax.numpy as jnp
from jax import lax
from jax.experimental import pallas as pl
from jax.experimental.pallas import tpu as pltpu
from jax.sharding import PartitionSpec as P

LANES = 128
SUB = 8
CHUNK = 64

NT = (((1,), (1,)), ((), ()))


def tile_kernel(
    n_col, side, count_s, rows_h, cols_h, ener_h, tiles, gath, *refs,
):
    seg, refs = refs[:n_col], refs[n_col:]
    (own_ref, send_ref, terms_ref, rows_s, cols_s, ener,
     buf, table, picked, select, part, wide, sems, small, *acc) = refs
    n_row, kvec, own = gath.shape
    slots = tiles.shape[0]
    blk_own = own // side
    per = LANES // side
    n_chunk = tiles.shape[1] // LANES
    my_col = lax.axis_index("col")

    copies = [
        pltpu.make_async_copy(src, dst, small.at[i])
        for i, (src, dst) in enumerate(
            ((cols_h, cols_s), (rows_h, rows_s), (ener_h, ener))
        )
    ]
    for copy in copies:
        copy.start()

    def tile_copy(ch):
        span = pl.ds(pl.multiple_of(ch * CHUNK, CHUNK), CHUNK)
        return pltpu.make_async_copy(tiles.at[span], buf.at[span], sems.at[ch])

    count = count_s[0]
    used = (count + CHUNK - 1) // CHUNK

    def start(ch, carry):
        tile_copy(ch).start()
        return carry

    lax.fori_loop(0, used, start, 0)

    lane = lax.broadcasted_iota(jnp.int32, (kvec, LANES), 1)
    low = lane < side
    zero = jnp.zeros((kvec, LANES), jnp.float32)

    for r in range(n_row):
        for p in range(own // LANES):
            x = gath[r, :, p * LANES:(p + 1) * LANES].astype(jnp.float32)
            y = pltpu.roll(x, side, 1)
            at = r * blk_own + p * per
            even = jnp.concatenate([jnp.where(low, x, zero), jnp.where(low, zero, y)], axis=0)
            odd = jnp.concatenate([jnp.where(low, y, zero), jnp.where(low, zero, x)], axis=0)
            table[at] = even.astype(jnp.bfloat16)
            table[at + 1] = odd.astype(jnp.bfloat16)
    n_blocks = n_row * blk_own
    table[n_blocks] = jnp.zeros((per * kvec, LANES), jnp.bfloat16)

    for copy in copies:
        copy.wait()
    n_seg = acc[0].shape[0]
    width = n_chunk * SUB

    def clear(r, carry):
        for a in acc:
            a[r] = jnp.zeros(a.shape[1:], jnp.float32)
        return carry

    lax.fori_loop(0, n_seg, clear, 0)

    k_id = lax.broadcasted_iota(jnp.int32, (width, LANES), 0)
    n_id = lax.broadcasted_iota(jnp.int32, (width, LANES), 1)
    base_id = n_id - per * (k_id // SUB)
    for par in range(per):
        for jp in range(per):
            at = (par * per + jp) * width
            hit = (base_id == side * par + jp).astype(jnp.float32)
            select[at:at + width, :] = hit.astype(jnp.bfloat16)

    rows_of = per * kvec

    def product(base, half, x):
        xh = x[half * SUB:(half + 1) * SUB]
        w = jnp.concatenate(
            [xh[:, c * LANES:(c + 1) * LANES] for c in range(n_chunk)], axis=0
        ).astype(jnp.bfloat16)
        entries = []
        for t in range(SUB):
            slot = base + half * SUB + t
            entries.append(table[jnp.where(slot < count, cols_s[slot], n_blocks)])
        left = jnp.concatenate(entries, axis=0)
        return lax.dot_general(left, w, NT, preferred_element_type=jnp.float32)

    def accumulate(at, out):
        for t in range(SUB):
            r = rows_s[at + t]
            acc[t][r] += out[t * rows_of:(t + 1) * rows_of]

    def one_chunk(ch, carry):
        tile_copy(ch).wait()
        waiting = None
        for q in range(CHUNK // (2 * SUB)):
            base = pl.multiple_of(ch * CHUNK + q * 2 * SUB, 2 * SUB)
            x = buf[pl.ds(base, 2 * SUB), :].astype(jnp.float32)
            for half in range(2):
                out = product(base, half, x)
                if waiting is not None:
                    accumulate(*waiting)
                waiting = (base + half * SUB, out)
        accumulate(*waiting)
        return carry

    lax.fori_loop(0, used, one_chunk, 0)

    lane_w = lax.broadcasted_iota(jnp.int32, (rows_of, width), 1) % SUB
    pairs = n_seg // per

    def pick(m, carry):
        pieces = []
        for par in range(per):
            total = jnp.zeros((rows_of, width), jnp.float32)
            for t in range(SUB):
                total = jnp.where(lane_w == t, acc[t][m * per + par], total)
            for jp in range(per):
                pieces.append(total[jp * kvec:(jp + 1) * kvec])
        a = jnp.concatenate(pieces, axis=1)
        hi = a.astype(jnp.bfloat16).astype(jnp.float32)
        both = jnp.concatenate([hi, a - hi], axis=0).astype(jnp.bfloat16)
        picked[pl.ds(pl.multiple_of(m * 2 * kvec, 2 * kvec), 2 * kvec), :] = both
        return carry

    lax.fori_loop(0, pairs, pick, 0)

    spread = jnp.dot(picked[...], select[...], preferred_element_type=jnp.float32)
    for m in range(pairs):
        at = m * 2 * kvec
        row = spread[at:at + kvec] + spread[at + kvec:at + 2 * kvec]
        c, lane0 = divmod(m * LANES, own)
        part[c, :, lane0:lane0 + LANES] = row

    part[my_col] += ener[...] * seg[0][...].astype(jnp.float32)
    own_ref[...] = part[my_col]
    terms = jnp.zeros((kvec, kvec), jnp.float32)
    for s in range(n_col):
        share = part[lax.rem(my_col + s, n_col)]
        if s > 0:
            send_ref[s - 1] = share.astype(jnp.bfloat16)
        terms = terms + lax.dot_general(
            share, seg[(n_col - s) % n_col][...].astype(jnp.float32), NT,
            precision=lax.Precision.HIGHEST, preferred_element_type=jnp.float32,
        )
    wide[...] = jnp.zeros(wide.shape, jnp.float32)
    wide[:, :kvec] = terms
    spaced = pltpu.roll(wide[...], 0, 1, stride=kvec, stride_axis=0)
    flat = jnp.sum(spaced, axis=0, keepdims=True)
    for i in range(terms_ref.shape[0]):
        terms_ref[i] = flat


def tile_work(rows, cols, count, gath, seg, ener, tiles):
    n_col = len(seg)
    n_row, kvec, own = gath.shape
    slots, area = tiles.shape
    side = math.isqrt(area)
    per = LANES // side
    blk_own = own // side
    n_seg = n_col * blk_own
    width = area // LANES * SUB
    vmem = pl.BlockSpec(memory_space=pltpu.VMEM)
    far_away = pl.BlockSpec(memory_space=pltpu.HBM)
    return pl.pallas_call(
        functools.partial(tile_kernel, n_col, side),
        out_shape=(
            jax.ShapeDtypeStruct((kvec, own), jnp.float32),
            jax.ShapeDtypeStruct((n_col - 1, kvec, own), jnp.bfloat16),
            jax.ShapeDtypeStruct((n_row * n_col, 1, LANES), jnp.float32),
        ),
        in_specs=[pl.BlockSpec(memory_space=pltpu.SMEM)] + [far_away] * 4 + [vmem] * (1 + n_col),
        out_specs=(vmem, vmem, vmem),
        scratch_shapes=[
            pltpu.SMEM((slots,), jnp.int32),
            pltpu.SMEM((slots,), jnp.int32),
            pltpu.VMEM((1, own), jnp.float32),
            pltpu.VMEM((slots, area), jnp.bfloat16),
            pltpu.VMEM((n_row * blk_own + 1, per * kvec, LANES), jnp.bfloat16),
            pltpu.VMEM((n_seg // per * 2 * kvec, per * per * width), jnp.bfloat16),
            pltpu.VMEM((per * per * width, LANES), jnp.bfloat16),
            pltpu.VMEM((n_col, kvec, own), jnp.float32),
            pltpu.VMEM((kvec, LANES), jnp.float32),
            pltpu.SemaphoreType.DMA((slots // CHUNK,)),
            pltpu.SemaphoreType.DMA((3,)),
        ] + [pltpu.VMEM((n_seg, per * kvec, width), jnp.float32)] * SUB,
        compiler_params=pltpu.CompilerParams(vmem_limit_bytes=48 * 2**20),
        cost_estimate=pl.CostEstimate(
            flops=2 * slots * area * kvec, bytes_accessed=2 * slots * area, transcendentals=0
        ),
        name="tile_work",
    )(count, *[pltpu.with_memory_space_constraint(x, pltpu.HBM) for x in (rows, cols, ener, tiles)],
      gath, *seg)


def finish_kernel(scale, base, gram_parts, vec, *refs):
    got, (product, residual) = refs[:-2], refs[-2:]
    whole = base[...]
    for piece in got:
        whole = whole + piece[...].astype(jnp.float32)
    product[...] = whole.astype(jnp.bfloat16)
    flat = gram_parts[0]
    for i in range(1, gram_parts.shape[0]):
        flat = flat + gram_parts[i]
    kvec = vec.shape[0]
    lane = lax.broadcasted_iota(jnp.int32, (kvec, LANES), 1)
    first = kvec * lax.broadcasted_iota(jnp.int32, (kvec, LANES), 0)
    wide = jnp.broadcast_to(flat * scale, (kvec, LANES))
    vec32 = vec[...].astype(jnp.float32)
    for a in range(kvec):
        column = jnp.sum(jnp.where(lane == first + a, wide, 0.0), axis=1, keepdims=True)
        whole = whole - column * vec32[a:a + 1, :]
    residual[...] = whole


def finish(scale, base, gram_parts, vectors, got):
    vmem = pl.BlockSpec(memory_space=pltpu.VMEM)
    return pl.pallas_call(
        functools.partial(finish_kernel, scale),
        out_shape=(
            jax.ShapeDtypeStruct(vectors.shape, jnp.bfloat16),
            jax.ShapeDtypeStruct(vectors.shape, jnp.float32),
        ),
        in_specs=[vmem] * (3 + len(got)),
        out_specs=(vmem, vmem),
        compiler_params=pltpu.CompilerParams(vmem_limit_bytes=4 * 2**20),
        name="finish",
    )(base, gram_parts, vectors, *got)


def from_all(x, axis):
    size = lax.axis_size(axis)
    got = [x]
    for s in range(1, size):
        got.append(lax.ppermute(x, axis, [(i, (i + s) % size) for i in range(size)]))
    return got


def copies_kernel(x, out):
    for i in range(out.shape[0]):
        out[i] = x[...]


def repeat(x, size):
    vmem = pl.BlockSpec(memory_space=pltpu.VMEM)
    return pl.pallas_call(
        copies_kernel,
        out_shape=jax.ShapeDtypeStruct((size,) + x.shape, x.dtype),
        in_specs=[vmem],
        out_specs=vmem,
        compiler_params=pltpu.CompilerParams(vmem_limit_bytes=4 * 2**20),
        name="copies",
    )(x)


def per_device(vectors, energies, tiles, tile_rows, tile_cols, tile_count):
    kvec, own = vectors.shape
    n_row = lax.axis_size("row")
    n_col = lax.axis_size("col")
    gath = lax.all_to_all(repeat(vectors, n_row), "row", 0, 0)
    seg = from_all(vectors, "col")
    base, send, terms = tile_work(
        tile_rows, tile_cols, tile_count, gath, seg, energies[None, :], tiles
    )
    got = [
        lax.ppermute(send[s - 1], "col", [(c, (c + s) % n_col) for c in range(n_col)])
        for s in range(1, n_col)
    ]
    gram_parts = lax.all_to_all(terms, ("row", "col"), 0, 0)
    return finish(1.0 / (n_row * n_col * own), base, gram_parts, vectors, got)


def solution(mesh):
    in_specs = (
        P(None, ("row", "col")),
        P(("row", "col")),
        P(("row", "col"), None),
        P(("row", "col")),
        P(("row", "col")),
        P(("row", "col")),
    )
    out_specs = (P(None, ("row", "col")), P(None, ("row", "col")))
    return jax.shard_map(
        per_device, mesh=mesh, in_specs=in_specs, out_specs=out_specs, check_vma=False
    )
```

```python
import functools
import math

import jax
import jax.numpy as jnp
from jax import lax
from jax.experimental import pallas as pl
from jax.experimental.pallas import tpu as pltpu
from jax.sharding import PartitionSpec as P

LANES = 128
SUB = 8
CHUNK = 64

NT = (((1,), (1,)), ((), ()))


def tile_kernel(
    places, relative, n_col, side, count_s, rows_h, cols_h, ener_h, tiles, *refs,
):
    gath, refs = refs[:len(places)], refs[len(places):]
    seg, refs = refs[:n_col], refs[n_col:]
    (own_ref, send_ref, terms_ref, rows_s, cols_s, ener,
     buf, table, picked, select, part, wide, sems, small, *acc) = refs
    kvec, own = seg[0].shape
    n_row = sum(len(held) for held in places)
    slots = tiles.shape[0]
    blk_own = own // side
    per = LANES // side
    n_chunk = tiles.shape[1] // LANES
    my_col = lax.axis_index("col")

    copies = [
        pltpu.make_async_copy(src, dst, small.at[i])
        for i, (src, dst) in enumerate(
            ((cols_h, cols_s), (rows_h, rows_s), (ener_h, ener))
        )
    ]
    for copy in copies:
        copy.start()

    def tile_copy(ch):
        span = pl.ds(pl.multiple_of(ch * CHUNK, CHUNK), CHUNK)
        return pltpu.make_async_copy(tiles.at[span], buf.at[span], sems.at[ch])

    count = count_s[0]
    used = (count + CHUNK - 1) // CHUNK

    def start(ch, carry):
        tile_copy(ch).start()
        return carry

    lax.fori_loop(0, used, start, 0)

    lane = lax.broadcasted_iota(jnp.int32, (kvec, LANES), 1)
    low = lane < side
    zero = jnp.zeros((kvec, LANES), jnp.float32)

    my_row = lax.axis_index("row") if relative else 0
    for piece, held in zip(gath, places):
        for i, place in enumerate(held):
            first = (my_row ^ place) * blk_own
            for p in range(own // LANES):
                x = piece[i, :, p * LANES:(p + 1) * LANES].astype(jnp.float32)
                y = pltpu.roll(x, side, 1)
                at = first + p * per
                even = jnp.concatenate([jnp.where(low, x, zero), jnp.where(low, zero, y)], axis=0)
                odd = jnp.concatenate([jnp.where(low, y, zero), jnp.where(low, zero, x)], axis=0)
                table[at] = even.astype(jnp.bfloat16)
                table[at + 1] = odd.astype(jnp.bfloat16)
    n_blocks = n_row * blk_own
    table[n_blocks] = jnp.zeros((per * kvec, LANES), jnp.bfloat16)

    for copy in copies:
        copy.wait()
    n_seg = acc[0].shape[0]
    width = n_chunk * SUB

    def clear(r, carry):
        for a in acc:
            a[r] = jnp.zeros(a.shape[1:], jnp.float32)
        return carry

    lax.fori_loop(0, n_seg, clear, 0)

    k_id = lax.broadcasted_iota(jnp.int32, (width, LANES), 0)
    n_id = lax.broadcasted_iota(jnp.int32, (width, LANES), 1)
    base_id = n_id - per * (k_id // SUB)
    for par in range(per):
        for jp in range(per):
            at = (par * per + jp) * width
            hit = (base_id == side * par + jp).astype(jnp.float32)
            select[at:at + width, :] = hit.astype(jnp.bfloat16)

    rows_of = per * kvec

    def product(base, half, x):
        xh = x[half * SUB:(half + 1) * SUB]
        w = jnp.concatenate(
            [xh[:, c * LANES:(c + 1) * LANES] for c in range(n_chunk)], axis=0
        ).astype(jnp.bfloat16)
        entries = []
        for t in range(SUB):
            slot = base + half * SUB + t
            entries.append(table[jnp.where(slot < count, cols_s[slot], n_blocks)])
        left = jnp.concatenate(entries, axis=0)
        return lax.dot_general(left, w, NT, preferred_element_type=jnp.float32)

    def accumulate(at, out):
        for t in range(SUB):
            r = rows_s[at + t]
            acc[t][r] += out[t * rows_of:(t + 1) * rows_of]

    def one_chunk(ch, carry):
        tile_copy(ch).wait()
        waiting = None
        for q in range(CHUNK // (2 * SUB)):
            base = pl.multiple_of(ch * CHUNK + q * 2 * SUB, 2 * SUB)
            x = buf[pl.ds(base, 2 * SUB), :].astype(jnp.float32)
            for half in range(2):
                out = product(base, half, x)
                if waiting is not None:
                    accumulate(*waiting)
                waiting = (base + half * SUB, out)
        accumulate(*waiting)
        return carry

    lax.fori_loop(0, used, one_chunk, 0)

    lane_w = lax.broadcasted_iota(jnp.int32, (rows_of, width), 1) % SUB
    pairs = n_seg // per

    def pick(m, carry):
        pieces = []
        for par in range(per):
            total = jnp.zeros((rows_of, width), jnp.float32)
            for t in range(SUB):
                total = jnp.where(lane_w == t, acc[t][m * per + par], total)
            for jp in range(per):
                pieces.append(total[jp * kvec:(jp + 1) * kvec])
        a = jnp.concatenate(pieces, axis=1)
        hi = a.astype(jnp.bfloat16).astype(jnp.float32)
        both = jnp.concatenate([hi, a - hi], axis=0).astype(jnp.bfloat16)
        picked[pl.ds(pl.multiple_of(m * 2 * kvec, 2 * kvec), 2 * kvec), :] = both
        return carry

    lax.fori_loop(0, pairs, pick, 0)

    spread = jnp.dot(picked[...], select[...], preferred_element_type=jnp.float32)
    for m in range(pairs):
        at = m * 2 * kvec
        row = spread[at:at + kvec] + spread[at + kvec:at + 2 * kvec]
        c, lane0 = divmod(m * LANES, own)
        part[c, :, lane0:lane0 + LANES] = row

    part[my_col] += ener[...] * seg[0][...].astype(jnp.float32)
    own_ref[...] = part[my_col]
    terms = jnp.zeros((kvec, kvec), jnp.float32)
    for s in range(n_col):
        share = part[lax.rem(my_col + s, n_col)]
        if s > 0:
            send_ref[s - 1] = share.astype(jnp.bfloat16)
        terms = terms + lax.dot_general(
            share, seg[(n_col - s) % n_col][...].astype(jnp.float32), NT,
            precision=lax.Precision.HIGHEST, preferred_element_type=jnp.float32,
        )
    wide[...] = jnp.zeros(wide.shape, jnp.float32)
    wide[:, :kvec] = terms
    spaced = pltpu.roll(wide[...], 0, 1, stride=kvec, stride_axis=0)
    flat = jnp.sum(spaced, axis=0, keepdims=True)
    for i in range(terms_ref.shape[0]):
        terms_ref[i] = flat


def tile_work(rows, cols, count, gath, places, relative, seg, ener, tiles):
    n_col = len(seg)
    kvec, own = seg[0].shape
    n_row = sum(len(held) for held in places)
    slots, area = tiles.shape
    side = math.isqrt(area)
    per = LANES // side
    blk_own = own // side
    n_seg = n_col * blk_own
    width = area // LANES * SUB
    vmem = pl.BlockSpec(memory_space=pltpu.VMEM)
    far_away = pl.BlockSpec(memory_space=pltpu.HBM)
    return pl.pallas_call(
        functools.partial(tile_kernel, places, relative, n_col, side),
        out_shape=(
            jax.ShapeDtypeStruct((kvec, own), jnp.float32),
            jax.ShapeDtypeStruct((n_col - 1, kvec, own), jnp.bfloat16),
            jax.ShapeDtypeStruct((n_row * n_col, 1, LANES), jnp.float32),
        ),
        in_specs=[pl.BlockSpec(memory_space=pltpu.SMEM)] + [far_away] * 4 + [vmem] * (len(gath) + n_col),
        out_specs=(vmem, vmem, vmem),
        scratch_shapes=[
            pltpu.SMEM((slots,), jnp.int32),
            pltpu.SMEM((slots,), jnp.int32),
            pltpu.VMEM((1, own), jnp.float32),
            pltpu.VMEM((slots, area), jnp.bfloat16),
            pltpu.VMEM((n_row * blk_own + 1, per * kvec, LANES), jnp.bfloat16),
            pltpu.VMEM((n_seg // per * 2 * kvec, per * per * width), jnp.bfloat16),
            pltpu.VMEM((per * per * width, LANES), jnp.bfloat16),
            pltpu.VMEM((n_col, kvec, own), jnp.float32),
            pltpu.VMEM((kvec, LANES), jnp.float32),
            pltpu.SemaphoreType.DMA((slots // CHUNK,)),
            pltpu.SemaphoreType.DMA((3,)),
        ] + [pltpu.VMEM((n_seg, per * kvec, width), jnp.float32)] * SUB,
        compiler_params=pltpu.CompilerParams(vmem_limit_bytes=48 * 2**20),
        cost_estimate=pl.CostEstimate(
            flops=2 * slots * area * kvec, bytes_accessed=2 * slots * area, transcendentals=0
        ),
        name="tile_work",
    )(count, *[pltpu.with_memory_space_constraint(x, pltpu.HBM) for x in (rows, cols, ener, tiles)],
      *gath, *seg)


def finish_kernel(scale, base, gram_parts, vec, *refs):
    got, (product, residual) = refs[:-2], refs[-2:]
    whole = base[...]
    for piece in got:
        whole = whole + piece[...].astype(jnp.float32)
    product[...] = whole.astype(jnp.bfloat16)
    flat = gram_parts[0]
    for i in range(1, gram_parts.shape[0]):
        flat = flat + gram_parts[i]
    kvec = vec.shape[0]
    lane = lax.broadcasted_iota(jnp.int32, (kvec, LANES), 1)
    first = kvec * lax.broadcasted_iota(jnp.int32, (kvec, LANES), 0)
    wide = jnp.broadcast_to(flat * scale, (kvec, LANES))
    vec32 = vec[...].astype(jnp.float32)
    for a in range(kvec):
        column = jnp.sum(jnp.where(lane == first + a, wide, 0.0), axis=1, keepdims=True)
        whole = whole - column * vec32[a:a + 1, :]
    residual[...] = whole


def finish(scale, base, gram_parts, vectors, got):
    vmem = pl.BlockSpec(memory_space=pltpu.VMEM)
    return pl.pallas_call(
        functools.partial(finish_kernel, scale),
        out_shape=(
            jax.ShapeDtypeStruct(vectors.shape, jnp.bfloat16),
            jax.ShapeDtypeStruct(vectors.shape, jnp.float32),
        ),
        in_specs=[vmem] * (3 + len(got)),
        out_specs=(vmem, vmem),
        compiler_params=pltpu.CompilerParams(vmem_limit_bytes=4 * 2**20),
        name="finish",
    )(base, gram_parts, vectors, *got)


def from_all(x, axis):
    size = lax.axis_size(axis)
    got = [x]
    for s in range(1, size):
        got.append(lax.ppermute(x, axis, [(i, (i + s) % size) for i in range(size)]))
    return got


def gather(x, axis):
    size = lax.axis_size(axis)
    if size & (size - 1):
        return [lax.all_to_all(repeat(x, size), axis, 0, 0)], [list(range(size))], False
    pieces, places = [x[None]], [[0]]
    step = size // 2
    while step:
        held = pieces[0] if len(pieces) == 1 else jnp.concatenate(pieces, axis=0)
        got = lax.ppermute(held, axis, [(i, i ^ step) for i in range(size)])
        places.append([step ^ place for known in places for place in known])
        pieces.append(got)
        step //= 2
    return pieces, places, True


def copies_kernel(x, out):
    for i in range(out.shape[0]):
        out[i] = x[...]


def repeat(x, size):
    vmem = pl.BlockSpec(memory_space=pltpu.VMEM)
    return pl.pallas_call(
        copies_kernel,
        out_shape=jax.ShapeDtypeStruct((size,) + x.shape, x.dtype),
        in_specs=[vmem],
        out_specs=vmem,
        compiler_params=pltpu.CompilerParams(vmem_limit_bytes=4 * 2**20),
        name="copies",
    )(x)


def per_device(vectors, energies, tiles, tile_rows, tile_cols, tile_count):
    kvec, own = vectors.shape
    n_row = lax.axis_size("row")
    n_col = lax.axis_size("col")
    gath, places, relative = gather(vectors, "row")
    seg = from_all(vectors, "col")
    base, send, terms = tile_work(
        tile_rows, tile_cols, tile_count, gath, places, relative, seg, energies[None, :], tiles
    )
    got = [
        lax.ppermute(send[s - 1], "col", [(c, (c + s) % n_col) for c in range(n_col)])
        for s in range(1, n_col)
    ]
    gram_parts = lax.all_to_all(terms, ("row", "col"), 0, 0)
    return finish(1.0 / (n_row * n_col * own), base, gram_parts, vectors, got)


def solution(mesh):
    in_specs = (
        P(None, ("row", "col")),
        P(("row", "col")),
        P(("row", "col"), None),
        P(("row", "col")),
        P(("row", "col")),
        P(("row", "col")),
    )
    out_specs = (P(None, ("row", "col")), P(None, ("row", "col")))
    return jax.shard_map(
        per_device, mesh=mesh, in_specs=in_specs, out_specs=out_specs, check_vma=False
    )
```

```python
import functools
import math

import jax
import jax.numpy as jnp
from jax import lax
from jax.experimental import pallas as pl
from jax.experimental.pallas import tpu as pltpu
from jax.sharding import Mesh, PartitionSpec as P

LANES = 128
SUB = 8
CHUNK = 64

NT = (((1,), (1,)), ((), ()))


def tile_kernel(
    n_core, n_col, side, count_s, rows_h, cols_h, ener_h, tiles, *refs,
):
    gath, refs = refs[:n_core], refs[n_core:]
    (own_ref, send_ref, rest_ref, rows_s, cols_s, ener,
     buf, table, picked, select, part, sems, small, *acc) = refs
    n_far, kvec, own = gath[0].shape
    slots = tiles.shape[0]
    blk_own = own // side
    per = LANES // side
    n_chunk = tiles.shape[1] // LANES
    my_far, my_core, my_col = (lax.axis_index(name) for name in ("far", "core", "col"))

    copies = [
        pltpu.make_async_copy(src, dst, small.at[i])
        for i, (src, dst) in enumerate(
            ((cols_h, cols_s), (rows_h, rows_s), (ener_h, ener))
        )
    ]
    for copy in copies:
        copy.start()

    def tile_copy(ch):
        span = pl.ds(pl.multiple_of(ch * CHUNK, CHUNK), CHUNK)
        return pltpu.make_async_copy(tiles.at[span], buf.at[span], sems.at[ch])

    count = count_s[0]
    used = (count + CHUNK - 1) // CHUNK

    def start(ch, carry):
        tile_copy(ch).start()
        return carry

    lax.fori_loop(0, used, start, 0)

    lane = lax.broadcasted_iota(jnp.int32, (kvec, LANES), 1)
    low = lane < side
    zero = jnp.zeros((kvec, LANES), jnp.float32)

    for s in range(n_core):
        core = lax.rem(my_core + (n_core - s), n_core)
        for f in range(n_far):
            for p in range(own // LANES):
                x = gath[s][f, :, p * LANES:(p + 1) * LANES].astype(jnp.float32)
                y = pltpu.roll(x, side, 1)
                at = (f * n_core + core) * blk_own + p * per
                even = jnp.concatenate([jnp.where(low, x, zero), jnp.where(low, zero, y)], axis=0)
                odd = jnp.concatenate([jnp.where(low, y, zero), jnp.where(low, zero, x)], axis=0)
                table[at] = even.astype(jnp.bfloat16)
                table[at + 1] = odd.astype(jnp.bfloat16)
    n_blocks = n_far * n_core * blk_own
    table[n_blocks] = jnp.zeros((per * kvec, LANES), jnp.bfloat16)

    for copy in copies:
        copy.wait()
    n_seg = acc[0].shape[0]
    width = n_chunk * SUB

    def clear(r, carry):
        for a in acc:
            a[r] = jnp.zeros(a.shape[1:], jnp.float32)
        return carry

    lax.fori_loop(0, n_seg, clear, 0)

    k_id = lax.broadcasted_iota(jnp.int32, (width, LANES), 0)
    n_id = lax.broadcasted_iota(jnp.int32, (width, LANES), 1)
    base_id = n_id - per * (k_id // SUB)
    for par in range(per):
        for jp in range(per):
            at = (par * per + jp) * width
            hit = (base_id == side * par + jp).astype(jnp.float32)
            select[at:at + width, :] = hit.astype(jnp.bfloat16)

    rows_of = per * kvec

    def product(base, half, x):
        xh = x[half * SUB:(half + 1) * SUB]
        w = jnp.concatenate(
            [xh[:, c * LANES:(c + 1) * LANES] for c in range(n_chunk)], axis=0
        ).astype(jnp.bfloat16)
        entries = []
        for t in range(SUB):
            slot = base + half * SUB + t
            entries.append(table[jnp.where(slot < count, cols_s[slot], n_blocks)])
        left = jnp.concatenate(entries, axis=0)
        return lax.dot_general(left, w, NT, preferred_element_type=jnp.float32)

    def accumulate(at, out):
        for t in range(SUB):
            r = rows_s[at + t]
            acc[t][r] += out[t * rows_of:(t + 1) * rows_of]

    def one_chunk(ch, carry):
        tile_copy(ch).wait()
        waiting = None
        for q in range(CHUNK // (2 * SUB)):
            base = pl.multiple_of(ch * CHUNK + q * 2 * SUB, 2 * SUB)
            x = buf[pl.ds(base, 2 * SUB), :].astype(jnp.float32)
            for half in range(2):
                out = product(base, half, x)
                if waiting is not None:
                    accumulate(*waiting)
                waiting = (base + half * SUB, out)
        accumulate(*waiting)
        return carry

    lax.fori_loop(0, used, one_chunk, 0)

    lane_w = lax.broadcasted_iota(jnp.int32, (rows_of, width), 1) % SUB
    pairs = n_seg // per

    def pick(m, carry):
        pieces = []
        for par in range(per):
            total = jnp.zeros((rows_of, width), jnp.float32)
            for t in range(SUB):
                total = jnp.where(lane_w == t, acc[t][m * per + par], total)
            for jp in range(per):
                pieces.append(total[jp * kvec:(jp + 1) * kvec])
        a = jnp.concatenate(pieces, axis=1)
        hi = a.astype(jnp.bfloat16).astype(jnp.float32)
        both = jnp.concatenate([hi, a - hi], axis=0).astype(jnp.bfloat16)
        picked[pl.ds(pl.multiple_of(m * 2 * kvec, 2 * kvec), 2 * kvec), :] = both
        return carry

    lax.fori_loop(0, pairs, pick, 0)

    spread = jnp.dot(picked[...], select[...], preferred_element_type=jnp.float32)
    for m in range(pairs):
        at = m * 2 * kvec
        row = spread[at:at + kvec] + spread[at + kvec:at + 2 * kvec]
        c, lane0 = divmod(m * LANES, own)
        part[c, :, lane0:lane0 + LANES] = row

    own_ref[...] = part[my_col] + ener[...] * gath[0][my_far].astype(jnp.float32)
    for s in range(1, n_col):
        share = part[lax.rem(my_col + s, n_col)]
        send_ref[s - 1] = share.astype(jnp.bfloat16)
        rest_ref[s - 1] = share


def tile_work(rows, cols, count, gath, n_col, ener, tiles):
    n_core = len(gath)
    n_far, kvec, own = gath[0].shape
    slots, area = tiles.shape
    side = math.isqrt(area)
    per = LANES // side
    blk_own = own // side
    n_seg = n_col * blk_own
    width = area // LANES * SUB
    vmem = pl.BlockSpec(memory_space=pltpu.VMEM)
    far_away = pl.BlockSpec(memory_space=pltpu.HBM)
    return pl.pallas_call(
        functools.partial(tile_kernel, n_core, n_col, side),
        out_shape=(
            jax.ShapeDtypeStruct((kvec, own), jnp.float32),
            jax.ShapeDtypeStruct((n_col - 1, kvec, own), jnp.bfloat16),
            jax.ShapeDtypeStruct((n_col - 1, kvec, own), jnp.float32),
        ),
        in_specs=[pl.BlockSpec(memory_space=pltpu.SMEM)] + [far_away] * 4 + [vmem] * n_core,
        out_specs=(vmem, vmem, vmem),
        scratch_shapes=[
            pltpu.SMEM((slots,), jnp.int32),
            pltpu.SMEM((slots,), jnp.int32),
            pltpu.VMEM((1, own), jnp.float32),
            pltpu.VMEM((slots, area), jnp.bfloat16),
            pltpu.VMEM((n_far * n_core * blk_own + 1, per * kvec, LANES), jnp.bfloat16),
            pltpu.VMEM((n_seg // per * 2 * kvec, per * per * width), jnp.bfloat16),
            pltpu.VMEM((per * per * width, LANES), jnp.bfloat16),
            pltpu.VMEM((n_col, kvec, own), jnp.float32),
            pltpu.SemaphoreType.DMA((slots // CHUNK,)),
            pltpu.SemaphoreType.DMA((3,)),
        ] + [pltpu.VMEM((n_seg, per * kvec, width), jnp.float32)] * SUB,
        compiler_params=pltpu.CompilerParams(vmem_limit_bytes=48 * 2**20),
        cost_estimate=pl.CostEstimate(
            flops=2 * slots * area * kvec, bytes_accessed=2 * slots * area, transcendentals=0
        ),
        name="tile_work",
    )(count, *[pltpu.with_memory_space_constraint(x, pltpu.HBM) for x in (rows, cols, ener, tiles)],
      *gath)


def terms_kernel(own, rest, vec, *refs):
    others, (terms_ref, wide) = refs[:-2], refs[-2:]
    n_col = len(others) + 1
    kvec = vec.shape[0]

    def outer(share, seg):
        return lax.dot_general(
            share, seg[...].astype(jnp.float32), NT,
            precision=lax.Precision.HIGHEST, preferred_element_type=jnp.float32,
        )

    terms = outer(own[...], vec)
    for s in range(1, n_col):
        terms = terms + outer(rest[s - 1], others[n_col - s - 1])
    wide[...] = jnp.zeros(wide.shape, jnp.float32)
    wide[:, :kvec] = terms
    spaced = pltpu.roll(wide[...], 0, 1, stride=kvec, stride_axis=0)
    flat = jnp.sum(spaced, axis=0, keepdims=True)
    for i in range(terms_ref.shape[0]):
        terms_ref[i] = flat


def gram_terms(own, rest, vectors, others, members):
    vmem = pl.BlockSpec(memory_space=pltpu.VMEM)
    return pl.pallas_call(
        terms_kernel,
        out_shape=jax.ShapeDtypeStruct((members, 1, LANES), jnp.float32),
        in_specs=[vmem] * (3 + len(others)),
        out_specs=vmem,
        scratch_shapes=[pltpu.VMEM((vectors.shape[0], LANES), jnp.float32)],
        compiler_params=pltpu.CompilerParams(vmem_limit_bytes=4 * 2**20),
        name="gram_terms",
    )(own, rest, vectors, *others)


def finish_kernel(scale, base, gram_parts, vec, *refs):
    got, (product, residual) = refs[:-2], refs[-2:]
    whole = base[...]
    for piece in got:
        whole = whole + piece[...].astype(jnp.float32)
    product[...] = whole.astype(jnp.bfloat16)
    flat = gram_parts[0]
    for i in range(1, gram_parts.shape[0]):
        flat = flat + gram_parts[i]
    kvec = vec.shape[0]
    lane = lax.broadcasted_iota(jnp.int32, (kvec, LANES), 1)
    first = kvec * lax.broadcasted_iota(jnp.int32, (kvec, LANES), 0)
    wide = jnp.broadcast_to(flat * scale, (kvec, LANES))
    vec32 = vec[...].astype(jnp.float32)
    for a in range(kvec):
        column = jnp.sum(jnp.where(lane == first + a, wide, 0.0), axis=1, keepdims=True)
        whole = whole - column * vec32[a:a + 1, :]
    residual[...] = whole


def finish(scale, base, gram_parts, vectors, got):
    vmem = pl.BlockSpec(memory_space=pltpu.VMEM)
    return pl.pallas_call(
        functools.partial(finish_kernel, scale),
        out_shape=(
            jax.ShapeDtypeStruct(vectors.shape, jnp.bfloat16),
            jax.ShapeDtypeStruct(vectors.shape, jnp.float32),
        ),
        in_specs=[vmem] * (3 + len(got)),
        out_specs=(vmem, vmem),
        compiler_params=pltpu.CompilerParams(vmem_limit_bytes=4 * 2**20),
        name="finish",
    )(base, gram_parts, vectors, *got)


def from_all(x, axis):
    size = lax.axis_size(axis)
    got = [x]
    for s in range(1, size):
        got.append(lax.ppermute(x, axis, [(i, (i + s) % size) for i in range(size)]))
    return got


def copies_kernel(x, out, sems):
    copies = [pltpu.make_async_copy(x, out.at[i], sems.at[i]) for i in range(out.shape[0])]
    for copy in copies:
        copy.start()
    for copy in copies:
        copy.wait()


def repeat(x, size):
    return pl.pallas_call(
        copies_kernel,
        out_shape=jax.ShapeDtypeStruct((size,) + x.shape, x.dtype),
        in_specs=[pl.BlockSpec(memory_space=pltpu.HBM)],
        out_specs=pl.BlockSpec(memory_space=pltpu.VMEM),
        scratch_shapes=[pltpu.SemaphoreType.DMA((size,))],
        compiler_params=pltpu.CompilerParams(vmem_limit_bytes=4 * 2**20),
        name="copies",
    )(pltpu.with_memory_space_constraint(x, pltpu.HBM))


def per_device(vectors, energies, tiles, tile_rows, tile_cols, tile_count):
    kvec, own = vectors.shape
    n_col = lax.axis_size("col")
    gath = lax.all_to_all(repeat(vectors, lax.axis_size("far")), "far", 0, 0)
    gath = from_all(gath, "core")
    base, send, rest = tile_work(
        tile_rows, tile_cols, tile_count, gath, n_col, energies[None, :], tiles
    )
    got = [
        lax.ppermute(send[s - 1], "col", [(c, (c + s) % n_col) for c in range(n_col)])
        for s in range(1, n_col)
    ]
    others = from_all(vectors, "col")[1:]
    members = lax.axis_size(("far", "core", "col"))
    terms = gram_terms(base, rest, vectors, others, members)
    gram_parts = lax.all_to_all(terms, ("far", "core", "col"), 0, 0)
    return finish(1.0 / (members * own), base, gram_parts, vectors, got)


def solution(mesh):
    n_row, n_col = mesh.devices.shape
    n_core = 2 if n_row % 2 == 0 else 1
    split = ("far", "core", "col")
    chips = Mesh(mesh.devices.reshape(n_row // n_core, n_core, n_col), split)
    in_specs = (P(None, split), P(split), P(split, None), P(split), P(split), P(split))
    out_specs = (P(None, split), P(None, split))
    return jax.shard_map(
        per_device, mesh=chips, in_specs=in_specs, out_specs=out_specs, check_vma=False
    )
```

```python
import functools
import math

import jax
import jax.numpy as jnp
from jax import lax
from jax.experimental import pallas as pl
from jax.experimental.pallas import tpu as pltpu
from jax.sharding import Mesh, PartitionSpec as P

LANES = 128
SUB = 8
CHUNK = 64

NT = (((1,), (1,)), ((), ()))


def tile_kernel(
    n_core, n_col, side, count_s, rows_h, cols_h, ener_h, tiles, *refs,
):
    gath, refs = refs[:n_core], refs[n_core:]
    (own_ref, send_ref, rest_ref, rows_s, cols_s, ener,
     buf, table, picked, select, part, sems, small, *acc) = refs
    n_far, kvec, own = gath[0].shape
    slots = tiles.shape[0]
    blk_own = own // side
    per = LANES // side
    n_chunk = tiles.shape[1] // LANES
    my_far, my_core, my_col = (lax.axis_index(name) for name in ("far", "core", "col"))

    copies = [
        pltpu.make_async_copy(src, dst, small.at[i])
        for i, (src, dst) in enumerate(
            ((cols_h, cols_s), (rows_h, rows_s), (ener_h, ener))
        )
    ]
    for copy in copies:
        copy.start()

    def tile_copy(ch):
        span = pl.ds(pl.multiple_of(ch * CHUNK, CHUNK), CHUNK)
        return pltpu.make_async_copy(tiles.at[span], buf.at[span], sems.at[ch])

    count = count_s[0]
    used = (count + CHUNK - 1) // CHUNK

    def start(ch, carry):
        tile_copy(ch).start()
        return carry

    lax.fori_loop(0, used, start, 0)

    lane = lax.broadcasted_iota(jnp.int32, (kvec, LANES), 1)
    low = lane < side
    zero = jnp.zeros((kvec, LANES), jnp.float32)

    for s in range(n_core):
        core = lax.rem(my_core + (n_core - s), n_core)
        for f in range(n_far):
            for p in range(own // LANES):
                x = gath[s][f, :, p * LANES:(p + 1) * LANES].astype(jnp.float32)
                y = pltpu.roll(x, side, 1)
                at = (f * n_core + core) * blk_own + p * per
                even = jnp.concatenate([jnp.where(low, x, zero), jnp.where(low, zero, y)], axis=0)
                odd = jnp.concatenate([jnp.where(low, y, zero), jnp.where(low, zero, x)], axis=0)
                table[at] = even.astype(jnp.bfloat16)
                table[at + 1] = odd.astype(jnp.bfloat16)
    n_blocks = n_far * n_core * blk_own
    table[n_blocks] = jnp.zeros((per * kvec, LANES), jnp.bfloat16)

    for copy in copies:
        copy.wait()
    n_seg = acc[0].shape[0]
    width = n_chunk * SUB

    def clear(r, carry):
        for a in acc:
            a[r] = jnp.zeros(a.shape[1:], jnp.float32)
        return carry

    lax.fori_loop(0, n_seg, clear, 0)

    k_id = lax.broadcasted_iota(jnp.int32, (width, LANES), 0)
    n_id = lax.broadcasted_iota(jnp.int32, (width, LANES), 1)
    base_id = n_id - per * (k_id // SUB)
    for par in range(per):
        for jp in range(per):
            at = (par * per + jp) * width
            hit = (base_id == side * par + jp).astype(jnp.float32)
            select[at:at + width, :] = hit.astype(jnp.bfloat16)

    rows_of = per * kvec

    def product(base, half, x):
        xh = x[half * SUB:(half + 1) * SUB]
        w = jnp.concatenate(
            [xh[:, c * LANES:(c + 1) * LANES] for c in range(n_chunk)], axis=0
        ).astype(jnp.bfloat16)
        entries = []
        for t in range(SUB):
            slot = base + half * SUB + t
            entries.append(table[jnp.where(slot < count, cols_s[slot], n_blocks)])
        left = jnp.concatenate(entries, axis=0)
        return lax.dot_general(left, w, NT, preferred_element_type=jnp.float32)

    def accumulate(at, out):
        for t in range(SUB):
            r = rows_s[at + t]
            acc[t][r] += out[t * rows_of:(t + 1) * rows_of]

    def one_chunk(ch, carry):
        tile_copy(ch).wait()
        waiting = None
        for q in range(CHUNK // (2 * SUB)):
            base = pl.multiple_of(ch * CHUNK + q * 2 * SUB, 2 * SUB)
            x = buf[pl.ds(base, 2 * SUB), :].astype(jnp.float32)
            for half in range(2):
                out = product(base, half, x)
                if waiting is not None:
                    accumulate(*waiting)
                waiting = (base + half * SUB, out)
        accumulate(*waiting)
        return carry

    lax.fori_loop(0, used, one_chunk, 0)

    lane_w = lax.broadcasted_iota(jnp.int32, (rows_of, width), 1) % SUB
    pairs = n_seg // per

    def pick(m, carry):
        pieces = []
        for par in range(per):
            total = jnp.zeros((rows_of, width), jnp.float32)
            for t in range(SUB):
                total = jnp.where(lane_w == t, acc[t][m * per + par], total)
            for jp in range(per):
                pieces.append(total[jp * kvec:(jp + 1) * kvec])
        a = jnp.concatenate(pieces, axis=1)
        hi = a.astype(jnp.bfloat16).astype(jnp.float32)
        both = jnp.concatenate([hi, a - hi], axis=0).astype(jnp.bfloat16)
        picked[pl.ds(pl.multiple_of(m * 2 * kvec, 2 * kvec), 2 * kvec), :] = both
        return carry

    lax.fori_loop(0, pairs, pick, 0)

    spread = jnp.dot(picked[...], select[...], preferred_element_type=jnp.float32)
    for m in range(pairs):
        at = m * 2 * kvec
        row = spread[at:at + kvec] + spread[at + kvec:at + 2 * kvec]
        c, lane0 = divmod(m * LANES, own)
        part[c, :, lane0:lane0 + LANES] = row

    own_ref[...] = part[my_col] + ener[...] * gath[0][my_far].astype(jnp.float32)
    for s in range(1, n_col):
        share = part[lax.rem(my_col + s, n_col)]
        send_ref[s - 1] = share.astype(jnp.bfloat16)
        rest_ref[s - 1] = share


def tile_work(rows, cols, count, gath, n_col, ener, tiles):
    n_core = len(gath)
    n_far, kvec, own = gath[0].shape
    slots, area = tiles.shape
    side = math.isqrt(area)
    per = LANES // side
    blk_own = own // side
    n_seg = n_col * blk_own
    width = area // LANES * SUB
    vmem = pl.BlockSpec(memory_space=pltpu.VMEM)
    far_away = pl.BlockSpec(memory_space=pltpu.HBM)
    return pl.pallas_call(
        functools.partial(tile_kernel, n_core, n_col, side),
        out_shape=(
            jax.ShapeDtypeStruct((kvec, own), jnp.float32),
            jax.ShapeDtypeStruct((n_col - 1, kvec, own), jnp.bfloat16),
            jax.ShapeDtypeStruct((n_col - 1, kvec, own), jnp.float32),
        ),
        in_specs=[pl.BlockSpec(memory_space=pltpu.SMEM)] + [far_away] * 4 + [vmem] * n_core,
        out_specs=(vmem, vmem, vmem),
        scratch_shapes=[
            pltpu.SMEM((slots,), jnp.int32),
            pltpu.SMEM((slots,), jnp.int32),
            pltpu.VMEM((1, own), jnp.float32),
            pltpu.VMEM((slots, area), jnp.bfloat16),
            pltpu.VMEM((n_far * n_core * blk_own + 1, per * kvec, LANES), jnp.bfloat16),
            pltpu.VMEM((n_seg // per * 2 * kvec, per * per * width), jnp.bfloat16),
            pltpu.VMEM((per * per * width, LANES), jnp.bfloat16),
            pltpu.VMEM((n_col, kvec, own), jnp.float32),
            pltpu.SemaphoreType.DMA((slots // CHUNK,)),
            pltpu.SemaphoreType.DMA((3,)),
        ] + [pltpu.VMEM((n_seg, per * kvec, width), jnp.float32)] * SUB,
        compiler_params=pltpu.CompilerParams(vmem_limit_bytes=48 * 2**20),
        cost_estimate=pl.CostEstimate(
            flops=2 * slots * area * kvec, bytes_accessed=2 * slots * area, transcendentals=0
        ),
        name="tile_work",
    )(count, *[pltpu.with_memory_space_constraint(x, pltpu.HBM) for x in (rows, cols, ener, tiles)],
      *gath)


def terms_kernel(own, rest, vec, *refs):
    others, (terms_ref, wide) = refs[:-2], refs[-2:]
    n_col = len(others) + 1
    kvec = vec.shape[0]

    def outer(share, seg):
        return lax.dot_general(
            share, seg[...].astype(jnp.float32), NT,
            precision=lax.Precision.HIGHEST, preferred_element_type=jnp.float32,
        )

    terms = outer(own[...], vec)
    for s in range(1, n_col):
        terms = terms + outer(rest[s - 1], others[n_col - s - 1])
    wide[...] = jnp.zeros(wide.shape, jnp.float32)
    wide[:, :kvec] = terms
    spaced = pltpu.roll(wide[...], 0, 1, stride=kvec, stride_axis=0)
    flat = jnp.sum(spaced, axis=0, keepdims=True)
    for i in range(terms_ref.shape[0]):
        terms_ref[i] = flat


def gram_terms(own, rest, vectors, others, members):
    vmem = pl.BlockSpec(memory_space=pltpu.VMEM)
    return pl.pallas_call(
        terms_kernel,
        out_shape=jax.ShapeDtypeStruct((members, 1, LANES), jnp.float32),
        in_specs=[vmem] * (3 + len(others)),
        out_specs=vmem,
        scratch_shapes=[pltpu.VMEM((vectors.shape[0], LANES), jnp.float32)],
        compiler_params=pltpu.CompilerParams(vmem_limit_bytes=4 * 2**20),
        name="gram_terms",
    )(own, rest, vectors, *others)


def finish_kernel(scale, base, gram_parts, vec, *refs):
    got, (product, residual) = refs[:-2], refs[-2:]
    whole = base[...]
    for piece in got:
        whole = whole + piece[...].astype(jnp.float32)
    product[...] = whole.astype(jnp.bfloat16)
    flat = gram_parts[0]
    for i in range(1, gram_parts.shape[0]):
        flat = flat + gram_parts[i]
    kvec = vec.shape[0]
    lane = lax.broadcasted_iota(jnp.int32, (kvec, LANES), 1)
    first = kvec * lax.broadcasted_iota(jnp.int32, (kvec, LANES), 0)
    wide = jnp.broadcast_to(flat * scale, (kvec, LANES))
    vec32 = vec[...].astype(jnp.float32)
    for a in range(kvec):
        column = jnp.sum(jnp.where(lane == first + a, wide, 0.0), axis=1, keepdims=True)
        whole = whole - column * vec32[a:a + 1, :]
    residual[...] = whole


def finish(scale, base, gram_parts, vectors, got):
    vmem = pl.BlockSpec(memory_space=pltpu.VMEM)
    return pl.pallas_call(
        functools.partial(finish_kernel, scale),
        out_shape=(
            jax.ShapeDtypeStruct(vectors.shape, jnp.bfloat16),
            jax.ShapeDtypeStruct(vectors.shape, jnp.float32),
        ),
        in_specs=[vmem] * (3 + len(got)),
        out_specs=(vmem, vmem),
        compiler_params=pltpu.CompilerParams(vmem_limit_bytes=4 * 2**20),
        name="finish",
    )(base, gram_parts, vectors, *got)


def from_all(x, axis):
    size = lax.axis_size(axis)
    got = [x]
    for s in range(1, size):
        got.append(lax.ppermute(x, axis, [(i, (i + s) % size) for i in range(size)]))
    return got


def per_device(vectors, energies, tiles, tile_rows, tile_cols, tile_count):
    kvec, own = vectors.shape
    n_col = lax.axis_size("col")
    gath = lax.all_gather(vectors, "far", axis=0)
    gath = from_all(gath, "core")
    base, send, rest = tile_work(
        tile_rows, tile_cols, tile_count, gath, n_col, energies[None, :], tiles
    )
    got = [
        lax.ppermute(send[s - 1], "col", [(c, (c + s) % n_col) for c in range(n_col)])
        for s in range(1, n_col)
    ]
    others = from_all(vectors, "col")[1:]
    members = lax.axis_size(("far", "core", "col"))
    terms = gram_terms(base, rest, vectors, others, members)
    gram_parts = lax.all_to_all(terms, ("far", "core", "col"), 0, 0)
    return finish(1.0 / (members * own), base, gram_parts, vectors, got)


def solution(mesh):
    n_row, n_col = mesh.devices.shape
    n_core = 2 if n_row % 2 == 0 else 1
    split = ("far", "core", "col")
    chips = Mesh(mesh.devices.reshape(n_row // n_core, n_core, n_col), split)
    in_specs = (P(None, split), P(split), P(split, None), P(split), P(split), P(split))
    out_specs = (P(None, split), P(None, split))
    return jax.shard_map(
        per_device, mesh=chips, in_specs=in_specs, out_specs=out_specs, check_vma=False
    )
```

```python
import functools
import math

import jax
import jax.numpy as jnp
from jax import lax
from jax.experimental import pallas as pl
from jax.experimental.pallas import tpu as pltpu
from jax.sharding import Mesh, PartitionSpec as P

LANES = 128
SUB = 8
CHUNK = 64

NT = (((1,), (1,)), ((), ()))


def tile_kernel(
    n_core, n_col, side, count_s, rows_h, cols_h, ener_h, tiles, *refs,
):
    gath, refs = refs[:n_core], refs[n_core:]
    (own_ref, send_ref, rest_ref, rows_s, cols_s, ener,
     table, picked, select, part, small, *acc) = refs
    n_far, kvec, own = gath[0].shape
    slots = tiles.shape[0]
    blk_own = own // side
    per = LANES // side
    n_chunk = tiles.shape[1] // LANES
    my_far, my_core, my_col = (lax.axis_index(name) for name in ("far", "core", "col"))

    copies = [
        pltpu.make_async_copy(src, dst, small.at[i])
        for i, (src, dst) in enumerate(
            ((cols_h, cols_s), (rows_h, rows_s), (ener_h, ener))
        )
    ]
    for copy in copies:
        copy.start()

    count = count_s[0]
    used = (count + CHUNK - 1) // CHUNK

    lane = lax.broadcasted_iota(jnp.int32, (kvec, LANES), 1)
    low = lane < side
    zero = jnp.zeros((kvec, LANES), jnp.float32)

    for s in range(n_core):
        core = lax.rem(my_core + (n_core - s), n_core)
        for f in range(n_far):
            for p in range(own // LANES):
                x = gath[s][f, :, p * LANES:(p + 1) * LANES].astype(jnp.float32)
                y = pltpu.roll(x, side, 1)
                at = (f * n_core + core) * blk_own + p * per
                even = jnp.concatenate([jnp.where(low, x, zero), jnp.where(low, zero, y)], axis=0)
                odd = jnp.concatenate([jnp.where(low, y, zero), jnp.where(low, zero, x)], axis=0)
                table[at] = even.astype(jnp.bfloat16)
                table[at + 1] = odd.astype(jnp.bfloat16)
    n_blocks = n_far * n_core * blk_own
    table[n_blocks] = jnp.zeros((per * kvec, LANES), jnp.bfloat16)

    for copy in copies:
        copy.wait()
    n_seg = acc[0].shape[0]
    width = n_chunk * SUB

    def clear(r, carry):
        for a in acc:
            a[r] = jnp.zeros(a.shape[1:], jnp.float32)
        return carry

    lax.fori_loop(0, n_seg, clear, 0)

    k_id = lax.broadcasted_iota(jnp.int32, (width, LANES), 0)
    n_id = lax.broadcasted_iota(jnp.int32, (width, LANES), 1)
    base_id = n_id - per * (k_id // SUB)
    for par in range(per):
        for jp in range(per):
            at = (par * per + jp) * width
            hit = (base_id == side * par + jp).astype(jnp.float32)
            select[at:at + width, :] = hit.astype(jnp.bfloat16)

    rows_of = per * kvec

    def product(base, half, x):
        xh = x[half * SUB:(half + 1) * SUB]
        w = jnp.concatenate(
            [xh[:, c * LANES:(c + 1) * LANES] for c in range(n_chunk)], axis=0
        ).astype(jnp.bfloat16)
        entries = []
        for t in range(SUB):
            slot = base + half * SUB + t
            entries.append(table[jnp.where(slot < count, cols_s[slot], n_blocks)])
        left = jnp.concatenate(entries, axis=0)
        return lax.dot_general(left, w, NT, preferred_element_type=jnp.float32)

    def accumulate(at, out):
        for t in range(SUB):
            r = rows_s[at + t]
            acc[t][r] += out[t * rows_of:(t + 1) * rows_of]

    def one_chunk(ch, carry):
        waiting = None
        for q in range(CHUNK // (2 * SUB)):
            base = pl.multiple_of(ch * CHUNK + q * 2 * SUB, 2 * SUB)
            x = tiles[pl.ds(base, 2 * SUB), :].astype(jnp.float32)
            for half in range(2):
                out = product(base, half, x)
                if waiting is not None:
                    accumulate(*waiting)
                waiting = (base + half * SUB, out)
        accumulate(*waiting)
        return carry

    lax.fori_loop(0, used, one_chunk, 0)

    lane_w = lax.broadcasted_iota(jnp.int32, (rows_of, width), 1) % SUB
    pairs = n_seg // per

    def pick(m, carry):
        pieces = []
        for par in range(per):
            total = jnp.zeros((rows_of, width), jnp.float32)
            for t in range(SUB):
                total = jnp.where(lane_w == t, acc[t][m * per + par], total)
            for jp in range(per):
                pieces.append(total[jp * kvec:(jp + 1) * kvec])
        a = jnp.concatenate(pieces, axis=1)
        hi = a.astype(jnp.bfloat16).astype(jnp.float32)
        both = jnp.concatenate([hi, a - hi], axis=0).astype(jnp.bfloat16)
        picked[pl.ds(pl.multiple_of(m * 2 * kvec, 2 * kvec), 2 * kvec), :] = both
        return carry

    lax.fori_loop(0, pairs, pick, 0)

    spread = jnp.dot(picked[...], select[...], preferred_element_type=jnp.float32)
    for m in range(pairs):
        at = m * 2 * kvec
        row = spread[at:at + kvec] + spread[at + kvec:at + 2 * kvec]
        c, lane0 = divmod(m * LANES, own)
        part[c, :, lane0:lane0 + LANES] = row

    own_ref[...] = part[my_col] + ener[...] * gath[0][my_far].astype(jnp.float32)
    for s in range(1, n_col):
        share = part[lax.rem(my_col + s, n_col)]
        send_ref[s - 1] = share.astype(jnp.bfloat16)
        rest_ref[s - 1] = share


def fetch_kernel(count_s, tiles, buf, sems):
    used = (count_s[0] + CHUNK - 1) // CHUNK

    def tile_copy(ch):
        span = pl.ds(pl.multiple_of(ch * CHUNK, CHUNK), CHUNK)
        return pltpu.make_async_copy(tiles.at[span], buf.at[span], sems.at[ch])

    def start(ch, carry):
        tile_copy(ch).start()
        return carry

    def wait(ch, carry):
        tile_copy(ch).wait()
        return carry

    lax.fori_loop(0, used, start, 0)
    lax.fori_loop(0, used, wait, 0)


def fetch_tiles(count, tiles):
    return pl.pallas_call(
        fetch_kernel,
        out_shape=jax.ShapeDtypeStruct(tiles.shape, tiles.dtype),
        in_specs=[
            pl.BlockSpec(memory_space=pltpu.SMEM),
            pl.BlockSpec(memory_space=pltpu.HBM),
        ],
        out_specs=pl.BlockSpec(memory_space=pltpu.VMEM),
        scratch_shapes=[pltpu.SemaphoreType.DMA((tiles.shape[0] // CHUNK,))],
        compiler_params=pltpu.CompilerParams(vmem_limit_bytes=12 * 2**20),
        cost_estimate=pl.CostEstimate(
            flops=0, bytes_accessed=4 * math.prod(tiles.shape), transcendentals=0
        ),
        name="fetch_tiles",
    )(count, pltpu.with_memory_space_constraint(tiles, pltpu.HBM))


def tile_work(rows, cols, count, gath, n_col, ener, tiles):
    n_core = len(gath)
    n_far, kvec, own = gath[0].shape
    slots, area = tiles.shape
    side = math.isqrt(area)
    per = LANES // side
    blk_own = own // side
    n_seg = n_col * blk_own
    width = area // LANES * SUB
    vmem = pl.BlockSpec(memory_space=pltpu.VMEM)
    far_away = pl.BlockSpec(memory_space=pltpu.HBM)
    return pl.pallas_call(
        functools.partial(tile_kernel, n_core, n_col, side),
        out_shape=(
            jax.ShapeDtypeStruct((kvec, own), jnp.float32),
            jax.ShapeDtypeStruct((n_col - 1, kvec, own), jnp.bfloat16),
            jax.ShapeDtypeStruct((n_col - 1, kvec, own), jnp.float32),
        ),
        in_specs=[pl.BlockSpec(memory_space=pltpu.SMEM)] + [far_away] * 3 + [vmem] + [vmem] * n_core,
        out_specs=(vmem, vmem, vmem),
        scratch_shapes=[
            pltpu.SMEM((slots,), jnp.int32),
            pltpu.SMEM((slots,), jnp.int32),
            pltpu.VMEM((1, own), jnp.float32),
            pltpu.VMEM((n_far * n_core * blk_own + 1, per * kvec, LANES), jnp.bfloat16),
            pltpu.VMEM((n_seg // per * 2 * kvec, per * per * width), jnp.bfloat16),
            pltpu.VMEM((per * per * width, LANES), jnp.bfloat16),
            pltpu.VMEM((n_col, kvec, own), jnp.float32),
            pltpu.SemaphoreType.DMA((3,)),
        ] + [pltpu.VMEM((n_seg, per * kvec, width), jnp.float32)] * SUB,
        compiler_params=pltpu.CompilerParams(vmem_limit_bytes=32 * 2**20),
        cost_estimate=pl.CostEstimate(
            flops=2 * slots * area * kvec, bytes_accessed=2 * slots * area, transcendentals=0
        ),
        name="tile_work",
    )(count, *[pltpu.with_memory_space_constraint(x, pltpu.HBM) for x in (rows, cols, ener)],
      tiles,
      *gath)


def terms_kernel(own, rest, vec, *refs):
    others, (terms_ref, wide) = refs[:-2], refs[-2:]
    n_col = len(others) + 1
    kvec = vec.shape[0]

    def outer(share, seg):
        return lax.dot_general(
            share, seg[...].astype(jnp.float32), NT,
            precision=lax.Precision.HIGHEST, preferred_element_type=jnp.float32,
        )

    terms = outer(own[...], vec)
    for s in range(1, n_col):
        terms = terms + outer(rest[s - 1], others[n_col - s - 1])
    wide[...] = jnp.zeros(wide.shape, jnp.float32)
    wide[:, :kvec] = terms
    spaced = pltpu.roll(wide[...], 0, 1, stride=kvec, stride_axis=0)
    flat = jnp.sum(spaced, axis=0, keepdims=True)
    for i in range(terms_ref.shape[0]):
        terms_ref[i] = flat


def gram_terms(own, rest, vectors, others, members):
    vmem = pl.BlockSpec(memory_space=pltpu.VMEM)
    return pl.pallas_call(
        terms_kernel,
        out_shape=jax.ShapeDtypeStruct((members, 1, LANES), jnp.float32),
        in_specs=[vmem] * (3 + len(others)),
        out_specs=vmem,
        scratch_shapes=[pltpu.VMEM((vectors.shape[0], LANES), jnp.float32)],
        compiler_params=pltpu.CompilerParams(vmem_limit_bytes=4 * 2**20),
        name="gram_terms",
    )(own, rest, vectors, *others)


def finish_kernel(scale, base, gram_parts, vec, *refs):
    got, (product, residual) = refs[:-2], refs[-2:]
    whole = base[...]
    for piece in got:
        whole = whole + piece[...].astype(jnp.float32)
    product[...] = whole.astype(jnp.bfloat16)
    flat = gram_parts[0]
    for i in range(1, gram_parts.shape[0]):
        flat = flat + gram_parts[i]
    kvec = vec.shape[0]
    lane = lax.broadcasted_iota(jnp.int32, (kvec, LANES), 1)
    first = kvec * lax.broadcasted_iota(jnp.int32, (kvec, LANES), 0)
    wide = jnp.broadcast_to(flat * scale, (kvec, LANES))
    vec32 = vec[...].astype(jnp.float32)
    for a in range(kvec):
        column = jnp.sum(jnp.where(lane == first + a, wide, 0.0), axis=1, keepdims=True)
        whole = whole - column * vec32[a:a + 1, :]
    residual[...] = whole


def finish(scale, base, gram_parts, vectors, got):
    vmem = pl.BlockSpec(memory_space=pltpu.VMEM)
    return pl.pallas_call(
        functools.partial(finish_kernel, scale),
        out_shape=(
            jax.ShapeDtypeStruct(vectors.shape, jnp.bfloat16),
            jax.ShapeDtypeStruct(vectors.shape, jnp.float32),
        ),
        in_specs=[vmem] * (3 + len(got)),
        out_specs=(vmem, vmem),
        compiler_params=pltpu.CompilerParams(vmem_limit_bytes=4 * 2**20),
        name="finish",
    )(base, gram_parts, vectors, *got)


def from_all(x, axis):
    size = lax.axis_size(axis)
    got = [x]
    for s in range(1, size):
        got.append(lax.ppermute(x, axis, [(i, (i + s) % size) for i in range(size)]))
    return got


def copies_kernel(x, out, sems):
    copies = [pltpu.make_async_copy(x, out.at[i], sems.at[i]) for i in range(out.shape[0])]
    for copy in copies:
        copy.start()
    for copy in copies:
        copy.wait()


def repeat(x, size):
    return pl.pallas_call(
        copies_kernel,
        out_shape=jax.ShapeDtypeStruct((size,) + x.shape, x.dtype),
        in_specs=[pl.BlockSpec(memory_space=pltpu.HBM)],
        out_specs=pl.BlockSpec(memory_space=pltpu.VMEM),
        scratch_shapes=[pltpu.SemaphoreType.DMA((size,))],
        compiler_params=pltpu.CompilerParams(vmem_limit_bytes=4 * 2**20),
        name="copies",
    )(pltpu.with_memory_space_constraint(x, pltpu.HBM))


def per_device(vectors, energies, tiles, tile_rows, tile_cols, tile_count):
    kvec, own = vectors.shape
    n_col = lax.axis_size("col")
    fetched = fetch_tiles(tile_count, tiles)
    gath = lax.all_to_all(repeat(vectors, lax.axis_size("far")), "far", 0, 0)
    gath = from_all(gath, "core")
    base, send, rest = tile_work(
        tile_rows, tile_cols, tile_count, gath, n_col, energies[None, :], fetched
    )
    got = [
        lax.ppermute(send[s - 1], "col", [(c, (c + s) % n_col) for c in range(n_col)])
        for s in range(1, n_col)
    ]
    others = from_all(vectors, "col")[1:]
    members = lax.axis_size(("far", "core", "col"))
    terms = gram_terms(base, rest, vectors, others, members)
    gram_parts = lax.all_to_all(terms, ("far", "core", "col"), 0, 0)
    return finish(1.0 / (members * own), base, gram_parts, vectors, got)


def solution(mesh):
    n_row, n_col = mesh.devices.shape
    n_core = 2 if n_row % 2 == 0 else 1
    split = ("far", "core", "col")
    chips = Mesh(mesh.devices.reshape(n_row // n_core, n_core, n_col), split)
    in_specs = (P(None, split), P(split), P(split, None), P(split), P(split), P(split))
    out_specs = (P(None, split), P(None, split))
    return jax.shard_map(
        per_device, mesh=chips, in_specs=in_specs, out_specs=out_specs, check_vma=False
    )
```

```python
import functools
import math

import jax
import jax.numpy as jnp
from jax import lax
from jax.experimental import pallas as pl
from jax.experimental.pallas import tpu as pltpu
from jax.sharding import Mesh, PartitionSpec as P

LANES = 128
SUB = 8
CHUNK = 128

NT = (((1,), (1,)), ((), ()))


def tile_kernel(
    n_core, n_col, side, count_s, rows_h, cols_h, ener_h, tiles, *refs,
):
    gath, refs = refs[:n_core], refs[n_core:]
    (own_ref, send_ref, rest_ref, rows_s, cols_s, ener,
     buf, table, picked, select, part, sems, small, *acc) = refs
    n_far, kvec, own = gath[0].shape
    slots = tiles.shape[0]
    blk_own = own // side
    per = LANES // side
    n_chunk = tiles.shape[1] // LANES
    my_far, my_core, my_col = (lax.axis_index(name) for name in ("far", "core", "col"))

    copies = [
        pltpu.make_async_copy(src, dst, small.at[i])
        for i, (src, dst) in enumerate(
            ((cols_h, cols_s), (rows_h, rows_s), (ener_h, ener))
        )
    ]
    for copy in copies:
        copy.start()

    def tile_copy(ch):
        span = pl.ds(pl.multiple_of(ch * CHUNK, CHUNK), CHUNK)
        return pltpu.make_async_copy(tiles.at[span], buf.at[span], sems.at[ch])

    count = count_s[0]
    used = (count + CHUNK - 1) // CHUNK

    def start(ch, carry):
        tile_copy(ch).start()
        return carry

    lax.fori_loop(0, used, start, 0)

    lane = lax.broadcasted_iota(jnp.int32, (kvec, LANES), 1)
    low = lane < side
    zero = jnp.zeros((kvec, LANES), jnp.float32)

    for s in range(n_core):
        core = lax.rem(my_core + (n_core - s), n_core)
        for f in range(n_far):
            for p in range(own // LANES):
                x = gath[s][f, :, p * LANES:(p + 1) * LANES].astype(jnp.float32)
                y = pltpu.roll(x, side, 1)
                at = (f * n_core + core) * blk_own + p * per
                even = jnp.concatenate([jnp.where(low, x, zero), jnp.where(low, zero, y)], axis=0)
                odd = jnp.concatenate([jnp.where(low, y, zero), jnp.where(low, zero, x)], axis=0)
                table[at] = even
                table[at + 1] = odd
    n_blocks = n_far * n_core * blk_own
    table[n_blocks] = jnp.zeros((per * kvec, LANES), jnp.float32)

    for copy in copies:
        copy.wait()
    n_seg = acc[0].shape[0]
    width = n_chunk * SUB

    def clear(r, carry):
        for a in acc:
            a[r] = jnp.zeros(a.shape[1:], jnp.float32)
        return carry

    lax.fori_loop(0, n_seg, clear, 0)

    k_id = lax.broadcasted_iota(jnp.int32, (width, LANES), 0)
    n_id = lax.broadcasted_iota(jnp.int32, (width, LANES), 1)
    base_id = n_id - per * (k_id // SUB)
    for par in range(per):
        for jp in range(per):
            at = (par * per + jp) * width
            hit = (base_id == side * par + jp).astype(jnp.float32)
            select[at:at + width, :] = hit.astype(jnp.bfloat16)

    rows_of = per * kvec

    def product(base, half, x, check):
        xh = x[half * SUB:(half + 1) * SUB]
        w = jnp.concatenate(
            [xh[:, c * LANES:(c + 1) * LANES] for c in range(n_chunk)], axis=0
        ).astype(jnp.bfloat16)
        entries = []
        for t in range(SUB):
            slot = base + half * SUB + t
            at = cols_s[slot]
            entries.append(table[jnp.where(slot < count, at, n_blocks) if check else at])
        left = jnp.concatenate(entries, axis=0).astype(jnp.bfloat16)
        return lax.dot_general(left, w, NT, preferred_element_type=jnp.float32)

    def accumulate(at, out):
        for t in range(SUB):
            r = rows_s[at + t]
            acc[t][r] += out[t * rows_of:(t + 1) * rows_of]

    def one_chunk(ch, check):
        tile_copy(ch).wait()
        waiting = None
        for q in range(CHUNK // (2 * SUB)):
            base = pl.multiple_of(ch * CHUNK + q * 2 * SUB, 2 * SUB)
            x = buf[pl.ds(base, 2 * SUB), :].astype(jnp.float32)
            for half in range(2):
                out = product(base, half, x, check)
                if waiting is not None:
                    accumulate(*waiting)
                waiting = (base + half * SUB, out)
        accumulate(*waiting)

    def full_chunk(ch, carry):
        one_chunk(ch, False)
        return carry

    lax.fori_loop(0, count // CHUNK, full_chunk, 0)

    @pl.when(used > count // CHUNK)
    def _():
        one_chunk(used - 1, True)

    lane_w = lax.broadcasted_iota(jnp.int32, (rows_of, width), 1) % SUB
    pairs = n_seg // per

    def pick(m, carry):
        pieces = []
        for par in range(per):
            total = jnp.zeros((rows_of, width), jnp.float32)
            for t in range(SUB):
                total = jnp.where(lane_w == t, acc[t][m * per + par], total)
            for jp in range(per):
                pieces.append(total[jp * kvec:(jp + 1) * kvec])
        a = jnp.concatenate(pieces, axis=1)
        hi = a.astype(jnp.bfloat16).astype(jnp.float32)
        both = jnp.concatenate([hi, a - hi], axis=0).astype(jnp.bfloat16)
        picked[pl.ds(pl.multiple_of(m * 2 * kvec, 2 * kvec), 2 * kvec), :] = both
        return carry

    lax.fori_loop(0, pairs, pick, 0)

    spread = jnp.dot(picked[...], select[...], preferred_element_type=jnp.float32)
    for m in range(pairs):
        at = m * 2 * kvec
        row = spread[at:at + kvec] + spread[at + kvec:at + 2 * kvec]
        c, lane0 = divmod(m * LANES, own)
        part[c, :, lane0:lane0 + LANES] = row

    own_ref[...] = part[my_col] + ener[...] * gath[0][my_far].astype(jnp.float32)
    for s in range(1, n_col):
        share = part[lax.rem(my_col + s, n_col)]
        send_ref[s - 1] = share.astype(jnp.bfloat16)
        rest_ref[s - 1] = share


def tile_work(rows, cols, count, gath, n_col, ener, tiles):
    n_core = len(gath)
    n_far, kvec, own = gath[0].shape
    slots, area = tiles.shape
    side = math.isqrt(area)
    per = LANES // side
    blk_own = own // side
    n_seg = n_col * blk_own
    width = area // LANES * SUB
    vmem = pl.BlockSpec(memory_space=pltpu.VMEM)
    far_away = pl.BlockSpec(memory_space=pltpu.HBM)
    return pl.pallas_call(
        functools.partial(tile_kernel, n_core, n_col, side),
        out_shape=(
            jax.ShapeDtypeStruct((kvec, own), jnp.float32),
            jax.ShapeDtypeStruct((n_col - 1, kvec, own), jnp.bfloat16),
            jax.ShapeDtypeStruct((n_col - 1, kvec, own), jnp.float32),
        ),
        in_specs=[pl.BlockSpec(memory_space=pltpu.SMEM)] + [far_away] * 4 + [vmem] * n_core,
        out_specs=(vmem, vmem, vmem),
        scratch_shapes=[
            pltpu.SMEM((slots,), jnp.int32),
            pltpu.SMEM((slots,), jnp.int32),
            pltpu.VMEM((1, own), jnp.float32),
            pltpu.VMEM((slots, area), jnp.bfloat16),
            pltpu.VMEM((n_far * n_core * blk_own + 1, per * kvec, LANES), jnp.float32),
            pltpu.VMEM((n_seg // per * 2 * kvec, per * per * width), jnp.bfloat16),
            pltpu.VMEM((per * per * width, LANES), jnp.bfloat16),
            pltpu.VMEM((n_col, kvec, own), jnp.float32),
            pltpu.SemaphoreType.DMA((slots // CHUNK,)),
            pltpu.SemaphoreType.DMA((3,)),
        ] + [pltpu.VMEM((n_seg, per * kvec, width), jnp.float32)] * SUB,
        compiler_params=pltpu.CompilerParams(vmem_limit_bytes=48 * 2**20),
        cost_estimate=pl.CostEstimate(
            flops=2 * slots * area * kvec, bytes_accessed=2 * slots * area, transcendentals=0
        ),
        name="tile_work",
    )(count, *[pltpu.with_memory_space_constraint(x, pltpu.HBM) for x in (rows, cols, ener, tiles)],
      *gath)


def terms_kernel(own, rest, vec, *refs):
    others, (terms_ref, wide) = refs[:-2], refs[-2:]
    n_col = len(others) + 1
    kvec = vec.shape[0]

    def outer(share, seg):
        return lax.dot_general(
            share, seg[...].astype(jnp.float32), NT,
            precision=lax.Precision.HIGHEST, preferred_element_type=jnp.float32,
        )

    terms = outer(own[...], vec)
    for s in range(1, n_col):
        terms = terms + outer(rest[s - 1], others[n_col - s - 1])
    wide[...] = jnp.zeros(wide.shape, jnp.float32)
    wide[:, :kvec] = terms
    spaced = pltpu.roll(wide[...], 0, 1, stride=kvec, stride_axis=0)
    flat = jnp.sum(spaced, axis=0, keepdims=True)
    for i in range(terms_ref.shape[0]):
        terms_ref[i] = flat


def gram_terms(own, rest, vectors, others, members):
    vmem = pl.BlockSpec(memory_space=pltpu.VMEM)
    return pl.pallas_call(
        terms_kernel,
        out_shape=jax.ShapeDtypeStruct((members, 1, LANES), jnp.float32),
        in_specs=[vmem] * (3 + len(others)),
        out_specs=vmem,
        scratch_shapes=[pltpu.VMEM((vectors.shape[0], LANES), jnp.float32)],
        compiler_params=pltpu.CompilerParams(vmem_limit_bytes=4 * 2**20),
        name="gram_terms",
    )(own, rest, vectors, *others)


def finish_kernel(scale, base, gram_parts, vec, *refs):
    got, (product, residual) = refs[:-2], refs[-2:]
    whole = base[...]
    for piece in got:
        whole = whole + piece[...].astype(jnp.float32)
    product[...] = whole.astype(jnp.bfloat16)
    flat = gram_parts[0]
    for i in range(1, gram_parts.shape[0]):
        flat = flat + gram_parts[i]
    kvec = vec.shape[0]
    lane = lax.broadcasted_iota(jnp.int32, (kvec, LANES), 1)
    first = kvec * lax.broadcasted_iota(jnp.int32, (kvec, LANES), 0)
    wide = jnp.broadcast_to(flat * scale, (kvec, LANES))
    vec32 = vec[...].astype(jnp.float32)
    for a in range(kvec):
        column = jnp.sum(jnp.where(lane == first + a, wide, 0.0), axis=1, keepdims=True)
        whole = whole - column * vec32[a:a + 1, :]
    residual[...] = whole


def finish(scale, base, gram_parts, vectors, got):
    vmem = pl.BlockSpec(memory_space=pltpu.VMEM)
    return pl.pallas_call(
        functools.partial(finish_kernel, scale),
        out_shape=(
            jax.ShapeDtypeStruct(vectors.shape, jnp.bfloat16),
            jax.ShapeDtypeStruct(vectors.shape, jnp.float32),
        ),
        in_specs=[vmem] * (3 + len(got)),
        out_specs=(vmem, vmem),
        compiler_params=pltpu.CompilerParams(vmem_limit_bytes=4 * 2**20),
        name="finish",
    )(base, gram_parts, vectors, *got)


def from_all(x, axis):
    size = lax.axis_size(axis)
    got = [x]
    for s in range(1, size):
        got.append(lax.ppermute(x, axis, [(i, (i + s) % size) for i in range(size)]))
    return got


def per_device(vectors, energies, tiles, tile_rows, tile_cols, tile_count):
    kvec, own = vectors.shape
    n_col = lax.axis_size("col")
    copies = jnp.broadcast_to(vectors[None], (lax.axis_size("far"), kvec, own))
    gath = lax.all_to_all(copies, "far", 0, 0)
    gath = from_all(gath, "core")
    base, send, rest = tile_work(
        tile_rows, tile_cols, tile_count, gath, n_col, energies[None, :], tiles
    )
    got = [
        lax.ppermute(send[s - 1], "col", [(c, (c + s) % n_col) for c in range(n_col)])
        for s in range(1, n_col)
    ]
    others = from_all(vectors, "col")[1:]
    members = lax.axis_size(("far", "core", "col"))
    terms = gram_terms(base, rest, vectors, others, members)
    gram_parts = lax.all_to_all(terms, ("far", "core", "col"), 0, 0)
    return finish(1.0 / (members * own), base, gram_parts, vectors, got)


def solution(mesh):
    n_row, n_col = mesh.devices.shape
    n_core = 2 if n_row % 2 == 0 else 1
    split = ("far", "core", "col")
    chips = Mesh(mesh.devices.reshape(n_row // n_core, n_core, n_col), split)
    in_specs = (P(None, split), P(split), P(split, None), P(split), P(split), P(split))
    out_specs = (P(None, split), P(None, split))
    return jax.shard_map(
        per_device, mesh=chips, in_specs=in_specs, out_specs=out_specs, check_vma=False
    )
```

```python
import functools
import math

import jax
import jax.numpy as jnp
from jax import lax
from jax.experimental import pallas as pl
from jax.experimental.pallas import tpu as pltpu
from jax.sharding import Mesh, PartitionSpec as P

LANES = 128
SUB = 8
CHUNK = 128

NT = (((1,), (1,)), ((), ()))


def tile_kernel(
    n_core, n_col, side, count_s, rows_h, cols_h, ener_h, tiles, *refs,
):
    gath, refs = refs[:n_core], refs[n_core:]
    (own_ref, send_ref, rest_ref, rows_s, cols_s, ener,
     buf, table, picked, select, part, sems, small, *acc) = refs
    n_far, kvec, own = gath[0].shape
    slots = tiles.shape[0]
    blk_own = own // side
    per = LANES // side
    n_chunk = tiles.shape[1] // LANES
    my_far, my_core, my_col = (lax.axis_index(name) for name in ("far", "core", "col"))

    copies = [
        pltpu.make_async_copy(src, dst, small.at[i])
        for i, (src, dst) in enumerate(
            ((cols_h, cols_s), (rows_h, rows_s), (ener_h, ener))
        )
    ]
    for copy in copies:
        copy.start()

    def tile_copy(ch):
        span = pl.ds(pl.multiple_of(ch * CHUNK, CHUNK), CHUNK)
        return pltpu.make_async_copy(tiles.at[span], buf.at[span], sems.at[ch])

    count = count_s[0]
    used = (count + CHUNK - 1) // CHUNK

    def start(ch, carry):
        tile_copy(ch).start()
        return carry

    lax.fori_loop(0, used, start, 0)

    lane = lax.broadcasted_iota(jnp.int32, (kvec, LANES), 1)
    low = lane < side
    zero = jnp.zeros((kvec, LANES), jnp.float32)

    for s in range(n_core):
        core = lax.rem(my_core + (n_core - s), n_core)
        for f in range(n_far):
            for p in range(own // LANES):
                x = gath[s][f, :, p * LANES:(p + 1) * LANES].astype(jnp.float32)
                y = pltpu.roll(x, side, 1)
                at = (f * n_core + core) * blk_own + p * per
                even = jnp.concatenate([jnp.where(low, x, zero), jnp.where(low, zero, y)], axis=0)
                odd = jnp.concatenate([jnp.where(low, y, zero), jnp.where(low, zero, x)], axis=0)
                table[at] = even
                table[at + 1] = odd
    n_blocks = n_far * n_core * blk_own
    table[n_blocks] = jnp.zeros((per * kvec, LANES), jnp.float32)

    for copy in copies:
        copy.wait()
    n_seg = acc[0].shape[0]
    width = n_chunk * SUB

    def clear(r, carry):
        for a in acc:
            a[r] = jnp.zeros(a.shape[1:], jnp.float32)
        return carry

    lax.fori_loop(0, n_seg, clear, 0)

    k_id = lax.broadcasted_iota(jnp.int32, (width, LANES), 0)
    n_id = lax.broadcasted_iota(jnp.int32, (width, LANES), 1)
    base_id = n_id - per * (k_id // SUB)
    for par in range(per):
        for jp in range(per):
            at = (par * per + jp) * width
            hit = (base_id == side * par + jp).astype(jnp.float32)
            select[at:at + width, :] = hit.astype(jnp.bfloat16)

    rows_of = per * kvec

    def product(base, half, x, check):
        xh = x[half * SUB:(half + 1) * SUB]
        w = jnp.concatenate(
            [xh[:, c * LANES:(c + 1) * LANES] for c in range(n_chunk)], axis=0
        ).astype(jnp.bfloat16)
        entries = []
        for t in range(SUB):
            slot = base + half * SUB + t
            at = cols_s[slot]
            entries.append(table[jnp.where(slot < count, at, n_blocks) if check else at])
        left = jnp.concatenate(entries, axis=0).astype(jnp.bfloat16)
        return lax.dot_general(left, w, NT, preferred_element_type=jnp.float32)

    def accumulate(at, out):
        for t in range(SUB):
            r = rows_s[at + t]
            acc[t][r] += out[t * rows_of:(t + 1) * rows_of]

    def one_chunk(ch, check):
        tile_copy(ch).wait()
        waiting = None
        for q in range(CHUNK // (2 * SUB)):
            base = pl.multiple_of(ch * CHUNK + q * 2 * SUB, 2 * SUB)
            x = buf[pl.ds(base, 2 * SUB), :].astype(jnp.float32)
            for half in range(2):
                out = product(base, half, x, check)
                if waiting is not None:
                    accumulate(*waiting)
                waiting = (base + half * SUB, out)
        accumulate(*waiting)

    def full_chunk(ch, carry):
        one_chunk(ch, False)
        return carry

    lax.fori_loop(0, count // CHUNK, full_chunk, 0)

    @pl.when(used > count // CHUNK)
    def _():
        one_chunk(used - 1, True)

    lane_w = lax.broadcasted_iota(jnp.int32, (rows_of, width), 1) % SUB
    pairs = n_seg // per

    def pick(m, carry):
        pieces = []
        for par in range(per):
            total = jnp.zeros((rows_of, width), jnp.float32)
            for t in range(SUB):
                total = jnp.where(lane_w == t, acc[t][m * per + par], total)
            for jp in range(per):
                pieces.append(total[jp * kvec:(jp + 1) * kvec])
        a = jnp.concatenate(pieces, axis=1)
        hi = a.astype(jnp.bfloat16).astype(jnp.float32)
        both = jnp.concatenate([hi, a - hi], axis=0).astype(jnp.bfloat16)
        picked[pl.ds(pl.multiple_of(m * 2 * kvec, 2 * kvec), 2 * kvec), :] = both
        return carry

    lax.fori_loop(0, pairs, pick, 0)

    spread = jnp.dot(picked[...], select[...], preferred_element_type=jnp.float32)
    for m in range(pairs):
        at = m * 2 * kvec
        row = spread[at:at + kvec] + spread[at + kvec:at + 2 * kvec]
        c, lane0 = divmod(m * LANES, own)
        part[c, :, lane0:lane0 + LANES] = row

    own_ref[...] = part[my_col] + ener[...] * gath[0][my_far].astype(jnp.float32)
    for s in range(1, n_col):
        share = part[lax.rem(my_col + s, n_col)]
        send_ref[s - 1] = share.astype(jnp.bfloat16)
        rest_ref[s - 1] = share


def tile_work(rows, cols, count, gath, n_col, ener, tiles):
    n_core = len(gath)
    n_far, kvec, own = gath[0].shape
    slots, area = tiles.shape
    side = math.isqrt(area)
    per = LANES // side
    blk_own = own // side
    n_seg = n_col * blk_own
    width = area // LANES * SUB
    vmem = pl.BlockSpec(memory_space=pltpu.VMEM)
    far_away = pl.BlockSpec(memory_space=pltpu.HBM)
    return pl.pallas_call(
        functools.partial(tile_kernel, n_core, n_col, side),
        out_shape=(
            jax.ShapeDtypeStruct((kvec, own), jnp.float32),
            jax.ShapeDtypeStruct((n_col - 1, kvec, own), jnp.bfloat16),
            jax.ShapeDtypeStruct((n_col - 1, kvec, own), jnp.float32),
        ),
        in_specs=[pl.BlockSpec(memory_space=pltpu.SMEM)] + [far_away] * 4 + [vmem] * n_core,
        out_specs=(vmem, vmem, vmem),
        scratch_shapes=[
            pltpu.SMEM((slots,), jnp.int32),
            pltpu.SMEM((slots,), jnp.int32),
            pltpu.VMEM((1, own), jnp.float32),
            pltpu.VMEM((slots, area), jnp.bfloat16),
            pltpu.VMEM((n_far * n_core * blk_own + 1, per * kvec, LANES), jnp.float32),
            pltpu.VMEM((n_seg // per * 2 * kvec, per * per * width), jnp.bfloat16),
            pltpu.VMEM((per * per * width, LANES), jnp.bfloat16),
            pltpu.VMEM((n_col, kvec, own), jnp.float32),
            pltpu.SemaphoreType.DMA((slots // CHUNK,)),
            pltpu.SemaphoreType.DMA((3,)),
        ] + [pltpu.VMEM((n_seg, per * kvec, width), jnp.float32)] * SUB,
        compiler_params=pltpu.CompilerParams(vmem_limit_bytes=48 * 2**20),
        cost_estimate=pl.CostEstimate(
            flops=2 * slots * area * kvec, bytes_accessed=2 * slots * area, transcendentals=0
        ),
        name="tile_work",
    )(count, *[pltpu.with_memory_space_constraint(x, pltpu.HBM) for x in (rows, cols, ener, tiles)],
      *gath)


def terms_kernel(own, rest, vec, *refs):
    others, (terms_ref, wide) = refs[:-2], refs[-2:]
    n_col = len(others) + 1
    kvec = vec.shape[0]

    def outer(share, seg):
        return lax.dot_general(
            share, seg[...].astype(jnp.float32), NT,
            precision=lax.Precision.HIGHEST, preferred_element_type=jnp.float32,
        )

    terms = outer(own[...], vec)
    for s in range(1, n_col):
        terms = terms + outer(rest[s - 1], others[n_col - s - 1])
    wide[...] = jnp.zeros(wide.shape, jnp.float32)
    wide[:, :kvec] = terms
    spaced = pltpu.roll(wide[...], 0, 1, stride=kvec, stride_axis=0)
    terms_ref[...] = jnp.sum(spaced, axis=0, keepdims=True)


def gram_terms(own, rest, vectors, others):
    vmem = pl.BlockSpec(memory_space=pltpu.VMEM)
    return pl.pallas_call(
        terms_kernel,
        out_shape=jax.ShapeDtypeStruct((1, LANES), jnp.float32),
        in_specs=[vmem] * (3 + len(others)),
        out_specs=vmem,
        scratch_shapes=[pltpu.VMEM((vectors.shape[0], LANES), jnp.float32)],
        compiler_params=pltpu.CompilerParams(vmem_limit_bytes=4 * 2**20),
        name="gram_terms",
    )(own, rest, vectors, *others)


def finish_kernel(scale, base, gram_parts, vec, *refs):
    got, (product, residual) = refs[:-2], refs[-2:]
    whole = base[...]
    for piece in got:
        whole = whole + piece[...].astype(jnp.float32)
    product[...] = whole.astype(jnp.bfloat16)
    flat = gram_parts[0]
    for i in range(1, gram_parts.shape[0]):
        flat = flat + gram_parts[i]
    kvec = vec.shape[0]
    lane = lax.broadcasted_iota(jnp.int32, (kvec, LANES), 1)
    first = kvec * lax.broadcasted_iota(jnp.int32, (kvec, LANES), 0)
    wide = jnp.broadcast_to(flat * scale, (kvec, LANES))
    vec32 = vec[...].astype(jnp.float32)
    for a in range(kvec):
        column = jnp.sum(jnp.where(lane == first + a, wide, 0.0), axis=1, keepdims=True)
        whole = whole - column * vec32[a:a + 1, :]
    residual[...] = whole


def finish(scale, base, gram_parts, vectors, got):
    vmem = pl.BlockSpec(memory_space=pltpu.VMEM)
    return pl.pallas_call(
        functools.partial(finish_kernel, scale),
        out_shape=(
            jax.ShapeDtypeStruct(vectors.shape, jnp.bfloat16),
            jax.ShapeDtypeStruct(vectors.shape, jnp.float32),
        ),
        in_specs=[vmem] * (3 + len(got)),
        out_specs=(vmem, vmem),
        compiler_params=pltpu.CompilerParams(vmem_limit_bytes=4 * 2**20),
        name="finish",
    )(base, gram_parts, vectors, *got)


def from_all(x, axis):
    size = lax.axis_size(axis)
    got = [x]
    for s in range(1, size):
        got.append(lax.ppermute(x, axis, [(i, (i + s) % size) for i in range(size)]))
    return got


def per_device(vectors, energies, tiles, tile_rows, tile_cols, tile_count):
    kvec, own = vectors.shape
    n_col = lax.axis_size("col")
    copies = jnp.broadcast_to(vectors[None], (lax.axis_size("far"), kvec, own))
    gath = lax.all_to_all(copies, "far", 0, 0)
    gath = from_all(gath, "core")
    base, send, rest = tile_work(
        tile_rows, tile_cols, tile_count, gath, n_col, energies[None, :], tiles
    )
    got = [
        lax.ppermute(send[s - 1], "col", [(c, (c + s) % n_col) for c in range(n_col)])
        for s in range(1, n_col)
    ]
    others = from_all(vectors, "col")[1:]
    terms = sum(from_all(gram_terms(base, rest, vectors, others), "core"))
    members = lax.axis_size(("far", "col"))
    terms = jnp.broadcast_to(terms[None], (members,) + terms.shape)
    gram_parts = lax.all_to_all(terms, ("far", "col"), 0, 0)
    states = lax.axis_size(("far", "core", "col")) * own
    return finish(1.0 / states, base, gram_parts, vectors, got)


def solution(mesh):
    n_row, n_col = mesh.devices.shape
    n_core = 2 if n_row % 2 == 0 else 1
    split = ("far", "core", "col")
    chips = Mesh(mesh.devices.reshape(n_row // n_core, n_core, n_col), split)
    in_specs = (P(None, split), P(split), P(split, None), P(split), P(split), P(split))
    out_specs = (P(None, split), P(None, split))
    return jax.shard_map(
        per_device, mesh=chips, in_specs=in_specs, out_specs=out_specs, check_vma=False
    )
```

```python
import functools
import math

import jax
import jax.numpy as jnp
from jax import lax
from jax.experimental import pallas as pl
from jax.experimental.pallas import tpu as pltpu
from jax.sharding import Mesh, PartitionSpec as P

LANES = 128
SUB = 8
CHUNK = 128
STEP = 256
SUMS = 4

NT = (((1,), (1,)), ((), ()))


def tile_kernel(
    n_core, n_col, side, count_s, rows_h, cols_h, ener_h, tiles, *refs,
):
    gath, refs = refs[:n_core], refs[n_core:]
    (own_ref, send_ref, rest_ref, rows_s, cols_s, ener,
     buf, table, picked, select, part, sems, small, *acc) = refs
    n_far, kvec, own = gath[0].shape
    slots = tiles.shape[0]
    blk_own = own // side
    per = LANES // side
    n_chunk = tiles.shape[1] // LANES
    my_far, my_core, my_col = (lax.axis_index(name) for name in ("far", "core", "col"))

    copies = [
        pltpu.make_async_copy(src, dst, small.at[i])
        for i, (src, dst) in enumerate(
            ((cols_h, cols_s), (rows_h, rows_s), (ener_h, ener))
        )
    ]
    for copy in copies:
        copy.start()

    def tile_copy(ch):
        span = pl.ds(pl.multiple_of(ch * CHUNK, CHUNK), CHUNK)
        return pltpu.make_async_copy(tiles.at[span], buf.at[span], sems.at[ch])

    count = count_s[0]
    used = (count + CHUNK - 1) // CHUNK

    def start(ch, carry):
        tile_copy(ch).start()
        return carry

    lax.fori_loop(0, used, start, 0)

    lane = lax.broadcasted_iota(jnp.int32, (kvec, LANES), 1)
    low = lane < side
    zero = jnp.zeros((kvec, LANES), jnp.float32)

    for s in range(n_core):
        core = lax.rem(my_core + (n_core - s), n_core)
        for f in range(n_far):
            for p in range(own // LANES):
                x = gath[s][f, :, p * LANES:(p + 1) * LANES].astype(jnp.float32)
                y = pltpu.roll(x, side, 1)
                at = (f * n_core + core) * blk_own + p * per
                even = jnp.concatenate([jnp.where(low, x, zero), jnp.where(low, zero, y)], axis=0)
                odd = jnp.concatenate([jnp.where(low, y, zero), jnp.where(low, zero, x)], axis=0)
                table[at] = even
                table[at + 1] = odd
    n_blocks = n_far * n_core * blk_own
    table[n_blocks] = jnp.zeros((per * kvec, LANES), jnp.float32)

    for copy in copies:
        copy.wait()
    n_seg = acc[0].shape[0]
    width = n_chunk * SUB

    def clear(r, carry):
        for a in acc:
            a[r] = jnp.zeros(a.shape[1:], jnp.float32)
        return carry

    lax.fori_loop(0, n_seg, clear, 0)

    k_id = lax.broadcasted_iota(jnp.int32, (width, LANES), 0)
    n_id = lax.broadcasted_iota(jnp.int32, (width, LANES), 1)
    base_id = n_id - per * (k_id // SUB)
    for par in range(per):
        for jp in range(per):
            at = (par * per + jp) * width
            hit = (base_id == side * par + jp).astype(jnp.float32)
            select[at:at + width, :] = hit.astype(jnp.bfloat16)

    rows_of = per * kvec

    def product(base, half, x, check):
        xh = x[half * SUB:(half + 1) * SUB]
        w = jnp.concatenate(
            [xh[:, c * LANES:(c + 1) * LANES] for c in range(n_chunk)], axis=0
        ).astype(jnp.bfloat16)
        entries = []
        for t in range(SUB):
            slot = base + half * SUB + t
            at = cols_s[slot]
            entries.append(table[jnp.where(slot < count, at, n_blocks) if check else at])
        left = jnp.concatenate(entries, axis=0).astype(jnp.bfloat16)
        return lax.dot_general(left, w, NT, preferred_element_type=jnp.float32)

    lane_w = lax.broadcasted_iota(jnp.int32, (rows_of, width), 1) % SUB

    def accumulate(at, out):
        for t in range(SUB):
            r = rows_s[at + t]
            mine = jnp.where(lane_w == t, out[t * rows_of:(t + 1) * rows_of], 0.0)
            acc[t % len(acc)][r] += mine

    def step(first, slots_in, check):
        for i in range(slots_in // CHUNK):
            tile_copy(first // CHUNK + i).wait()
        waiting = None
        for q in range(slots_in // (2 * SUB)):
            base = pl.multiple_of(first + q * 2 * SUB, 2 * SUB)
            x = buf[pl.ds(base, 2 * SUB), :].astype(jnp.float32)
            for half in range(2):
                out = product(base, half, x, check)
                if waiting is not None:
                    accumulate(*waiting)
                waiting = (base + half * SUB, out)
        accumulate(*waiting)

    def full_step(i, carry):
        step(i * STEP, STEP, False)
        return carry

    def last_step(ch, carry):
        step(ch * CHUNK, CHUNK, True)
        return carry

    full = count // STEP
    lax.fori_loop(0, full, full_step, 0)
    lax.fori_loop(full * (STEP // CHUNK), used, last_step, 0)

    pairs = n_seg // per

    def pick(m, carry):
        pieces = []
        for par in range(per):
            total = acc[0][m * per + par]
            for other in acc[1:]:
                total = total + other[m * per + par]
            for jp in range(per):
                pieces.append(total[jp * kvec:(jp + 1) * kvec])
        a = jnp.concatenate(pieces, axis=1)
        hi = a.astype(jnp.bfloat16).astype(jnp.float32)
        both = jnp.concatenate([hi, a - hi], axis=0).astype(jnp.bfloat16)
        picked[pl.ds(pl.multiple_of(m * 2 * kvec, 2 * kvec), 2 * kvec), :] = both
        return carry

    lax.fori_loop(0, pairs, pick, 0)

    spread = jnp.dot(picked[...], select[...], preferred_element_type=jnp.float32)
    for m in range(pairs):
        at = m * 2 * kvec
        row = spread[at:at + kvec] + spread[at + kvec:at + 2 * kvec]
        c, lane0 = divmod(m * LANES, own)
        part[c, :, lane0:lane0 + LANES] = row

    own_ref[...] = part[my_col] + ener[...] * gath[0][my_far].astype(jnp.float32)
    for s in range(1, n_col):
        share = part[lax.rem(my_col + s, n_col)]
        send_ref[s - 1] = share.astype(jnp.bfloat16)
        rest_ref[s - 1] = share


def tile_work(rows, cols, count, gath, n_col, ener, tiles):
    n_core = len(gath)
    n_far, kvec, own = gath[0].shape
    slots, area = tiles.shape
    side = math.isqrt(area)
    per = LANES // side
    blk_own = own // side
    n_seg = n_col * blk_own
    width = area // LANES * SUB
    vmem = pl.BlockSpec(memory_space=pltpu.VMEM)
    far_away = pl.BlockSpec(memory_space=pltpu.HBM)
    return pl.pallas_call(
        functools.partial(tile_kernel, n_core, n_col, side),
        out_shape=(
            jax.ShapeDtypeStruct((kvec, own), jnp.float32),
            jax.ShapeDtypeStruct((n_col - 1, kvec, own), jnp.bfloat16),
            jax.ShapeDtypeStruct((n_col - 1, kvec, own), jnp.float32),
        ),
        in_specs=[pl.BlockSpec(memory_space=pltpu.SMEM)] + [far_away] * 4 + [vmem] * n_core,
        out_specs=(vmem, vmem, vmem),
        scratch_shapes=[
            pltpu.SMEM((slots,), jnp.int32),
            pltpu.SMEM((slots,), jnp.int32),
            pltpu.VMEM((1, own), jnp.float32),
            pltpu.VMEM((slots, area), jnp.bfloat16),
            pltpu.VMEM((n_far * n_core * blk_own + 1, per * kvec, LANES), jnp.float32),
            pltpu.VMEM((n_seg // per * 2 * kvec, per * per * width), jnp.bfloat16),
            pltpu.VMEM((per * per * width, LANES), jnp.bfloat16),
            pltpu.VMEM((n_col, kvec, own), jnp.float32),
            pltpu.SemaphoreType.DMA((slots // CHUNK,)),
            pltpu.SemaphoreType.DMA((3,)),
        ] + [pltpu.VMEM((n_seg, per * kvec, width), jnp.float32)] * SUMS,
        compiler_params=pltpu.CompilerParams(vmem_limit_bytes=48 * 2**20),
        cost_estimate=pl.CostEstimate(
            flops=2 * slots * area * kvec, bytes_accessed=2 * slots * area, transcendentals=0
        ),
        name="tile_work",
    )(count, *[pltpu.with_memory_space_constraint(x, pltpu.HBM) for x in (rows, cols, ener, tiles)],
      *gath)


def terms_kernel(own, rest, vec, *refs):
    others, (terms_ref, wide) = refs[:-2], refs[-2:]
    n_col = len(others) + 1
    kvec = vec.shape[0]

    def outer(share, seg):
        return lax.dot_general(
            share, seg[...].astype(jnp.float32), NT,
            precision=lax.Precision.HIGHEST, preferred_element_type=jnp.float32,
        )

    terms = outer(own[...], vec)
    for s in range(1, n_col):
        terms = terms + outer(rest[s - 1], others[n_col - s - 1])
    wide[...] = jnp.zeros(wide.shape, jnp.float32)
    wide[:, :kvec] = terms
    spaced = pltpu.roll(wide[...], 0, 1, stride=kvec, stride_axis=0)
    terms_ref[...] = jnp.sum(spaced, axis=0, keepdims=True)


def gram_terms(own, rest, vectors, others):
    vmem = pl.BlockSpec(memory_space=pltpu.VMEM)
    return pl.pallas_call(
        terms_kernel,
        out_shape=jax.ShapeDtypeStruct((1, LANES), jnp.float32),
        in_specs=[vmem] * (3 + len(others)),
        out_specs=vmem,
        scratch_shapes=[pltpu.VMEM((vectors.shape[0], LANES), jnp.float32)],
        compiler_params=pltpu.CompilerParams(vmem_limit_bytes=4 * 2**20),
        name="gram_terms",
    )(own, rest, vectors, *others)


def finish_kernel(scale, base, gram_parts, vec, *refs):
    got, (product, residual) = refs[:-2], refs[-2:]
    whole = base[...]
    for piece in got:
        whole = whole + piece[...].astype(jnp.float32)
    product[...] = whole.astype(jnp.bfloat16)
    flat = gram_parts[0]
    for i in range(1, gram_parts.shape[0]):
        flat = flat + gram_parts[i]
    kvec = vec.shape[0]
    lane = lax.broadcasted_iota(jnp.int32, (kvec, LANES), 1)
    first = kvec * lax.broadcasted_iota(jnp.int32, (kvec, LANES), 0)
    wide = jnp.broadcast_to(flat * scale, (kvec, LANES))
    vec32 = vec[...].astype(jnp.float32)
    for a in range(kvec):
        column = jnp.sum(jnp.where(lane == first + a, wide, 0.0), axis=1, keepdims=True)
        whole = whole - column * vec32[a:a + 1, :]
    residual[...] = whole


def finish(scale, base, gram_parts, vectors, got):
    vmem = pl.BlockSpec(memory_space=pltpu.VMEM)
    return pl.pallas_call(
        functools.partial(finish_kernel, scale),
        out_shape=(
            jax.ShapeDtypeStruct(vectors.shape, jnp.bfloat16),
            jax.ShapeDtypeStruct(vectors.shape, jnp.float32),
        ),
        in_specs=[vmem] * (3 + len(got)),
        out_specs=(vmem, vmem),
        compiler_params=pltpu.CompilerParams(vmem_limit_bytes=4 * 2**20),
        name="finish",
    )(base, gram_parts, vectors, *got)


def from_all(x, axis):
    size = lax.axis_size(axis)
    got = [x]
    for s in range(1, size):
        got.append(lax.ppermute(x, axis, [(i, (i + s) % size) for i in range(size)]))
    return got


def per_device(vectors, energies, tiles, tile_rows, tile_cols, tile_count):
    kvec, own = vectors.shape
    n_col = lax.axis_size("col")
    copies = jnp.broadcast_to(vectors[None], (lax.axis_size("far"), kvec, own))
    gath = lax.all_to_all(copies, "far", 0, 0)
    gath = from_all(gath, "core")
    base, send, rest = tile_work(
        tile_rows, tile_cols, tile_count, gath, n_col, energies[None, :], tiles
    )
    got = [
        lax.ppermute(send[s - 1], "col", [(c, (c + s) % n_col) for c in range(n_col)])
        for s in range(1, n_col)
    ]
    others = from_all(vectors, "col")[1:]
    members = lax.axis_size(("far", "core", "col"))
    terms = gram_terms(base, rest, vectors, others)
    terms = jnp.broadcast_to(terms[None], (members,) + terms.shape)
    gram_parts = lax.all_to_all(terms, ("far", "core", "col"), 0, 0)
    return finish(1.0 / (members * own), base, gram_parts, vectors, got)


def solution(mesh):
    n_row, n_col = mesh.devices.shape
    n_core = 2 if n_row % 2 == 0 else 1
    split = ("far", "core", "col")
    chips = Mesh(mesh.devices.reshape(n_row // n_core, n_core, n_col), split)
    in_specs = (P(None, split), P(split), P(split, None), P(split), P(split), P(split))
    out_specs = (P(None, split), P(None, split))
    return jax.shard_map(
        per_device, mesh=chips, in_specs=in_specs, out_specs=out_specs, check_vma=False
    )
```

```python
import functools
import math

import jax
import jax.numpy as jnp
from jax import lax
from jax.experimental import pallas as pl
from jax.experimental.pallas import tpu as pltpu
from jax.sharding import Mesh, PartitionSpec as P

LANES = 128
SUB = 8
CHUNK = 128
STEP = 256
SUMS = 4

NT = (((1,), (1,)), ((), ()))


def tile_kernel(
    n_core, n_col, side, count_s, rows_h, cols_h, ener_h, vec_h, tiles, *refs,
):
    gath, refs = refs[:n_core], refs[n_core:]
    (own_ref, send_ref, rest_ref, rows_s, cols_s, ener, vec,
     buf, table, picked, select, part, sems, small, *acc) = refs
    kvec, own = vec.shape
    n_row = gath[0].shape[0]
    slots = tiles.shape[0]
    blk_own = own // side
    per = LANES // side
    n_chunk = tiles.shape[1] // LANES
    my_core, my_col = lax.axis_index("core"), lax.axis_index("col")

    copies = [
        pltpu.make_async_copy(src, dst, small.at[i])
        for i, (src, dst) in enumerate(
            ((cols_h, cols_s), (rows_h, rows_s), (ener_h, ener), (vec_h, vec))
        )
    ]
    for copy in copies:
        copy.start()

    def tile_copy(ch):
        span = pl.ds(pl.multiple_of(ch * CHUNK, CHUNK), CHUNK)
        return pltpu.make_async_copy(tiles.at[span], buf.at[span], sems.at[ch])

    count = count_s[0]
    used = (count + CHUNK - 1) // CHUNK

    def start(ch, carry):
        tile_copy(ch).start()
        return carry

    lax.fori_loop(0, used, start, 0)

    lane = lax.broadcasted_iota(jnp.int32, (kvec, LANES), 1)
    low = lane < side
    zero = jnp.zeros((kvec, LANES), jnp.float32)

    half = own // n_core
    for s in range(n_core):
        part_of = lax.rem(my_core + (n_core - s), n_core) * (half // side)
        for r in range(n_row):
            for p in range(half // LANES):
                x = gath[s][r, :, p * LANES:(p + 1) * LANES].astype(jnp.float32)
                y = pltpu.roll(x, side, 1)
                at = r * blk_own + part_of + p * per
                even = jnp.concatenate([jnp.where(low, x, zero), jnp.where(low, zero, y)], axis=0)
                odd = jnp.concatenate([jnp.where(low, y, zero), jnp.where(low, zero, x)], axis=0)
                table[at] = even
                table[at + 1] = odd
    n_blocks = n_row * blk_own
    table[n_blocks] = jnp.zeros((per * kvec, LANES), jnp.float32)

    for copy in copies:
        copy.wait()
    n_seg = acc[0].shape[0]
    width = n_chunk * SUB

    def clear(r, carry):
        for a in acc:
            a[r] = jnp.zeros(a.shape[1:], jnp.float32)
        return carry

    lax.fori_loop(0, n_seg, clear, 0)

    k_id = lax.broadcasted_iota(jnp.int32, (width, LANES), 0)
    n_id = lax.broadcasted_iota(jnp.int32, (width, LANES), 1)
    base_id = n_id - per * (k_id // SUB)
    for par in range(per):
        for jp in range(per):
            at = (par * per + jp) * width
            hit = (base_id == side * par + jp).astype(jnp.float32)
            select[at:at + width, :] = hit.astype(jnp.bfloat16)

    rows_of = per * kvec

    def product(base, half, x, check):
        xh = x[half * SUB:(half + 1) * SUB]
        w = jnp.concatenate(
            [xh[:, c * LANES:(c + 1) * LANES] for c in range(n_chunk)], axis=0
        ).astype(jnp.bfloat16)
        entries = []
        for t in range(SUB):
            slot = base + half * SUB + t
            at = cols_s[slot]
            entries.append(table[jnp.where(slot < count, at, n_blocks) if check else at])
        left = jnp.concatenate(entries, axis=0).astype(jnp.bfloat16)
        return lax.dot_general(left, w, NT, preferred_element_type=jnp.float32)

    lane_w = lax.broadcasted_iota(jnp.int32, (rows_of, width), 1) % SUB

    def accumulate(at, out):
        for t in range(SUB):
            r = rows_s[at + t]
            mine = jnp.where(lane_w == t, out[t * rows_of:(t + 1) * rows_of], 0.0)
            acc[t % len(acc)][r] += mine

    def step(first, slots_in, check):
        for i in range(slots_in // CHUNK):
            tile_copy(first // CHUNK + i).wait()
        waiting = None
        for q in range(slots_in // (2 * SUB)):
            base = pl.multiple_of(first + q * 2 * SUB, 2 * SUB)
            x = buf[pl.ds(base, 2 * SUB), :].astype(jnp.float32)
            for half in range(2):
                out = product(base, half, x, check)
                if waiting is not None:
                    accumulate(*waiting)
                waiting = (base + half * SUB, out)
        accumulate(*waiting)

    def full_step(i, carry):
        step(i * STEP, STEP, False)
        return carry

    def last_step(ch, carry):
        step(ch * CHUNK, CHUNK, True)
        return carry

    full = count // STEP
    lax.fori_loop(0, full, full_step, 0)
    lax.fori_loop(full * (STEP // CHUNK), used, last_step, 0)

    pairs = n_seg // per

    def pick(m, carry):
        pieces = []
        for par in range(per):
            total = acc[0][m * per + par]
            for other in acc[1:]:
                total = total + other[m * per + par]
            for jp in range(per):
                pieces.append(total[jp * kvec:(jp + 1) * kvec])
        a = jnp.concatenate(pieces, axis=1)
        hi = a.astype(jnp.bfloat16).astype(jnp.float32)
        both = jnp.concatenate([hi, a - hi], axis=0).astype(jnp.bfloat16)
        picked[pl.ds(pl.multiple_of(m * 2 * kvec, 2 * kvec), 2 * kvec), :] = both
        return carry

    lax.fori_loop(0, pairs, pick, 0)

    spread = jnp.dot(picked[...], select[...], preferred_element_type=jnp.float32)
    for m in range(pairs):
        at = m * 2 * kvec
        row = spread[at:at + kvec] + spread[at + kvec:at + 2 * kvec]
        c, lane0 = divmod(m * LANES, own)
        part[c, :, lane0:lane0 + LANES] = row

    own_ref[...] = part[my_col] + ener[...] * vec[...].astype(jnp.float32)
    for s in range(1, n_col):
        share = part[lax.rem(my_col + s, n_col)]
        send_ref[s - 1] = share.astype(jnp.bfloat16)
        rest_ref[s - 1] = share


def tile_work(rows, cols, count, vec, gath, n_col, ener, tiles):
    n_core = len(gath)
    kvec, own = vec.shape
    n_row = gath[0].shape[0]
    slots, area = tiles.shape
    side = math.isqrt(area)
    per = LANES // side
    blk_own = own // side
    n_seg = n_col * blk_own
    width = area // LANES * SUB
    vmem = pl.BlockSpec(memory_space=pltpu.VMEM)
    far_away = pl.BlockSpec(memory_space=pltpu.HBM)
    return pl.pallas_call(
        functools.partial(tile_kernel, n_core, n_col, side),
        out_shape=(
            jax.ShapeDtypeStruct((kvec, own), jnp.float32),
            jax.ShapeDtypeStruct((n_col - 1, kvec, own), jnp.bfloat16),
            jax.ShapeDtypeStruct((n_col - 1, kvec, own), jnp.float32),
        ),
        in_specs=[pl.BlockSpec(memory_space=pltpu.SMEM)] + [far_away] * 5 + [vmem] * n_core,
        out_specs=(vmem, vmem, vmem),
        scratch_shapes=[
            pltpu.SMEM((slots,), jnp.int32),
            pltpu.SMEM((slots,), jnp.int32),
            pltpu.VMEM((1, own), jnp.float32),
            pltpu.VMEM((kvec, own), jnp.bfloat16),
            pltpu.VMEM((slots, area), jnp.bfloat16),
            pltpu.VMEM((n_row * blk_own + 1, per * kvec, LANES), jnp.float32),
            pltpu.VMEM((n_seg // per * 2 * kvec, per * per * width), jnp.bfloat16),
            pltpu.VMEM((per * per * width, LANES), jnp.bfloat16),
            pltpu.VMEM((n_col, kvec, own), jnp.float32),
            pltpu.SemaphoreType.DMA((slots // CHUNK,)),
            pltpu.SemaphoreType.DMA((4,)),
        ] + [pltpu.VMEM((n_seg, per * kvec, width), jnp.float32)] * SUMS,
        compiler_params=pltpu.CompilerParams(vmem_limit_bytes=48 * 2**20),
        cost_estimate=pl.CostEstimate(
            flops=2 * slots * area * kvec, bytes_accessed=2 * slots * area, transcendentals=0
        ),
        name="tile_work",
    )(count, *[pltpu.with_memory_space_constraint(x, pltpu.HBM) for x in (rows, cols, ener, vec, tiles)],
      *gath)


def terms_kernel(own, rest, vec, *refs):
    others, (terms_ref, wide) = refs[:-2], refs[-2:]
    n_col = len(others) + 1
    kvec = vec.shape[0]

    def outer(share, seg):
        return lax.dot_general(
            share, seg[...].astype(jnp.float32), NT,
            precision=lax.Precision.HIGHEST, preferred_element_type=jnp.float32,
        )

    terms = outer(own[...], vec)
    for s in range(1, n_col):
        terms = terms + outer(rest[s - 1], others[n_col - s - 1])
    wide[...] = jnp.zeros(wide.shape, jnp.float32)
    wide[:, :kvec] = terms
    spaced = pltpu.roll(wide[...], 0, 1, stride=kvec, stride_axis=0)
    terms_ref[...] = jnp.sum(spaced, axis=0, keepdims=True)


def gram_terms(own, rest, vectors, others):
    vmem = pl.BlockSpec(memory_space=pltpu.VMEM)
    return pl.pallas_call(
        terms_kernel,
        out_shape=jax.ShapeDtypeStruct((1, LANES), jnp.float32),
        in_specs=[vmem] * (3 + len(others)),
        out_specs=vmem,
        scratch_shapes=[pltpu.VMEM((vectors.shape[0], LANES), jnp.float32)],
        compiler_params=pltpu.CompilerParams(vmem_limit_bytes=4 * 2**20),
        name="gram_terms",
    )(own, rest, vectors, *others)


def finish_kernel(scale, base, gram_parts, vec, *refs):
    got, (product, residual) = refs[:-2], refs[-2:]
    whole = base[...]
    for piece in got:
        whole = whole + piece[...].astype(jnp.float32)
    product[...] = whole.astype(jnp.bfloat16)
    flat = gram_parts[0]
    for i in range(1, gram_parts.shape[0]):
        flat = flat + gram_parts[i]
    kvec = vec.shape[0]
    lane = lax.broadcasted_iota(jnp.int32, (kvec, LANES), 1)
    first = kvec * lax.broadcasted_iota(jnp.int32, (kvec, LANES), 0)
    wide = jnp.broadcast_to(flat * scale, (kvec, LANES))
    vec32 = vec[...].astype(jnp.float32)
    for a in range(kvec):
        column = jnp.sum(jnp.where(lane == first + a, wide, 0.0), axis=1, keepdims=True)
        whole = whole - column * vec32[a:a + 1, :]
    residual[...] = whole


def finish(scale, base, gram_parts, vectors, got):
    vmem = pl.BlockSpec(memory_space=pltpu.VMEM)
    return pl.pallas_call(
        functools.partial(finish_kernel, scale),
        out_shape=(
            jax.ShapeDtypeStruct(vectors.shape, jnp.bfloat16),
            jax.ShapeDtypeStruct(vectors.shape, jnp.float32),
        ),
        in_specs=[vmem] * (3 + len(got)),
        out_specs=(vmem, vmem),
        compiler_params=pltpu.CompilerParams(vmem_limit_bytes=4 * 2**20),
        name="finish",
    )(base, gram_parts, vectors, *got)


def from_all(x, axis):
    size = lax.axis_size(axis)
    got = [x]
    for s in range(1, size):
        got.append(lax.ppermute(x, axis, [(i, (i + s) % size) for i in range(size)]))
    return got


def per_device(vectors, energies, tiles, tile_rows, tile_cols, tile_count):
    kvec, own = vectors.shape
    n_col = lax.axis_size("col")
    n_core = lax.axis_size("core")
    n_row = lax.axis_size("far") * n_core
    halves = vectors.reshape(kvec, n_core, own // n_core).swapaxes(0, 1)
    copies = jnp.broadcast_to(halves[None], (n_row // n_core,) + halves.shape)
    gath = lax.all_to_all(copies.reshape((n_row,) + halves.shape[1:]), ("far", "core"), 0, 0)
    gath = from_all(gath, "core")
    base, send, rest = tile_work(
        tile_rows, tile_cols, tile_count, vectors, gath, n_col, energies[None, :], tiles
    )
    got = [
        lax.ppermute(send[s - 1], "col", [(c, (c + s) % n_col) for c in range(n_col)])
        for s in range(1, n_col)
    ]
    others = from_all(vectors, "col")[1:]
    members = lax.axis_size(("far", "core", "col"))
    terms = gram_terms(base, rest, vectors, others)
    terms = jnp.broadcast_to(terms[None], (members,) + terms.shape)
    gram_parts = lax.all_to_all(terms, ("far", "core", "col"), 0, 0)
    return finish(1.0 / (members * own), base, gram_parts, vectors, got)


def solution(mesh):
    n_row, n_col = mesh.devices.shape
    n_core = 2 if n_row % 2 == 0 else 1
    split = ("far", "core", "col")
    chips = Mesh(mesh.devices.reshape(n_row // n_core, n_core, n_col), split)
    in_specs = (P(None, split), P(split), P(split, None), P(split), P(split), P(split))
    out_specs = (P(None, split), P(None, split))
    return jax.shard_map(
        per_device, mesh=chips, in_specs=in_specs, out_specs=out_specs, check_vma=False
    )
```

```python
import functools
import math

import jax
import jax.numpy as jnp
from jax import lax
from jax.experimental import pallas as pl
from jax.experimental.pallas import tpu as pltpu
from jax.sharding import PartitionSpec as P

LANES = 128
SUB = 8
CHUNK = 128
STEP = 256
SUMS = 4

NT = (((1,), (1,)), ((), ()))


def tile_kernel(
    n_core, n_col, side, count_s, rows_h, cols_h, ener_h, vec_h, tiles, *refs,
):
    gath, refs = refs[:n_core], refs[n_core:]
    (own_ref, send_ref, rest_ref, rows_s, cols_s, ener, vec,
     buf, table, picked, select, part, sems, small, *acc) = refs
    kvec, own = vec.shape
    n_row = gath[0].shape[0]
    slots = tiles.shape[0]
    blk_own = own // side
    per = LANES // side
    n_chunk = tiles.shape[1] // LANES
    my_core, my_col = lax.axis_index("row") % n_core, lax.axis_index("col")

    copies = [
        pltpu.make_async_copy(src, dst, small.at[i])
        for i, (src, dst) in enumerate(
            ((cols_h, cols_s), (rows_h, rows_s), (ener_h, ener), (vec_h, vec))
        )
    ]
    for copy in copies:
        copy.start()

    def tile_copy(ch):
        span = pl.ds(pl.multiple_of(ch * CHUNK, CHUNK), CHUNK)
        return pltpu.make_async_copy(tiles.at[span], buf.at[span], sems.at[ch])

    count = count_s[0]
    used = (count + CHUNK - 1) // CHUNK

    def start(ch, carry):
        tile_copy(ch).start()
        return carry

    lax.fori_loop(0, used, start, 0)

    lane = lax.broadcasted_iota(jnp.int32, (kvec, LANES), 1)
    low = lane < side
    zero = jnp.zeros((kvec, LANES), jnp.float32)

    half = own // n_core
    for s in range(n_core):
        part_of = lax.rem(my_core + (n_core - s), n_core) * (half // side)
        for r in range(n_row):
            for p in range(half // LANES):
                x = gath[s][r, :, p * LANES:(p + 1) * LANES].astype(jnp.float32)
                y = pltpu.roll(x, side, 1)
                at = r * blk_own + part_of + p * per
                even = jnp.concatenate([jnp.where(low, x, zero), jnp.where(low, zero, y)], axis=0)
                odd = jnp.concatenate([jnp.where(low, y, zero), jnp.where(low, zero, x)], axis=0)
                table[at] = even
                table[at + 1] = odd
    n_blocks = n_row * blk_own
    table[n_blocks] = jnp.zeros((per * kvec, LANES), jnp.float32)

    for copy in copies:
        copy.wait()
    n_seg = acc[0].shape[0]
    width = n_chunk * SUB

    def clear(r, carry):
        for a in acc:
            a[r] = jnp.zeros(a.shape[1:], jnp.float32)
        return carry

    lax.fori_loop(0, n_seg, clear, 0)

    k_id = lax.broadcasted_iota(jnp.int32, (width, LANES), 0)
    n_id = lax.broadcasted_iota(jnp.int32, (width, LANES), 1)
    base_id = n_id - per * (k_id // SUB)
    for par in range(per):
        for jp in range(per):
            at = (par * per + jp) * width
            hit = (base_id == side * par + jp).astype(jnp.float32)
            select[at:at + width, :] = hit.astype(jnp.bfloat16)

    rows_of = per * kvec

    def product(base, half, x, check):
        xh = x[half * SUB:(half + 1) * SUB]
        w = jnp.concatenate(
            [xh[:, c * LANES:(c + 1) * LANES] for c in range(n_chunk)], axis=0
        ).astype(jnp.bfloat16)
        entries = []
        for t in range(SUB):
            slot = base + half * SUB + t
            at = cols_s[slot]
            entries.append(table[jnp.where(slot < count, at, n_blocks) if check else at])
        left = jnp.concatenate(entries, axis=0).astype(jnp.bfloat16)
        return lax.dot_general(left, w, NT, preferred_element_type=jnp.float32)

    lane_w = lax.broadcasted_iota(jnp.int32, (rows_of, width), 1) % SUB

    def accumulate(at, out):
        for t in range(SUB):
            r = rows_s[at + t]
            mine = jnp.where(lane_w == t, out[t * rows_of:(t + 1) * rows_of], 0.0)
            acc[t % len(acc)][r] += mine

    def step(first, slots_in, check):
        for i in range(slots_in // CHUNK):
            tile_copy(first // CHUNK + i).wait()
        waiting = None
        for q in range(slots_in // (2 * SUB)):
            base = pl.multiple_of(first + q * 2 * SUB, 2 * SUB)
            x = buf[pl.ds(base, 2 * SUB), :].astype(jnp.float32)
            for half in range(2):
                out = product(base, half, x, check)
                if waiting is not None:
                    accumulate(*waiting)
                waiting = (base + half * SUB, out)
        accumulate(*waiting)

    def full_step(i, carry):
        step(i * STEP, STEP, False)
        return carry

    def last_step(ch, carry):
        step(ch * CHUNK, CHUNK, True)
        return carry

    full = count // STEP
    lax.fori_loop(0, full, full_step, 0)
    lax.fori_loop(full * (STEP // CHUNK), used, last_step, 0)

    pairs = n_seg // per

    def pick(m, carry):
        pieces = []
        for par in range(per):
            total = acc[0][m * per + par]
            for other in acc[1:]:
                total = total + other[m * per + par]
            for jp in range(per):
                pieces.append(total[jp * kvec:(jp + 1) * kvec])
        a = jnp.concatenate(pieces, axis=1)
        hi = a.astype(jnp.bfloat16).astype(jnp.float32)
        both = jnp.concatenate([hi, a - hi], axis=0).astype(jnp.bfloat16)
        picked[pl.ds(pl.multiple_of(m * 2 * kvec, 2 * kvec), 2 * kvec), :] = both
        return carry

    lax.fori_loop(0, pairs, pick, 0)

    spread = jnp.dot(picked[...], select[...], preferred_element_type=jnp.float32)
    for m in range(pairs):
        at = m * 2 * kvec
        row = spread[at:at + kvec] + spread[at + kvec:at + 2 * kvec]
        c, lane0 = divmod(m * LANES, own)
        part[c, :, lane0:lane0 + LANES] = row

    own_ref[...] = part[my_col] + ener[...] * vec[...].astype(jnp.float32)
    for s in range(1, n_col):
        share = part[lax.rem(my_col + s, n_col)]
        send_ref[s - 1] = share.astype(jnp.bfloat16)
        rest_ref[s - 1] = share


def tile_work(rows, cols, count, vec, gath, n_col, ener, tiles):
    n_core = len(gath)
    kvec, own = vec.shape
    n_row = gath[0].shape[0]
    slots, area = tiles.shape
    side = math.isqrt(area)
    per = LANES // side
    blk_own = own // side
    n_seg = n_col * blk_own
    width = area // LANES * SUB
    vmem = pl.BlockSpec(memory_space=pltpu.VMEM)
    far_away = pl.BlockSpec(memory_space=pltpu.HBM)
    return pl.pallas_call(
        functools.partial(tile_kernel, n_core, n_col, side),
        out_shape=(
            jax.ShapeDtypeStruct((kvec, own), jnp.float32),
            jax.ShapeDtypeStruct((n_col - 1, kvec, own), jnp.bfloat16),
            jax.ShapeDtypeStruct((n_col - 1, kvec, own), jnp.float32),
        ),
        in_specs=[pl.BlockSpec(memory_space=pltpu.SMEM)] + [far_away] * 5 + [vmem] * n_core,
        out_specs=(vmem, vmem, vmem),
        scratch_shapes=[
            pltpu.SMEM((slots,), jnp.int32),
            pltpu.SMEM((slots,), jnp.int32),
            pltpu.VMEM((1, own), jnp.float32),
            pltpu.VMEM((kvec, own), jnp.bfloat16),
            pltpu.VMEM((slots, area), jnp.bfloat16),
            pltpu.VMEM((n_row * blk_own + 1, per * kvec, LANES), jnp.float32),
            pltpu.VMEM((n_seg // per * 2 * kvec, per * per * width), jnp.bfloat16),
            pltpu.VMEM((per * per * width, LANES), jnp.bfloat16),
            pltpu.VMEM((n_col, kvec, own), jnp.float32),
            pltpu.SemaphoreType.DMA((slots // CHUNK,)),
            pltpu.SemaphoreType.DMA((4,)),
        ] + [pltpu.VMEM((n_seg, per * kvec, width), jnp.float32)] * SUMS,
        compiler_params=pltpu.CompilerParams(vmem_limit_bytes=48 * 2**20),
        cost_estimate=pl.CostEstimate(
            flops=2 * slots * area * kvec, bytes_accessed=2 * slots * area, transcendentals=0
        ),
        name="tile_work",
    )(count, *[pltpu.with_memory_space_constraint(x, pltpu.HBM) for x in (rows, cols, ener, vec, tiles)],
      *gath)


def terms_kernel(own, rest, vec, *refs):
    others, (terms_ref, wide) = refs[:-2], refs[-2:]
    n_col = len(others) + 1
    kvec = vec.shape[0]

    def outer(share, seg):
        return lax.dot_general(
            share, seg[...].astype(jnp.float32), NT,
            precision=lax.Precision.HIGHEST, preferred_element_type=jnp.float32,
        )

    terms = outer(own[...], vec)
    for s in range(1, n_col):
        terms = terms + outer(rest[s - 1], others[n_col - s - 1])
    wide[...] = jnp.zeros(wide.shape, jnp.float32)
    wide[:, :kvec] = terms
    spaced = pltpu.roll(wide[...], 0, 1, stride=kvec, stride_axis=0)
    terms_ref[...] = jnp.sum(spaced, axis=0, keepdims=True)


def gram_terms(own, rest, vectors, others):
    vmem = pl.BlockSpec(memory_space=pltpu.VMEM)
    return pl.pallas_call(
        terms_kernel,
        out_shape=jax.ShapeDtypeStruct((1, LANES), jnp.float32),
        in_specs=[vmem] * (3 + len(others)),
        out_specs=vmem,
        scratch_shapes=[pltpu.VMEM((vectors.shape[0], LANES), jnp.float32)],
        compiler_params=pltpu.CompilerParams(vmem_limit_bytes=4 * 2**20),
        name="gram_terms",
    )(own, rest, vectors, *others)


def finish_kernel(scale, base, gram_parts, vec, *refs):
    got, (product, residual) = refs[:-2], refs[-2:]
    whole = base[...]
    for piece in got:
        whole = whole + piece[...].astype(jnp.float32)
    product[...] = whole.astype(jnp.bfloat16)
    flat = gram_parts[0]
    for i in range(1, gram_parts.shape[0]):
        flat = flat + gram_parts[i]
    kvec = vec.shape[0]
    lane = lax.broadcasted_iota(jnp.int32, (kvec, LANES), 1)
    first = kvec * lax.broadcasted_iota(jnp.int32, (kvec, LANES), 0)
    wide = jnp.broadcast_to(flat * scale, (kvec, LANES))
    vec32 = vec[...].astype(jnp.float32)
    for a in range(kvec):
        column = jnp.sum(jnp.where(lane == first + a, wide, 0.0), axis=1, keepdims=True)
        whole = whole - column * vec32[a:a + 1, :]
    residual[...] = whole


def finish(scale, base, gram_parts, vectors, got):
    vmem = pl.BlockSpec(memory_space=pltpu.VMEM)
    return pl.pallas_call(
        functools.partial(finish_kernel, scale),
        out_shape=(
            jax.ShapeDtypeStruct(vectors.shape, jnp.bfloat16),
            jax.ShapeDtypeStruct(vectors.shape, jnp.float32),
        ),
        in_specs=[vmem] * (3 + len(got)),
        out_specs=(vmem, vmem),
        compiler_params=pltpu.CompilerParams(vmem_limit_bytes=4 * 2**20),
        name="finish",
    )(base, gram_parts, vectors, *got)


def from_all(x, axis, group):
    got = [x]
    for s in range(1, group):
        perm = [(i, i - i % group + (i + s) % group) for i in range(lax.axis_size(axis))]
        got.append(lax.ppermute(x, axis, perm))
    return got


def per_device(vectors, energies, tiles, tile_rows, tile_cols, tile_count):
    kvec, own = vectors.shape
    n_col = lax.axis_size("col")
    n_row = lax.axis_size("row")
    n_core = 2 if n_row % 2 == 0 else 1
    halves = vectors.reshape(kvec, n_core, own // n_core).swapaxes(0, 1)
    copies = jnp.broadcast_to(halves[None], (n_row // n_core,) + halves.shape)
    gath = lax.all_to_all(copies.reshape((n_row,) + halves.shape[1:]), "row", 0, 0)
    gath = from_all(gath, "row", n_core)
    base, send, rest = tile_work(
        tile_rows, tile_cols, tile_count, vectors, gath, n_col, energies[None, :], tiles
    )
    got = [
        lax.ppermute(send[s - 1], "col", [(c, (c + s) % n_col) for c in range(n_col)])
        for s in range(1, n_col)
    ]
    others = from_all(vectors, "col", n_col)[1:]
    members = n_row * n_col
    terms = gram_terms(base, rest, vectors, others)
    terms = jnp.broadcast_to(terms[None], (members,) + terms.shape)
    gram_parts = lax.all_to_all(terms, ("row", "col"), 0, 0)
    return finish(1.0 / (members * own), base, gram_parts, vectors, got)


def solution(mesh):
    in_specs = (
        P(None, ("row", "col")),
        P(("row", "col")),
        P(("row", "col"), None),
        P(("row", "col")),
        P(("row", "col")),
        P(("row", "col")),
    )
    out_specs = (P(None, ("row", "col")), P(None, ("row", "col")))
    return jax.shard_map(
        per_device, mesh=mesh, in_specs=in_specs, out_specs=out_specs, check_vma=False
    )
```

```python
import functools
import math

import jax
import jax.numpy as jnp
from jax import lax
from jax.experimental import pallas as pl
from jax.experimental.pallas import tpu as pltpu
from jax.sharding import Mesh, PartitionSpec as P

LANES = 128
SUB = 8
CHUNK = 128
STEP = 256
SUMS = 4

NT = (((1,), (1,)), ((), ()))


def outer(share, seg):
    return lax.dot_general(
        share, seg, NT, precision=lax.Precision.HIGHEST, preferred_element_type=jnp.float32
    )


def tile_kernel(
    n_core, n_col, side, count_s, rows_h, cols_h, ener_h, tiles, *refs,
):
    gath, refs = refs[:n_core], refs[n_core:]
    others, refs = refs[:n_col - 1], refs[n_col - 1:]
    (own_ref, send_ref, terms_ref, rows_s, cols_s, ener,
     buf, table, picked, select, part, wide, sems, small, *acc) = refs
    n_far, kvec, own = gath[0].shape
    slots = tiles.shape[0]
    blk_own = own // side
    per = LANES // side
    n_chunk = tiles.shape[1] // LANES
    my_far, my_core, my_col = (lax.axis_index(name) for name in ("far", "core", "col"))

    copies = [
        pltpu.make_async_copy(src, dst, small.at[i])
        for i, (src, dst) in enumerate(
            ((cols_h, cols_s), (rows_h, rows_s), (ener_h, ener))
        )
    ]
    for copy in copies:
        copy.start()

    def tile_copy(ch):
        span = pl.ds(pl.multiple_of(ch * CHUNK, CHUNK), CHUNK)
        return pltpu.make_async_copy(tiles.at[span], buf.at[span], sems.at[ch])

    count = count_s[0]
    used = (count + CHUNK - 1) // CHUNK

    def start(ch, carry):
        tile_copy(ch).start()
        return carry

    lax.fori_loop(0, used, start, 0)

    lane = lax.broadcasted_iota(jnp.int32, (kvec, LANES), 1)
    low = lane < side
    zero = jnp.zeros((kvec, LANES), jnp.float32)

    for s in range(n_core):
        core = lax.rem(my_core + (n_core - s), n_core)
        for f in range(n_far):
            for p in range(own // LANES):
                x = gath[s][f, :, p * LANES:(p + 1) * LANES].astype(jnp.float32)
                y = pltpu.roll(x, side, 1)
                at = (f * n_core + core) * blk_own + p * per
                even = jnp.concatenate([jnp.where(low, x, zero), jnp.where(low, zero, y)], axis=0)
                odd = jnp.concatenate([jnp.where(low, y, zero), jnp.where(low, zero, x)], axis=0)
                table[at] = even
                table[at + 1] = odd
    n_blocks = n_far * n_core * blk_own
    table[n_blocks] = jnp.zeros((per * kvec, LANES), jnp.float32)

    for copy in copies:
        copy.wait()
    n_seg = acc[0].shape[0]
    width = n_chunk * SUB

    def clear(r, carry):
        for a in acc:
            a[r] = jnp.zeros(a.shape[1:], jnp.float32)
        return carry

    lax.fori_loop(0, n_seg, clear, 0, unroll=4)

    k_id = lax.broadcasted_iota(jnp.int32, (width, LANES), 0)
    n_id = lax.broadcasted_iota(jnp.int32, (width, LANES), 1)
    base_id = n_id - per * (k_id // SUB)
    for par in range(per):
        for jp in range(per):
            at = (par * per + jp) * width
            hit = (base_id == side * par + jp).astype(jnp.float32)
            select[at:at + width, :] = hit.astype(jnp.bfloat16)

    rows_of = per * kvec

    def product(base, half, x, check):
        xh = x[half * SUB:(half + 1) * SUB]
        w = jnp.concatenate(
            [xh[:, c * LANES:(c + 1) * LANES] for c in range(n_chunk)], axis=0
        ).astype(jnp.bfloat16)
        entries = []
        for t in range(SUB):
            slot = base + half * SUB + t
            at = cols_s[slot]
            entries.append(table[jnp.where(slot < count, at, n_blocks) if check else at])
        left = jnp.concatenate(entries, axis=0).astype(jnp.bfloat16)
        return lax.dot_general(left, w, NT, preferred_element_type=jnp.float32)

    lane_w = lax.broadcasted_iota(jnp.int32, (rows_of, width), 1) % SUB

    def accumulate(at, out):
        for t in range(SUB):
            r = rows_s[at + t]
            mine = jnp.where(lane_w == t, out[t * rows_of:(t + 1) * rows_of], 0.0)
            acc[t % len(acc)][r] += mine

    def step(first, slots_in, check):
        for i in range(slots_in // CHUNK):
            tile_copy(first // CHUNK + i).wait()
        waiting = None
        for q in range(slots_in // (2 * SUB)):
            base = pl.multiple_of(first + q * 2 * SUB, 2 * SUB)
            x = buf[pl.ds(base, 2 * SUB), :].astype(jnp.float32)
            for half in range(2):
                out = product(base, half, x, check)
                if waiting is not None:
                    accumulate(*waiting)
                waiting = (base + half * SUB, out)
        accumulate(*waiting)

    def full_step(i, carry):
        step(i * STEP, STEP, False)
        return carry

    def last_step(ch, carry):
        step(ch * CHUNK, CHUNK, True)
        return carry

    full = count // STEP
    lax.fori_loop(0, full, full_step, 0)
    lax.fori_loop(full * (STEP // CHUNK), used, last_step, 0)

    pairs = n_seg // per

    def pick(m, carry):
        pieces = []
        for par in range(per):
            total = acc[0][m * per + par]
            for other in acc[1:]:
                total = total + other[m * per + par]
            for jp in range(per):
                pieces.append(total[jp * kvec:(jp + 1) * kvec])
        a = jnp.concatenate(pieces, axis=1)
        hi = a.astype(jnp.bfloat16).astype(jnp.float32)
        both = jnp.concatenate([hi, a - hi], axis=0).astype(jnp.bfloat16)
        picked[pl.ds(pl.multiple_of(m * 2 * kvec, 2 * kvec), 2 * kvec), :] = both
        return carry

    lax.fori_loop(0, pairs, pick, 0, unroll=4)

    spread = jnp.dot(picked[...], select[...], preferred_element_type=jnp.float32)
    for m in range(pairs):
        at = m * 2 * kvec
        row = spread[at:at + kvec] + spread[at + kvec:at + 2 * kvec]
        c, lane0 = divmod(m * LANES, own)
        part[c, :, lane0:lane0 + LANES] = row

    vec = gath[0][my_far].astype(jnp.float32)
    mine = part[my_col] + ener[...] * vec
    own_ref[...] = mine
    terms = outer(mine, vec)
    for s in range(1, n_col):
        share = part[lax.rem(my_col + s, n_col)]
        send_ref[s - 1] = share.astype(jnp.bfloat16)
        terms = terms + outer(share, others[n_col - s - 1][...].astype(jnp.float32))
    wide[...] = jnp.zeros(wide.shape, jnp.float32)
    wide[:, :kvec] = terms
    spaced = pltpu.roll(wide[...], 0, 1, stride=kvec, stride_axis=0)
    flat = jnp.sum(spaced, axis=0, keepdims=True)
    for i in range(terms_ref.shape[0]):
        terms_ref[i] = flat


def tile_work(rows, cols, count, gath, others, members, ener, tiles):
    n_core, n_col = len(gath), len(others) + 1
    n_far, kvec, own = gath[0].shape
    slots, area = tiles.shape
    side = math.isqrt(area)
    per = LANES // side
    blk_own = own // side
    n_seg = n_col * blk_own
    width = area // LANES * SUB
    vmem = pl.BlockSpec(memory_space=pltpu.VMEM)
    far_away = pl.BlockSpec(memory_space=pltpu.HBM)
    return pl.pallas_call(
        functools.partial(tile_kernel, n_core, n_col, side),
        out_shape=(
            jax.ShapeDtypeStruct((kvec, own), jnp.float32),
            jax.ShapeDtypeStruct((n_col - 1, kvec, own), jnp.bfloat16),
            jax.ShapeDtypeStruct((members, 1, LANES), jnp.float32),
        ),
        in_specs=[pl.BlockSpec(memory_space=pltpu.SMEM)] + [far_away] * 4 + [vmem] * (n_core + n_col - 1),
        out_specs=(vmem, vmem, vmem),
        scratch_shapes=[
            pltpu.SMEM((slots,), jnp.int32),
            pltpu.SMEM((slots,), jnp.int32),
            pltpu.VMEM((1, own), jnp.float32),
            pltpu.VMEM((slots, area), jnp.bfloat16),
            pltpu.VMEM((n_far * n_core * blk_own + 1, per * kvec, LANES), jnp.float32),
            pltpu.VMEM((n_seg // per * 2 * kvec, per * per * width), jnp.bfloat16),
            pltpu.VMEM((per * per * width, LANES), jnp.bfloat16),
            pltpu.VMEM((n_col, kvec, own), jnp.float32),
            pltpu.VMEM((kvec, LANES), jnp.float32),
            pltpu.SemaphoreType.DMA((slots // CHUNK,)),
            pltpu.SemaphoreType.DMA((3,)),
        ] + [pltpu.VMEM((n_seg, per * kvec, width), jnp.float32)] * SUMS,
        compiler_params=pltpu.CompilerParams(vmem_limit_bytes=48 * 2**20),
        cost_estimate=pl.CostEstimate(
            flops=2 * slots * area * kvec, bytes_accessed=2 * slots * area, transcendentals=0
        ),
        name="tile_work",
    )(count, *[pltpu.with_memory_space_constraint(x, pltpu.HBM) for x in (rows, cols, ener, tiles)],
      *gath, *others)


def finish_kernel(scale, base, gram_parts, vec, *refs):
    got, (product, residual) = refs[:-2], refs[-2:]
    whole = base[...]
    for piece in got:
        whole = whole + piece[...].astype(jnp.float32)
    product[...] = whole.astype(jnp.bfloat16)
    flat = gram_parts[0]
    for i in range(1, gram_parts.shape[0]):
        flat = flat + gram_parts[i]
    kvec = vec.shape[0]
    lane = lax.broadcasted_iota(jnp.int32, (kvec, LANES), 1)
    first = kvec * lax.broadcasted_iota(jnp.int32, (kvec, LANES), 0)
    wide = jnp.broadcast_to(flat * scale, (kvec, LANES))
    vec32 = vec[...].astype(jnp.float32)
    for a in range(kvec):
        column = jnp.sum(jnp.where(lane == first + a, wide, 0.0), axis=1, keepdims=True)
        whole = whole - column * vec32[a:a + 1, :]
    residual[...] = whole


def finish(scale, base, gram_parts, vectors, got):
    vmem = pl.BlockSpec(memory_space=pltpu.VMEM)
    return pl.pallas_call(
        functools.partial(finish_kernel, scale),
        out_shape=(
            jax.ShapeDtypeStruct(vectors.shape, jnp.bfloat16),
            jax.ShapeDtypeStruct(vectors.shape, jnp.float32),
        ),
        in_specs=[vmem] * (3 + len(got)),
        out_specs=(vmem, vmem),
        compiler_params=pltpu.CompilerParams(vmem_limit_bytes=4 * 2**20),
        name="finish",
    )(base, gram_parts, vectors, *got)


def from_all(x, axis):
    size = lax.axis_size(axis)
    got = [x]
    for s in range(1, size):
        got.append(lax.ppermute(x, axis, [(i, (i + s) % size) for i in range(size)]))
    return got


def per_device(vectors, energies, tiles, tile_rows, tile_cols, tile_count):
    kvec, own = vectors.shape
    n_col = lax.axis_size("col")
    copies = jnp.broadcast_to(vectors[None], (lax.axis_size("far"), kvec, own))
    gath = lax.all_to_all(copies, "far", 0, 0)
    others = from_all(vectors, "col")[1:]
    gath, others = lax.optimization_barrier((gath, others))
    gath = from_all(gath, "core")
    members = lax.axis_size(("far", "core", "col"))
    base, send, terms = tile_work(
        tile_rows, tile_cols, tile_count, gath, others, members, energies[None, :], tiles
    )
    got = [
        lax.ppermute(send[s - 1], "col", [(c, (c + s) % n_col) for c in range(n_col)])
        for s in range(1, n_col)
    ]
    gram_parts = lax.all_to_all(terms, ("far", "core", "col"), 0, 0)
    return finish(1.0 / (members * own), base, gram_parts, vectors, got)


def solution(mesh):
    n_row, n_col = mesh.devices.shape
    n_core = 2 if n_row % 2 == 0 else 1
    split = ("far", "core", "col")
    chips = Mesh(mesh.devices.reshape(n_row // n_core, n_core, n_col), split)
    in_specs = (P(None, split), P(split), P(split, None), P(split), P(split), P(split))
    out_specs = (P(None, split), P(None, split))
    return jax.shard_map(
        per_device, mesh=chips, in_specs=in_specs, out_specs=out_specs, check_vma=False
    )
```

```python
import functools
import math

import jax
import jax.numpy as jnp
from jax import lax
from jax.experimental import pallas as pl
from jax.experimental.pallas import tpu as pltpu
from jax.sharding import Mesh, PartitionSpec as P

LANES = 128
SUB = 8
CHUNK = 128
STEP = 256
SUMS = 4

NT = (((1,), (1,)), ((), ()))


def tile_kernel(
    n_core, n_col, side, count_s, rows_h, cols_h, ener_h, tiles, *refs,
):
    gath, refs = refs[:n_core], refs[n_core:]
    (own_ref, send_ref, rest_ref, rows_s, cols_s, ener,
     buf, table, picked, select, part, sems, small, *acc) = refs
    n_far, kvec, own = gath[0].shape
    slots = tiles.shape[0]
    blk_own = own // side
    per = LANES // side
    n_chunk = tiles.shape[1] // LANES
    my_far, my_core, my_col = (lax.axis_index(name) for name in ("far", "core", "col"))

    copies = [
        pltpu.make_async_copy(src, dst, small.at[i])
        for i, (src, dst) in enumerate(
            ((cols_h, cols_s), (rows_h, rows_s), (ener_h, ener))
        )
    ]
    for copy in copies:
        copy.start()

    def tile_copy(ch):
        span = pl.ds(pl.multiple_of(ch * CHUNK, CHUNK), CHUNK)
        return pltpu.make_async_copy(tiles.at[span], buf.at[span], sems.at[ch])

    count = count_s[0]
    used = (count + CHUNK - 1) // CHUNK

    def start(ch, carry):
        tile_copy(ch).start()
        return carry

    lax.fori_loop(0, used, start, 0)

    lane = lax.broadcasted_iota(jnp.int32, (kvec, LANES), 1)
    low = lane < side
    zero = jnp.zeros((kvec, LANES), jnp.float32)

    for s in range(n_core):
        core = lax.rem(my_core + (n_core - s), n_core)
        for f in range(n_far):
            for p in range(own // LANES):
                x = gath[s][f, :, p * LANES:(p + 1) * LANES].astype(jnp.float32)
                y = pltpu.roll(x, side, 1)
                at = (f * n_core + core) * blk_own + p * per
                even = jnp.concatenate([jnp.where(low, x, zero), jnp.where(low, zero, y)], axis=0)
                odd = jnp.concatenate([jnp.where(low, y, zero), jnp.where(low, zero, x)], axis=0)
                table[at] = even
                table[at + 1] = odd
    n_blocks = n_far * n_core * blk_own
    table[n_blocks] = jnp.zeros((per * kvec, LANES), jnp.float32)

    for copy in copies:
        copy.wait()
    n_seg = acc[0].shape[0]
    width = n_chunk * SUB

    def clear(r, carry):
        for a in acc:
            a[r] = jnp.zeros(a.shape[1:], jnp.float32)
        return carry

    lax.fori_loop(0, n_seg, clear, 0)

    k_id = lax.broadcasted_iota(jnp.int32, (width, LANES), 0)
    n_id = lax.broadcasted_iota(jnp.int32, (width, LANES), 1)
    base_id = n_id - per * (k_id // SUB)
    for par in range(per):
        for jp in range(per):
            at = (par * per + jp) * width
            hit = (base_id == side * par + jp).astype(jnp.float32)
            select[at:at + width, :] = hit.astype(jnp.bfloat16)

    rows_of = per * kvec

    def product(base, half, x, check):
        xh = x[half * SUB:(half + 1) * SUB]
        w = jnp.concatenate(
            [xh[:, c * LANES:(c + 1) * LANES] for c in range(n_chunk)], axis=0
        ).astype(jnp.bfloat16)
        entries = []
        for t in range(SUB):
            slot = base + half * SUB + t
            at = cols_s[slot]
            entries.append(table[jnp.where(slot < count, at, n_blocks) if check else at])
        left = jnp.concatenate(entries, axis=0).astype(jnp.bfloat16)
        return lax.dot_general(left, w, NT, preferred_element_type=jnp.float32)

    lane_w = lax.broadcasted_iota(jnp.int32, (rows_of, width), 1) % SUB

    def accumulate(at, out):
        for t in range(SUB):
            r = rows_s[at + t]
            mine = jnp.where(lane_w == t, out[t * rows_of:(t + 1) * rows_of], 0.0)
            acc[t % len(acc)][r] += mine

    def step(first, slots_in, check):
        for i in range(slots_in // CHUNK):
            tile_copy(first // CHUNK + i).wait()
        waiting = None
        for q in range(slots_in // (2 * SUB)):
            base = pl.multiple_of(first + q * 2 * SUB, 2 * SUB)
            x = buf[pl.ds(base, 2 * SUB), :].astype(jnp.float32)
            for half in range(2):
                out = product(base, half, x, check)
                if waiting is not None:
                    accumulate(*waiting)
                waiting = (base + half * SUB, out)
        accumulate(*waiting)

    def full_step(i, carry):
        step(i * STEP, STEP, False)
        return carry

    def last_step(ch, carry):
        step(ch * CHUNK, CHUNK, True)
        return carry

    full = count // STEP
    lax.fori_loop(0, full, full_step, 0)
    lax.fori_loop(full * (STEP // CHUNK), used, last_step, 0)

    pairs = n_seg // per

    def pick(m, carry):
        pieces = []
        for par in range(per):
            total = acc[0][m * per + par]
            for other in acc[1:]:
                total = total + other[m * per + par]
            for jp in range(per):
                pieces.append(total[jp * kvec:(jp + 1) * kvec])
        a = jnp.concatenate(pieces, axis=1)
        hi = a.astype(jnp.bfloat16).astype(jnp.float32)
        both = jnp.concatenate([hi, a - hi], axis=0).astype(jnp.bfloat16)
        picked[pl.ds(pl.multiple_of(m * 2 * kvec, 2 * kvec), 2 * kvec), :] = both
        return carry

    lax.fori_loop(0, pairs, pick, 0)

    spread = jnp.dot(picked[...], select[...], preferred_element_type=jnp.float32)
    for m in range(pairs):
        at = m * 2 * kvec
        row = spread[at:at + kvec] + spread[at + kvec:at + 2 * kvec]
        c, lane0 = divmod(m * LANES, own)
        part[c, :, lane0:lane0 + LANES] = row

    own_ref[...] = part[my_col] + ener[...] * gath[0][my_far].astype(jnp.float32)
    for s in range(1, n_col):
        share = part[lax.rem(my_col + s, n_col)]
        send_ref[s - 1] = share.astype(jnp.bfloat16)
        rest_ref[s - 1] = share


def tile_work(rows, cols, count, gath, n_col, ener, tiles):
    n_core = len(gath)
    n_far, kvec, own = gath[0].shape
    slots, area = tiles.shape
    side = math.isqrt(area)
    per = LANES // side
    blk_own = own // side
    n_seg = n_col * blk_own
    width = area // LANES * SUB
    vmem = pl.BlockSpec(memory_space=pltpu.VMEM)
    far_away = pl.BlockSpec(memory_space=pltpu.HBM)
    return pl.pallas_call(
        functools.partial(tile_kernel, n_core, n_col, side),
        out_shape=(
            jax.ShapeDtypeStruct((kvec, own), jnp.float32),
            jax.ShapeDtypeStruct((n_col - 1, kvec, own), jnp.bfloat16),
            jax.ShapeDtypeStruct((n_col - 1, kvec, own), jnp.float32),
        ),
        in_specs=[pl.BlockSpec(memory_space=pltpu.SMEM)] + [far_away] * 4 + [vmem] * n_core,
        out_specs=(vmem, vmem, vmem),
        scratch_shapes=[
            pltpu.SMEM((slots,), jnp.int32),
            pltpu.SMEM((slots,), jnp.int32),
            pltpu.VMEM((1, own), jnp.float32),
            pltpu.VMEM((slots, area), jnp.bfloat16),
            pltpu.VMEM((n_far * n_core * blk_own + 1, per * kvec, LANES), jnp.float32),
            pltpu.VMEM((n_seg // per * 2 * kvec, per * per * width), jnp.bfloat16),
            pltpu.VMEM((per * per * width, LANES), jnp.bfloat16),
            pltpu.VMEM((n_col, kvec, own), jnp.float32),
            pltpu.SemaphoreType.DMA((slots // CHUNK,)),
            pltpu.SemaphoreType.DMA((3,)),
        ] + [pltpu.VMEM((n_seg, per * kvec, width), jnp.float32)] * SUMS,
        compiler_params=pltpu.CompilerParams(vmem_limit_bytes=48 * 2**20),
        cost_estimate=pl.CostEstimate(
            flops=2 * slots * area * kvec, bytes_accessed=2 * slots * area, transcendentals=0
        ),
        name="tile_work",
    )(count, *[pltpu.with_memory_space_constraint(x, pltpu.HBM) for x in (rows, cols, ener, tiles)],
      *gath)


def terms_kernel(own, rest, vec, *refs):
    others, (terms_ref, wide) = refs[:-2], refs[-2:]
    n_col = len(others) + 1
    kvec = vec.shape[0]

    def outer(share, seg):
        return lax.dot_general(
            share, seg[...].astype(jnp.float32), NT,
            precision=lax.Precision.HIGHEST, preferred_element_type=jnp.float32,
        )

    terms = outer(own[...], vec)
    for s in range(1, n_col):
        terms = terms + outer(rest[s - 1], others[n_col - s - 1])
    wide[...] = jnp.zeros(wide.shape, jnp.float32)
    wide[:, :kvec] = terms
    spaced = pltpu.roll(wide[...], 0, 1, stride=kvec, stride_axis=0)
    terms_ref[...] = jnp.sum(spaced, axis=0, keepdims=True)


def gram_terms(own, rest, vectors, others):
    vmem = pl.BlockSpec(memory_space=pltpu.VMEM)
    return pl.pallas_call(
        terms_kernel,
        out_shape=jax.ShapeDtypeStruct((1, LANES), jnp.float32),
        in_specs=[vmem] * (3 + len(others)),
        out_specs=vmem,
        scratch_shapes=[pltpu.VMEM((vectors.shape[0], LANES), jnp.float32)],
        compiler_params=pltpu.CompilerParams(vmem_limit_bytes=4 * 2**20),
        name="gram_terms",
    )(own, rest, vectors, *others)


def finish_kernel(scale, base, gram_parts, vec, *refs):
    got, (product, residual) = refs[:-2], refs[-2:]
    whole = base[...]
    for piece in got:
        whole = whole + piece[...].astype(jnp.float32)
    product[...] = whole.astype(jnp.bfloat16)
    flat = gram_parts[0]
    for i in range(1, gram_parts.shape[0]):
        flat = flat + gram_parts[i]
    kvec = vec.shape[0]
    lane = lax.broadcasted_iota(jnp.int32, (kvec, LANES), 1)
    first = kvec * lax.broadcasted_iota(jnp.int32, (kvec, LANES), 0)
    wide = jnp.broadcast_to(flat * scale, (kvec, LANES))
    vec32 = vec[...].astype(jnp.float32)
    for a in range(kvec):
        column = jnp.sum(jnp.where(lane == first + a, wide, 0.0), axis=1, keepdims=True)
        whole = whole - column * vec32[a:a + 1, :]
    residual[...] = whole


def finish(scale, base, gram_parts, vectors, got):
    vmem = pl.BlockSpec(memory_space=pltpu.VMEM)
    return pl.pallas_call(
        functools.partial(finish_kernel, scale),
        out_shape=(
            jax.ShapeDtypeStruct(vectors.shape, jnp.bfloat16),
            jax.ShapeDtypeStruct(vectors.shape, jnp.float32),
        ),
        in_specs=[vmem] * (3 + len(got)),
        out_specs=(vmem, vmem),
        compiler_params=pltpu.CompilerParams(vmem_limit_bytes=4 * 2**20),
        name="finish",
    )(base, gram_parts, vectors, *got)


def from_all(x, axis):
    size = lax.axis_size(axis)
    got = [x]
    for s in range(1, size):
        got.append(lax.ppermute(x, axis, [(i, (i + s) % size) for i in range(size)]))
    return got


def per_device(vectors, energies, tiles, tile_rows, tile_cols, tile_count):
    kvec, own = vectors.shape
    n_col = lax.axis_size("col")
    copies = jnp.broadcast_to(vectors[None], (lax.axis_size("far"), kvec, own))
    gath = lax.all_to_all(copies, "far", 0, 0)
    gath = from_all(gath, "core")
    base, send, rest = tile_work(
        tile_rows, tile_cols, tile_count, gath, n_col, energies[None, :], tiles
    )
    others = from_all(vectors, "col")[1:]
    terms = sum(from_all(gram_terms(base, rest, vectors, others), "core"))
    send, terms = lax.optimization_barrier((send, terms))
    members = lax.axis_size(("far", "col"))
    terms = jnp.broadcast_to(terms[None], (members,) + terms.shape)
    gram_parts = lax.all_to_all(terms, ("far", "col"), 0, 0)
    got = [
        lax.ppermute(send[s - 1], "col", [(c, (c + s) % n_col) for c in range(n_col)])
        for s in range(1, n_col)
    ]
    states = lax.axis_size(("far", "core", "col")) * own
    return finish(1.0 / states, base, gram_parts, vectors, got)


def solution(mesh):
    n_row, n_col = mesh.devices.shape
    n_core = 2 if n_row % 2 == 0 else 1
    split = ("far", "core", "col")
    chips = Mesh(mesh.devices.reshape(n_row // n_core, n_core, n_col), split)
    in_specs = (P(None, split), P(split), P(split, None), P(split), P(split), P(split))
    out_specs = (P(None, split), P(None, split))
    return jax.shard_map(
        per_device, mesh=chips, in_specs=in_specs, out_specs=out_specs, check_vma=False
    )
```

```python
import functools
import math

import jax
import jax.numpy as jnp
from jax import lax
from jax.experimental import pallas as pl
from jax.experimental.pallas import tpu as pltpu
from jax.sharding import Mesh, PartitionSpec as P

LANES = 128
SUB = 8
CHUNK = 128
STEP = 256
SUMS = 4

NT = (((1,), (1,)), ((), ()))


def tile_kernel(
    n_core, n_col, side, count_s, rows_h, cols_h, ener_h, tiles, *refs,
):
    gath, refs = refs[:n_core], refs[n_core:]
    (own_ref, send_ref, rest_ref, rows_s, cols_s, ener,
     buf, table, picked, select, part, sems, small, *acc) = refs
    n_far, kvec, own = gath[0].shape
    slots = tiles.shape[0]
    blk_own = own // side
    per = LANES // side
    n_chunk = tiles.shape[1] // LANES
    my_far, my_core, my_col = (lax.axis_index(name) for name in ("far", "core", "col"))

    copies = [
        pltpu.make_async_copy(src, dst, small.at[i])
        for i, (src, dst) in enumerate(
            ((cols_h, cols_s), (rows_h, rows_s), (ener_h, ener))
        )
    ]
    for copy in copies:
        copy.start()

    def tile_copy(ch):
        span = pl.ds(pl.multiple_of(ch * CHUNK, CHUNK), CHUNK)
        return pltpu.make_async_copy(tiles.at[span], buf.at[span], sems.at[ch])

    count = count_s[0]
    used = (count + CHUNK - 1) // CHUNK

    def start(ch, carry):
        tile_copy(ch).start()
        return carry

    lax.fori_loop(0, used, start, 0)

    lane = lax.broadcasted_iota(jnp.int32, (kvec, LANES), 1)
    low = lane < side
    zero = jnp.zeros((kvec, LANES), jnp.float32)

    for s in range(n_core):
        core = lax.rem(my_core + (n_core - s), n_core)
        for f in range(n_far):
            for p in range(own // LANES):
                x = gath[s][f, :, p * LANES:(p + 1) * LANES].astype(jnp.float32)
                y = pltpu.roll(x, side, 1)
                at = (f * n_core + core) * blk_own + p * per
                even = jnp.concatenate([jnp.where(low, x, zero), jnp.where(low, zero, y)], axis=0)
                odd = jnp.concatenate([jnp.where(low, y, zero), jnp.where(low, zero, x)], axis=0)
                table[at] = even
                table[at + 1] = odd
    n_blocks = n_far * n_core * blk_own
    table[n_blocks] = jnp.zeros((per * kvec, LANES), jnp.float32)

    for copy in copies:
        copy.wait()
    n_seg = acc[0].shape[0]
    width = n_chunk * SUB

    def clear(r, carry):
        for a in acc:
            a[r] = jnp.zeros(a.shape[1:], jnp.float32)
        return carry

    lax.fori_loop(0, n_seg, clear, 0)

    k_id = lax.broadcasted_iota(jnp.int32, (width, LANES), 0)
    n_id = lax.broadcasted_iota(jnp.int32, (width, LANES), 1)
    base_id = n_id - per * (k_id // SUB)
    for par in range(per):
        for jp in range(per):
            at = (par * per + jp) * width
            hit = (base_id == side * par + jp).astype(jnp.float32)
            select[at:at + width, :] = hit.astype(jnp.bfloat16)

    rows_of = per * kvec

    def product(base, half, x, check):
        xh = x[half * SUB:(half + 1) * SUB]
        w = jnp.concatenate(
            [xh[:, c * LANES:(c + 1) * LANES] for c in range(n_chunk)], axis=0
        ).astype(jnp.bfloat16)
        entries = []
        for t in range(SUB):
            slot = base + half * SUB + t
            at = cols_s[slot]
            entries.append(table[jnp.where(slot < count, at, n_blocks) if check else at])
        left = jnp.concatenate(entries, axis=0).astype(jnp.bfloat16)
        return lax.dot_general(left, w, NT, preferred_element_type=jnp.float32)

    lane_w = lax.broadcasted_iota(jnp.int32, (rows_of, width), 1) % SUB

    def accumulate(at, out):
        for t in range(SUB):
            r = rows_s[at + t]
            mine = jnp.where(lane_w == t, out[t * rows_of:(t + 1) * rows_of], 0.0)
            acc[t % len(acc)][r] += mine

    def step(first, slots_in, check):
        for i in range(slots_in // CHUNK):
            tile_copy(first // CHUNK + i).wait()
        waiting = None
        for q in range(slots_in // (2 * SUB)):
            base = pl.multiple_of(first + q * 2 * SUB, 2 * SUB)
            x = buf[pl.ds(base, 2 * SUB), :].astype(jnp.float32)
            for half in range(2):
                out = product(base, half, x, check)
                if waiting is not None:
                    accumulate(*waiting)
                waiting = (base + half * SUB, out)
        accumulate(*waiting)

    def full_step(i, carry):
        step(i * STEP, STEP, False)
        return carry

    def last_step(ch, carry):
        step(ch * CHUNK, CHUNK, True)
        return carry

    full = count // STEP
    lax.fori_loop(0, full, full_step, 0)
    lax.fori_loop(full * (STEP // CHUNK), used, last_step, 0)

    pairs = n_seg // per

    def pick(m, carry):
        pieces = []
        for par in range(per):
            total = acc[0][m * per + par]
            for other in acc[1:]:
                total = total + other[m * per + par]
            for jp in range(per):
                pieces.append(total[jp * kvec:(jp + 1) * kvec])
        a = jnp.concatenate(pieces, axis=1)
        hi = a.astype(jnp.bfloat16).astype(jnp.float32)
        both = jnp.concatenate([hi, a - hi], axis=0).astype(jnp.bfloat16)
        picked[pl.ds(pl.multiple_of(m * 2 * kvec, 2 * kvec), 2 * kvec), :] = both
        return carry

    lax.fori_loop(0, pairs, pick, 0)

    spread = jnp.dot(picked[...], select[...], preferred_element_type=jnp.float32)
    for m in range(pairs):
        at = m * 2 * kvec
        row = spread[at:at + kvec] + spread[at + kvec:at + 2 * kvec]
        c, lane0 = divmod(m * LANES, own)
        part[c, :, lane0:lane0 + LANES] = row

    own_ref[...] = part[my_col] + ener[...] * gath[0][my_far].astype(jnp.float32)
    for s in range(1, n_col):
        share = part[lax.rem(my_col + s, n_col)]
        send_ref[s - 1] = share.astype(jnp.bfloat16)
        rest_ref[s - 1] = share


def tile_work(rows, cols, count, gath, n_col, ener, tiles):
    n_core = len(gath)
    n_far, kvec, own = gath[0].shape
    slots, area = tiles.shape
    side = math.isqrt(area)
    per = LANES // side
    blk_own = own // side
    n_seg = n_col * blk_own
    width = area // LANES * SUB
    vmem = pl.BlockSpec(memory_space=pltpu.VMEM)
    far_away = pl.BlockSpec(memory_space=pltpu.HBM)
    return pl.pallas_call(
        functools.partial(tile_kernel, n_core, n_col, side),
        out_shape=(
            jax.ShapeDtypeStruct((kvec, own), jnp.float32),
            jax.ShapeDtypeStruct((n_col - 1, kvec, own), jnp.bfloat16),
            jax.ShapeDtypeStruct((n_col - 1, kvec, own), jnp.float32),
        ),
        in_specs=[pl.BlockSpec(memory_space=pltpu.SMEM)] + [far_away] * 4 + [vmem] * n_core,
        out_specs=(vmem, vmem, vmem),
        scratch_shapes=[
            pltpu.SMEM((slots,), jnp.int32),
            pltpu.SMEM((slots,), jnp.int32),
            pltpu.VMEM((1, own), jnp.float32),
            pltpu.VMEM((slots, area), jnp.bfloat16),
            pltpu.VMEM((n_far * n_core * blk_own + 1, per * kvec, LANES), jnp.float32),
            pltpu.VMEM((n_seg // per * 2 * kvec, per * per * width), jnp.bfloat16),
            pltpu.VMEM((per * per * width, LANES), jnp.bfloat16),
            pltpu.VMEM((n_col, kvec, own), jnp.float32),
            pltpu.SemaphoreType.DMA((slots // CHUNK,)),
            pltpu.SemaphoreType.DMA((3,)),
        ] + [pltpu.VMEM((n_seg, per * kvec, width), jnp.float32)] * SUMS,
        compiler_params=pltpu.CompilerParams(vmem_limit_bytes=48 * 2**20),
        cost_estimate=pl.CostEstimate(
            flops=2 * slots * area * kvec, bytes_accessed=2 * slots * area, transcendentals=0
        ),
        name="tile_work",
    )(count, *[pltpu.with_memory_space_constraint(x, pltpu.HBM) for x in (rows, cols, ener, tiles)],
      *gath)


def terms_kernel(own, rest, vec, *refs):
    others, (terms_ref, wide) = refs[:-2], refs[-2:]
    n_col = len(others) + 1
    kvec = vec.shape[0]

    def outer(share, seg):
        return lax.dot_general(
            share, seg[...].astype(jnp.float32), NT,
            precision=lax.Precision.HIGHEST, preferred_element_type=jnp.float32,
        )

    terms = outer(own[...], vec)
    for s in range(1, n_col):
        terms = terms + outer(rest[s - 1], others[n_col - s - 1])
    wide[...] = jnp.zeros(wide.shape, jnp.float32)
    wide[:, :kvec] = terms
    spaced = pltpu.roll(wide[...], 0, 1, stride=kvec, stride_axis=0)
    terms_ref[...] = jnp.sum(spaced, axis=0, keepdims=True)


def gram_terms(own, rest, vectors, others):
    vmem = pl.BlockSpec(memory_space=pltpu.VMEM)
    return pl.pallas_call(
        terms_kernel,
        out_shape=jax.ShapeDtypeStruct((1, LANES), jnp.float32),
        in_specs=[vmem] * (3 + len(others)),
        out_specs=vmem,
        scratch_shapes=[pltpu.VMEM((vectors.shape[0], LANES), jnp.float32)],
        compiler_params=pltpu.CompilerParams(vmem_limit_bytes=4 * 2**20),
        name="gram_terms",
    )(own, rest, vectors, *others)


def finish_kernel(scale, base, gram_parts, vec, *refs):
    got, (product, residual) = refs[:-2], refs[-2:]
    whole = base[...]
    for piece in got:
        whole = whole + piece[...].astype(jnp.float32)
    product[...] = whole.astype(jnp.bfloat16)
    flat = gram_parts[0, :1]
    for i in range(1, gram_parts.shape[0]):
        flat = flat + gram_parts[i, :1]
    kvec = vec.shape[0]
    lane = lax.broadcasted_iota(jnp.int32, (kvec, LANES), 1)
    first = kvec * lax.broadcasted_iota(jnp.int32, (kvec, LANES), 0)
    wide = jnp.broadcast_to(flat * scale, (kvec, LANES))
    vec32 = vec[...].astype(jnp.float32)
    for a in range(kvec):
        column = jnp.sum(jnp.where(lane == first + a, wide, 0.0), axis=1, keepdims=True)
        whole = whole - column * vec32[a:a + 1, :]
    residual[...] = whole


def finish(scale, base, gram_parts, vectors, got):
    vmem = pl.BlockSpec(memory_space=pltpu.VMEM)
    return pl.pallas_call(
        functools.partial(finish_kernel, scale),
        out_shape=(
            jax.ShapeDtypeStruct(vectors.shape, jnp.bfloat16),
            jax.ShapeDtypeStruct(vectors.shape, jnp.float32),
        ),
        in_specs=[vmem] * (3 + len(got)),
        out_specs=(vmem, vmem),
        compiler_params=pltpu.CompilerParams(vmem_limit_bytes=4 * 2**20),
        name="finish",
    )(base, gram_parts, vectors, *got)


def from_all(x, axis):
    size = lax.axis_size(axis)
    got = [x]
    for s in range(1, size):
        got.append(lax.ppermute(x, axis, [(i, (i + s) % size) for i in range(size)]))
    return got


def per_device(vectors, energies, tiles, tile_rows, tile_cols, tile_count):
    kvec, own = vectors.shape
    n_col = lax.axis_size("col")
    copies = jnp.broadcast_to(vectors[None], (lax.axis_size("far"), kvec, own))
    gath = lax.all_to_all(copies, "far", 0, 0)
    gath = from_all(gath, "core")
    base, send, rest = tile_work(
        tile_rows, tile_cols, tile_count, gath, n_col, energies[None, :], tiles
    )
    others = from_all(vectors, "col")[1:]
    terms = sum(from_all(gram_terms(base, rest, vectors, others), "core"))
    send, terms = lax.optimization_barrier((send, terms))
    members = lax.axis_size(("far", "col"))
    terms = jnp.broadcast_to(terms[None], (members, 4, LANES))
    gram_parts = lax.all_to_all(terms, ("far", "col"), 0, 0)
    got = [
        lax.ppermute(send[s - 1], "col", [(c, (c + s) % n_col) for c in range(n_col)])
        for s in range(1, n_col)
    ]
    states = lax.axis_size(("far", "core", "col")) * own
    return finish(1.0 / states, base, gram_parts, vectors, got)


def solution(mesh):
    n_row, n_col = mesh.devices.shape
    n_core = 2 if n_row % 2 == 0 else 1
    split = ("far", "core", "col")
    chips = Mesh(mesh.devices.reshape(n_row // n_core, n_core, n_col), split)
    in_specs = (P(None, split), P(split), P(split, None), P(split), P(split), P(split))
    out_specs = (P(None, split), P(None, split))
    return jax.shard_map(
        per_device, mesh=chips, in_specs=in_specs, out_specs=out_specs, check_vma=False
    )
```

```python
import functools
import math

import jax
import jax.numpy as jnp
from jax import lax
from jax.experimental import pallas as pl
from jax.experimental.pallas import tpu as pltpu
from jax.sharding import Mesh, PartitionSpec as P

LANES = 128
SUB = 8
CHUNK = 128
STEP = 256
SUMS = 4

NT = (((1,), (1,)), ((), ()))


def tile_kernel(
    n_core, n_col, side, count_s, rows_h, cols_h, ener_h, tiles, *refs,
):
    gath, refs = refs[:n_core], refs[n_core:]
    (own_ref, send_ref, rest_ref, rows_s, cols_s, ener,
     buf, table, picked, select, part, sems, small, *acc) = refs
    n_far, kvec, own = gath[0].shape
    slots = tiles.shape[0]
    blk_own = own // side
    per = LANES // side
    n_chunk = tiles.shape[1] // LANES
    my_far, my_core, my_col = (lax.axis_index(name) for name in ("far", "core", "col"))

    copies = [
        pltpu.make_async_copy(src, dst, small.at[i])
        for i, (src, dst) in enumerate(
            ((cols_h, cols_s), (rows_h, rows_s), (ener_h, ener))
        )
    ]
    for copy in copies:
        copy.start()

    def tile_copy(ch):
        span = pl.ds(pl.multiple_of(ch * CHUNK, CHUNK), CHUNK)
        return pltpu.make_async_copy(tiles.at[span], buf.at[span], sems.at[ch])

    count = count_s[0]
    used = (count + CHUNK - 1) // CHUNK

    def start(ch, carry):
        tile_copy(ch).start()
        return carry

    lax.fori_loop(0, used, start, 0)

    lane = lax.broadcasted_iota(jnp.int32, (kvec, LANES), 1)
    low = lane < side
    zero = jnp.zeros((kvec, LANES), jnp.float32)

    for s in range(n_core):
        core = lax.rem(my_core + (n_core - s), n_core)
        for f in range(n_far):
            for p in range(own // LANES):
                x = gath[s][f, :, p * LANES:(p + 1) * LANES].astype(jnp.float32)
                y = pltpu.roll(x, side, 1)
                at = (f * n_core + core) * blk_own + p * per
                table[at] = jnp.where(low, x, y)
                table[at + 1] = jnp.where(low, y, x)
    n_blocks = n_far * n_core * blk_own
    table[n_blocks] = zero

    for copy in copies:
        copy.wait()
    n_seg = acc[0].shape[0]
    width = n_chunk * SUB

    def clear(r, carry):
        for a in acc:
            a[r] = jnp.zeros(a.shape[1:], jnp.float32)
        return carry

    lax.fori_loop(0, n_seg, clear, 0)

    k_id = lax.broadcasted_iota(jnp.int32, (width, LANES), 0)
    n_id = lax.broadcasted_iota(jnp.int32, (width, LANES), 1)
    base_id = n_id - per * (k_id // SUB)
    for par in range(per):
        for jp in range(per):
            at = (par * per + jp) * width
            hit = (base_id == side * par + jp).astype(jnp.float32)
            select[at:at + width, :] = hit.astype(jnp.bfloat16)

    rows_of = per * kvec

    def product(base, half, x, check):
        xh = x[half * SUB:(half + 1) * SUB]
        w = jnp.concatenate(
            [xh[:, c * LANES:(c + 1) * LANES] for c in range(n_chunk)], axis=0
        ).astype(jnp.bfloat16)
        entries = []
        for t in range(SUB):
            slot = base + half * SUB + t
            at = cols_s[slot]
            entry = table[jnp.where(slot < count, at, n_blocks) if check else at]
            entries.append(jnp.where(low, entry, zero))
            entries.append(jnp.where(low, zero, entry))
        left = jnp.concatenate(entries, axis=0).astype(jnp.bfloat16)
        return lax.dot_general(left, w, NT, preferred_element_type=jnp.float32)

    lane_w = lax.broadcasted_iota(jnp.int32, (rows_of, width), 1) % SUB

    def accumulate(at, out):
        for t in range(SUB):
            r = rows_s[at + t]
            mine = jnp.where(lane_w == t, out[t * rows_of:(t + 1) * rows_of], 0.0)
            acc[t % len(acc)][r] += mine

    def step(first, slots_in, check):
        for i in range(slots_in // CHUNK):
            tile_copy(first // CHUNK + i).wait()
        waiting = None
        for q in range(slots_in // (2 * SUB)):
            base = pl.multiple_of(first + q * 2 * SUB, 2 * SUB)
            x = buf[pl.ds(base, 2 * SUB), :].astype(jnp.float32)
            for half in range(2):
                out = product(base, half, x, check)
                if waiting is not None:
                    accumulate(*waiting)
                waiting = (base + half * SUB, out)
        accumulate(*waiting)

    def full_step(i, carry):
        step(i * STEP, STEP, False)
        return carry

    def last_step(ch, carry):
        step(ch * CHUNK, CHUNK, True)
        return carry

    full = count // STEP
    lax.fori_loop(0, full, full_step, 0)
    lax.fori_loop(full * (STEP // CHUNK), used, last_step, 0)

    pairs = n_seg // per

    def pick(m, carry):
        pieces = []
        for par in range(per):
            total = acc[0][m * per + par]
            for other in acc[1:]:
                total = total + other[m * per + par]
            for jp in range(per):
                pieces.append(total[jp * kvec:(jp + 1) * kvec])
        a = jnp.concatenate(pieces, axis=1)
        hi = a.astype(jnp.bfloat16).astype(jnp.float32)
        both = jnp.concatenate([hi, a - hi], axis=0).astype(jnp.bfloat16)
        picked[pl.ds(pl.multiple_of(m * 2 * kvec, 2 * kvec), 2 * kvec), :] = both
        return carry

    lax.fori_loop(0, pairs, pick, 0)

    spread = jnp.dot(picked[...], select[...], preferred_element_type=jnp.float32)
    for m in range(pairs):
        at = m * 2 * kvec
        row = spread[at:at + kvec] + spread[at + kvec:at + 2 * kvec]
        c, lane0 = divmod(m * LANES, own)
        part[c, :, lane0:lane0 + LANES] = row

    own_ref[...] = part[my_col] + ener[...] * gath[0][my_far].astype(jnp.float32)
    for s in range(1, n_col):
        share = part[lax.rem(my_col + s, n_col)]
        send_ref[s - 1] = share.astype(jnp.bfloat16)
        rest_ref[s - 1] = share


def tile_work(rows, cols, count, gath, n_col, ener, tiles):
    n_core = len(gath)
    n_far, kvec, own = gath[0].shape
    slots, area = tiles.shape
    side = math.isqrt(area)
    per = LANES // side
    blk_own = own // side
    n_seg = n_col * blk_own
    width = area // LANES * SUB
    vmem = pl.BlockSpec(memory_space=pltpu.VMEM)
    far_away = pl.BlockSpec(memory_space=pltpu.HBM)
    return pl.pallas_call(
        functools.partial(tile_kernel, n_core, n_col, side),
        out_shape=(
            jax.ShapeDtypeStruct((kvec, own), jnp.float32),
            jax.ShapeDtypeStruct((n_col - 1, kvec, own), jnp.bfloat16),
            jax.ShapeDtypeStruct((n_col - 1, kvec, own), jnp.float32),
        ),
        in_specs=[pl.BlockSpec(memory_space=pltpu.SMEM)] + [far_away] * 4 + [vmem] * n_core,
        out_specs=(vmem, vmem, vmem),
        scratch_shapes=[
            pltpu.SMEM((slots,), jnp.int32),
            pltpu.SMEM((slots,), jnp.int32),
            pltpu.VMEM((1, own), jnp.float32),
            pltpu.VMEM((slots, area), jnp.bfloat16),
            pltpu.VMEM((n_far * n_core * blk_own + 1, kvec, LANES), jnp.float32),
            pltpu.VMEM((n_seg // per * 2 * kvec, per * per * width), jnp.bfloat16),
            pltpu.VMEM((per * per * width, LANES), jnp.bfloat16),
            pltpu.VMEM((n_col, kvec, own), jnp.float32),
            pltpu.SemaphoreType.DMA((slots // CHUNK,)),
            pltpu.SemaphoreType.DMA((3,)),
        ] + [pltpu.VMEM((n_seg, per * kvec, width), jnp.float32)] * SUMS,
        compiler_params=pltpu.CompilerParams(vmem_limit_bytes=48 * 2**20),
        cost_estimate=pl.CostEstimate(
            flops=2 * slots * area * kvec, bytes_accessed=2 * slots * area, transcendentals=0
        ),
        name="tile_work",
    )(count, *[pltpu.with_memory_space_constraint(x, pltpu.HBM) for x in (rows, cols, ener, tiles)],
      *gath)


def terms_kernel(own, rest, vec, *refs):
    others, (terms_ref, wide) = refs[:-2], refs[-2:]
    n_col = len(others) + 1
    kvec = vec.shape[0]

    def outer(share, seg):
        return lax.dot_general(
            share, seg[...].astype(jnp.float32), NT,
            precision=lax.Precision.HIGHEST, preferred_element_type=jnp.float32,
        )

    terms = outer(own[...], vec)
    for s in range(1, n_col):
        terms = terms + outer(rest[s - 1], others[n_col - s - 1])
    wide[...] = jnp.zeros(wide.shape, jnp.float32)
    wide[:, :kvec] = terms
    spaced = pltpu.roll(wide[...], 0, 1, stride=kvec, stride_axis=0)
    terms_ref[...] = jnp.sum(spaced, axis=0, keepdims=True)


def gram_terms(own, rest, vectors, others):
    vmem = pl.BlockSpec(memory_space=pltpu.VMEM)
    return pl.pallas_call(
        terms_kernel,
        out_shape=jax.ShapeDtypeStruct((1, LANES), jnp.float32),
        in_specs=[vmem] * (3 + len(others)),
        out_specs=vmem,
        scratch_shapes=[pltpu.VMEM((vectors.shape[0], LANES), jnp.float32)],
        compiler_params=pltpu.CompilerParams(vmem_limit_bytes=4 * 2**20),
        name="gram_terms",
    )(own, rest, vectors, *others)


def finish_kernel(scale, base, gram_parts, vec, *refs):
    got, (product, residual) = refs[:-2], refs[-2:]
    whole = base[...]
    for piece in got:
        whole = whole + piece[...].astype(jnp.float32)
    product[...] = whole.astype(jnp.bfloat16)
    flat = gram_parts[0]
    for i in range(1, gram_parts.shape[0]):
        flat = flat + gram_parts[i]
    kvec = vec.shape[0]
    lane = lax.broadcasted_iota(jnp.int32, (kvec, LANES), 1)
    first = kvec * lax.broadcasted_iota(jnp.int32, (kvec, LANES), 0)
    wide = jnp.broadcast_to(flat * scale, (kvec, LANES))
    vec32 = vec[...].astype(jnp.float32)
    for a in range(kvec):
        column = jnp.sum(jnp.where(lane == first + a, wide, 0.0), axis=1, keepdims=True)
        whole = whole - column * vec32[a:a + 1, :]
    residual[...] = whole


def finish(scale, base, gram_parts, vectors, got):
    vmem = pl.BlockSpec(memory_space=pltpu.VMEM)
    return pl.pallas_call(
        functools.partial(finish_kernel, scale),
        out_shape=(
            jax.ShapeDtypeStruct(vectors.shape, jnp.bfloat16),
            jax.ShapeDtypeStruct(vectors.shape, jnp.float32),
        ),
        in_specs=[vmem] * (3 + len(got)),
        out_specs=(vmem, vmem),
        compiler_params=pltpu.CompilerParams(vmem_limit_bytes=4 * 2**20),
        name="finish",
    )(base, gram_parts, vectors, *got)


def from_all(x, axis):
    size = lax.axis_size(axis)
    got = [x]
    for s in range(1, size):
        got.append(lax.ppermute(x, axis, [(i, (i + s) % size) for i in range(size)]))
    return got


def per_device(vectors, energies, tiles, tile_rows, tile_cols, tile_count):
    kvec, own = vectors.shape
    n_col = lax.axis_size("col")
    copies = jnp.broadcast_to(vectors[None], (lax.axis_size("far"), kvec, own))
    gath = lax.all_to_all(copies, "far", 0, 0)
    gath = from_all(gath, "core")
    base, send, rest = tile_work(
        tile_rows, tile_cols, tile_count, gath, n_col, energies[None, :], tiles
    )
    got = [
        lax.ppermute(send[s - 1], "col", [(c, (c + s) % n_col) for c in range(n_col)])
        for s in range(1, n_col)
    ]
    others = from_all(vectors, "col")[1:]
    members = lax.axis_size(("far", "core", "col"))
    terms = gram_terms(base, rest, vectors, others)
    terms = jnp.broadcast_to(terms[None], (members,) + terms.shape)
    gram_parts = lax.all_to_all(terms, ("far", "core", "col"), 0, 0)
    return finish(1.0 / (members * own), base, gram_parts, vectors, got)


def solution(mesh):
    n_row, n_col = mesh.devices.shape
    n_core = 2 if n_row % 2 == 0 else 1
    split = ("far", "core", "col")
    chips = Mesh(mesh.devices.reshape(n_row // n_core, n_core, n_col), split)
    in_specs = (P(None, split), P(split), P(split, None), P(split), P(split), P(split))
    out_specs = (P(None, split), P(None, split))
    return jax.shard_map(
        per_device, mesh=chips, in_specs=in_specs, out_specs=out_specs, check_vma=False
    )
```

```python
import functools
import math

import jax
import jax.numpy as jnp
from jax import lax
from jax.experimental import pallas as pl
from jax.experimental.pallas import tpu as pltpu
from jax.sharding import Mesh, PartitionSpec as P

LANES = 128
SUB = 8
CHUNK = 128
STEP = 256
SUMS = 4

NT = (((1,), (1,)), ((), ()))


def tile_kernel(
    n_core, n_col, side, count_s, rows_h, cols_h, ener_h, tiles, *refs,
):
    gath, refs = refs[:n_core], refs[n_core:]
    (own_ref, send_ref, rest_ref, rows_s, cols_s, ener,
     buf, table, picked, select, part, sems, small, *acc) = refs
    n_far, kvec, own = gath[0].shape
    slots = tiles.shape[0]
    blk_own = own // side
    per = LANES // side
    n_chunk = tiles.shape[1] // LANES
    my_far, my_core, my_col = (lax.axis_index(name) for name in ("far", "core", "col"))

    copies = [
        pltpu.make_async_copy(src, dst, small.at[i])
        for i, (src, dst) in enumerate(
            ((cols_h, cols_s), (rows_h, rows_s), (ener_h, ener))
        )
    ]
    for copy in copies:
        copy.start()

    def tile_copy(ch):
        span = pl.ds(pl.multiple_of(ch * CHUNK, CHUNK), CHUNK)
        return pltpu.make_async_copy(tiles.at[span], buf.at[span], sems.at[ch])

    count = count_s[0]
    used = (count + CHUNK - 1) // CHUNK

    def start(ch, carry):
        tile_copy(ch).start()
        return carry

    lax.fori_loop(0, used, start, 0)

    lane = lax.broadcasted_iota(jnp.int32, (kvec, LANES), 1)
    low = lane < side
    zero = jnp.zeros((kvec, LANES), jnp.float32)

    for s in range(n_core):
        core = lax.rem(my_core + (n_core - s), n_core)
        for f in range(n_far):
            for p in range(own // LANES):
                x = gath[s][f, :, p * LANES:(p + 1) * LANES].astype(jnp.float32)
                y = pltpu.roll(x, side, 1)
                at = (f * n_core + core) * blk_own + p * per
                even = jnp.concatenate([jnp.where(low, x, zero), jnp.where(low, zero, y)], axis=0)
                odd = jnp.concatenate([jnp.where(low, y, zero), jnp.where(low, zero, x)], axis=0)
                table[at] = even
                table[at + 1] = odd
    n_blocks = n_far * n_core * blk_own
    table[n_blocks] = jnp.zeros((per * kvec, LANES), jnp.float32)

    for copy in copies:
        copy.wait()
    n_seg = acc[0].shape[0]
    width = n_chunk * SUB

    def clear(r, carry):
        for a in acc:
            a[r] = jnp.zeros(a.shape[1:], jnp.float32)
        return carry

    lax.fori_loop(0, n_seg, clear, 0)

    k_id = lax.broadcasted_iota(jnp.int32, (width, LANES), 0)
    n_id = lax.broadcasted_iota(jnp.int32, (width, LANES), 1)
    base_id = n_id - per * (k_id // SUB)
    for par in range(per):
        for jp in range(per):
            at = (par * per + jp) * width
            hit = (base_id == side * par + jp).astype(jnp.float32)
            select[at:at + width, :] = hit.astype(jnp.bfloat16)

    rows_of = per * kvec

    def product(base, half, x, check):
        xh = x[half * SUB:(half + 1) * SUB]
        w = jnp.concatenate(
            [xh[:, c * LANES:(c + 1) * LANES] for c in range(n_chunk)], axis=0
        ).astype(jnp.bfloat16)
        entries = []
        for t in range(SUB):
            slot = base + half * SUB + t
            at = cols_s[slot]
            entries.append(table[jnp.where(slot < count, at, n_blocks) if check else at])
        outs = []
        for i in range(0, SUB, SUB // 2):
            left = jnp.concatenate(entries[i:i + SUB // 2], axis=0).astype(jnp.bfloat16)
            out = lax.dot_general(left, w, NT, preferred_element_type=jnp.float32)
            outs += [out[t * rows_of:(t + 1) * rows_of] for t in range(SUB // 2)]
        return outs

    lane_w = lax.broadcasted_iota(jnp.int32, (rows_of, width), 1) % SUB

    def accumulate(at, out):
        for t in range(SUB):
            r = rows_s[at + t]
            mine = jnp.where(lane_w == t, out[t], 0.0)
            acc[t % len(acc)][r] += mine

    def step(first, slots_in, check):
        for i in range(slots_in // CHUNK):
            tile_copy(first // CHUNK + i).wait()
        waiting = None
        for q in range(slots_in // (2 * SUB)):
            base = pl.multiple_of(first + q * 2 * SUB, 2 * SUB)
            x = buf[pl.ds(base, 2 * SUB), :].astype(jnp.float32)
            for half in range(2):
                out = product(base, half, x, check)
                if waiting is not None:
                    accumulate(*waiting)
                waiting = (base + half * SUB, out)
        accumulate(*waiting)

    def full_step(i, carry):
        step(i * STEP, STEP, False)
        return carry

    def last_step(ch, carry):
        step(ch * CHUNK, CHUNK, True)
        return carry

    full = count // STEP
    lax.fori_loop(0, full, full_step, 0)
    lax.fori_loop(full * (STEP // CHUNK), used, last_step, 0)

    pairs = n_seg // per

    def pick(m, carry):
        pieces = []
        for par in range(per):
            total = acc[0][m * per + par]
            for other in acc[1:]:
                total = total + other[m * per + par]
            for jp in range(per):
                pieces.append(total[jp * kvec:(jp + 1) * kvec])
        a = jnp.concatenate(pieces, axis=1)
        hi = a.astype(jnp.bfloat16).astype(jnp.float32)
        both = jnp.concatenate([hi, a - hi], axis=0).astype(jnp.bfloat16)
        picked[pl.ds(pl.multiple_of(m * 2 * kvec, 2 * kvec), 2 * kvec), :] = both
        return carry

    lax.fori_loop(0, pairs, pick, 0)

    spread = jnp.dot(picked[...], select[...], preferred_element_type=jnp.float32)
    for m in range(pairs):
        at = m * 2 * kvec
        row = spread[at:at + kvec] + spread[at + kvec:at + 2 * kvec]
        c, lane0 = divmod(m * LANES, own)
        part[c, :, lane0:lane0 + LANES] = row

    own_ref[...] = part[my_col] + ener[...] * gath[0][my_far].astype(jnp.float32)
    for s in range(1, n_col):
        share = part[lax.rem(my_col + s, n_col)]
        send_ref[s - 1] = share.astype(jnp.bfloat16)
        rest_ref[s - 1] = share


def tile_work(rows, cols, count, gath, n_col, ener, tiles):
    n_core = len(gath)
    n_far, kvec, own = gath[0].shape
    slots, area = tiles.shape
    side = math.isqrt(area)
    per = LANES // side
    blk_own = own // side
    n_seg = n_col * blk_own
    width = area // LANES * SUB
    vmem = pl.BlockSpec(memory_space=pltpu.VMEM)
    far_away = pl.BlockSpec(memory_space=pltpu.HBM)
    return pl.pallas_call(
        functools.partial(tile_kernel, n_core, n_col, side),
        out_shape=(
            jax.ShapeDtypeStruct((kvec, own), jnp.float32),
            jax.ShapeDtypeStruct((n_col - 1, kvec, own), jnp.bfloat16),
            jax.ShapeDtypeStruct((n_col - 1, kvec, own), jnp.float32),
        ),
        in_specs=[pl.BlockSpec(memory_space=pltpu.SMEM)] + [far_away] * 4 + [vmem] * n_core,
        out_specs=(vmem, vmem, vmem),
        scratch_shapes=[
            pltpu.SMEM((slots,), jnp.int32),
            pltpu.SMEM((slots,), jnp.int32),
            pltpu.VMEM((1, own), jnp.float32),
            pltpu.VMEM((slots, area), jnp.bfloat16),
            pltpu.VMEM((n_far * n_core * blk_own + 1, per * kvec, LANES), jnp.float32),
            pltpu.VMEM((n_seg // per * 2 * kvec, per * per * width), jnp.bfloat16),
            pltpu.VMEM((per * per * width, LANES), jnp.bfloat16),
            pltpu.VMEM((n_col, kvec, own), jnp.float32),
            pltpu.SemaphoreType.DMA((slots // CHUNK,)),
            pltpu.SemaphoreType.DMA((3,)),
        ] + [pltpu.VMEM((n_seg, per * kvec, width), jnp.float32)] * SUMS,
        compiler_params=pltpu.CompilerParams(vmem_limit_bytes=48 * 2**20),
        cost_estimate=pl.CostEstimate(
            flops=2 * slots * area * kvec, bytes_accessed=2 * slots * area, transcendentals=0
        ),
        name="tile_work",
    )(count, *[pltpu.with_memory_space_constraint(x, pltpu.HBM) for x in (rows, cols, ener, tiles)],
      *gath)


def terms_kernel(own, rest, vec, *refs):
    others, (terms_ref, wide) = refs[:-2], refs[-2:]
    n_col = len(others) + 1
    kvec = vec.shape[0]

    def outer(share, seg):
        return lax.dot_general(
            share, seg[...].astype(jnp.float32), NT,
            precision=lax.Precision.HIGHEST, preferred_element_type=jnp.float32,
        )

    terms = outer(own[...], vec)
    for s in range(1, n_col):
        terms = terms + outer(rest[s - 1], others[n_col - s - 1])
    wide[...] = jnp.zeros(wide.shape, jnp.float32)
    wide[:, :kvec] = terms
    spaced = pltpu.roll(wide[...], 0, 1, stride=kvec, stride_axis=0)
    terms_ref[...] = jnp.sum(spaced, axis=0, keepdims=True)


def gram_terms(own, rest, vectors, others):
    vmem = pl.BlockSpec(memory_space=pltpu.VMEM)
    return pl.pallas_call(
        terms_kernel,
        out_shape=jax.ShapeDtypeStruct((1, LANES), jnp.float32),
        in_specs=[vmem] * (3 + len(others)),
        out_specs=vmem,
        scratch_shapes=[pltpu.VMEM((vectors.shape[0], LANES), jnp.float32)],
        compiler_params=pltpu.CompilerParams(vmem_limit_bytes=4 * 2**20),
        name="gram_terms",
    )(own, rest, vectors, *others)


def finish_kernel(scale, base, gram_parts, vec, *refs):
    got, (product, residual) = refs[:-2], refs[-2:]
    whole = base[...]
    for piece in got:
        whole = whole + piece[...].astype(jnp.float32)
    product[...] = whole.astype(jnp.bfloat16)
    flat = gram_parts[0]
    for i in range(1, gram_parts.shape[0]):
        flat = flat + gram_parts[i]
    kvec = vec.shape[0]
    lane = lax.broadcasted_iota(jnp.int32, (kvec, LANES), 1)
    first = kvec * lax.broadcasted_iota(jnp.int32, (kvec, LANES), 0)
    wide = jnp.broadcast_to(flat * scale, (kvec, LANES))
    vec32 = vec[...].astype(jnp.float32)
    for a in range(kvec):
        column = jnp.sum(jnp.where(lane == first + a, wide, 0.0), axis=1, keepdims=True)
        whole = whole - column * vec32[a:a + 1, :]
    residual[...] = whole


def finish(scale, base, gram_parts, vectors, got):
    vmem = pl.BlockSpec(memory_space=pltpu.VMEM)
    return pl.pallas_call(
        functools.partial(finish_kernel, scale),
        out_shape=(
            jax.ShapeDtypeStruct(vectors.shape, jnp.bfloat16),
            jax.ShapeDtypeStruct(vectors.shape, jnp.float32),
        ),
        in_specs=[vmem] * (3 + len(got)),
        out_specs=(vmem, vmem),
        compiler_params=pltpu.CompilerParams(vmem_limit_bytes=4 * 2**20),
        name="finish",
    )(base, gram_parts, vectors, *got)


def from_all(x, axis):
    size = lax.axis_size(axis)
    got = [x]
    for s in range(1, size):
        got.append(lax.ppermute(x, axis, [(i, (i + s) % size) for i in range(size)]))
    return got


def per_device(vectors, energies, tiles, tile_rows, tile_cols, tile_count):
    kvec, own = vectors.shape
    n_col = lax.axis_size("col")
    copies = jnp.broadcast_to(vectors[None], (lax.axis_size("far"), kvec, own))
    gath = lax.all_to_all(copies, "far", 0, 0)
    gath = from_all(gath, "core")
    base, send, rest = tile_work(
        tile_rows, tile_cols, tile_count, gath, n_col, energies[None, :], tiles
    )
    got = [
        lax.ppermute(send[s - 1], "col", [(c, (c + s) % n_col) for c in range(n_col)])
        for s in range(1, n_col)
    ]
    others = from_all(vectors, "col")[1:]
    members = lax.axis_size(("far", "core", "col"))
    terms = gram_terms(base, rest, vectors, others)
    terms = jnp.broadcast_to(terms[None], (members,) + terms.shape)
    gram_parts = lax.all_to_all(terms, ("far", "core", "col"), 0, 0)
    return finish(1.0 / (members * own), base, gram_parts, vectors, got)


def solution(mesh):
    n_row, n_col = mesh.devices.shape
    n_core = 2 if n_row % 2 == 0 else 1
    split = ("far", "core", "col")
    chips = Mesh(mesh.devices.reshape(n_row // n_core, n_core, n_col), split)
    in_specs = (P(None, split), P(split), P(split, None), P(split), P(split), P(split))
    out_specs = (P(None, split), P(None, split))
    return jax.shard_map(
        per_device, mesh=chips, in_specs=in_specs, out_specs=out_specs, check_vma=False
    )
```

```python
import functools
import math

import jax
import jax.numpy as jnp
from jax import lax
from jax.experimental import pallas as pl
from jax.experimental.pallas import tpu as pltpu
from jax.sharding import Mesh, PartitionSpec as P

LANES = 128
SUB = 8
CHUNK = 128
STEP = 256
SUMS = 4

NT = (((1,), (1,)), ((), ()))


def tile_kernel(
    n_core, n_col, side, count_s, rows_h, cols_h, ener_h, tiles, *refs,
):
    gath, refs = refs[:n_core], refs[n_core:]
    (own_ref, send_ref, rest_ref, rows_s, cols_s, ener,
     buf, table, picked, select, part, sems, small, *acc) = refs
    n_far, kvec, own = gath[0].shape
    slots = tiles.shape[0]
    blk_own = own // side
    per = LANES // side
    n_chunk = tiles.shape[1] // LANES
    my_far, my_core, my_col = (lax.axis_index(name) for name in ("far", "core", "col"))

    copies = [
        pltpu.make_async_copy(src, dst, small.at[i])
        for i, (src, dst) in enumerate(
            ((cols_h, cols_s), (rows_h, rows_s), (ener_h, ener))
        )
    ]
    for copy in copies:
        copy.start()

    def tile_copy(ch):
        span = pl.ds(pl.multiple_of(ch * CHUNK, CHUNK), CHUNK)
        return pltpu.make_async_copy(tiles.at[span], buf.at[span], sems.at[ch])

    count = count_s[0]
    used = (count + CHUNK - 1) // CHUNK

    def ask(ch):
        @pl.when(ch < used)
        def _():
            tile_copy(ch).start()

    ahead = STEP // CHUNK
    for ch in range(ahead):
        ask(ch)

    lane = lax.broadcasted_iota(jnp.int32, (kvec, LANES), 1)
    low = lane < side
    zero = jnp.zeros((kvec, LANES), jnp.float32)

    for s in range(n_core):
        core = lax.rem(my_core + (n_core - s), n_core)
        for f in range(n_far):
            for p in range(own // LANES):
                x = gath[s][f, :, p * LANES:(p + 1) * LANES].astype(jnp.float32)
                y = pltpu.roll(x, side, 1)
                at = (f * n_core + core) * blk_own + p * per
                table[at] = jnp.where(low, x, y)
                table[at + 1] = jnp.where(low, y, x)
    n_blocks = n_far * n_core * blk_own
    table[n_blocks] = zero

    n_seg = acc[0].shape[0]
    width = n_chunk * SUB

    def clear(r, carry):
        for a in acc:
            a[r] = jnp.zeros(a.shape[1:], jnp.float32)
        return carry

    lax.fori_loop(0, n_seg, clear, 0)

    k_id = lax.broadcasted_iota(jnp.int32, (width, LANES), 0)
    n_id = lax.broadcasted_iota(jnp.int32, (width, LANES), 1)
    base_id = n_id - per * (k_id // SUB)
    for par in range(per):
        for jp in range(per):
            at = (par * per + jp) * width
            hit = (base_id == side * par + jp).astype(jnp.float32)
            select[at:at + width, :] = hit.astype(jnp.bfloat16)

    rows_of = per * kvec

    def product(base, half, x, check):
        xh = x[half * SUB:(half + 1) * SUB]
        w = jnp.concatenate(
            [xh[:, c * LANES:(c + 1) * LANES] for c in range(n_chunk)], axis=0
        ).astype(jnp.bfloat16)
        entries = []
        for t in range(SUB):
            slot = base + half * SUB + t
            at = cols_s[slot]
            entry = table[jnp.where(slot < count, at, n_blocks) if check else at]
            entries.append(jnp.where(low, entry, zero))
            entries.append(jnp.where(low, zero, entry))
        left = jnp.concatenate(entries, axis=0).astype(jnp.bfloat16)
        return lax.dot_general(left, w, NT, preferred_element_type=jnp.float32)

    lane_w = lax.broadcasted_iota(jnp.int32, (rows_of, width), 1) % SUB

    def accumulate(at, out):
        for t in range(SUB):
            r = rows_s[at + t]
            mine = jnp.where(lane_w == t, out[t * rows_of:(t + 1) * rows_of], 0.0)
            acc[t % len(acc)][r] += mine

    def step(first, slots_in, check):
        for i in range(slots_in // CHUNK):
            tile_copy(first // CHUNK + i).wait()
        waiting = None
        for q in range(slots_in // (2 * SUB)):
            base = pl.multiple_of(first + q * 2 * SUB, 2 * SUB)
            x = buf[pl.ds(base, 2 * SUB), :].astype(jnp.float32)
            for half in range(2):
                out = product(base, half, x, check)
                if waiting is not None:
                    accumulate(*waiting)
                waiting = (base + half * SUB, out)
        accumulate(*waiting)

    def full_step(i, carry):
        for ch in range(ahead):
            ask((i + 2) * ahead + ch)
        step(i * STEP, STEP, False)
        return carry

    def last_step(ch, carry):
        step(ch * CHUNK, CHUNK, True)
        return carry

    for ch in range(ahead, 2 * ahead):
        ask(ch)
    for copy in copies[:2]:
        copy.wait()
    full = count // STEP
    lax.fori_loop(0, full, full_step, 0)
    lax.fori_loop(full * (STEP // CHUNK), used, last_step, 0)

    pairs = n_seg // per

    def pick(m, carry):
        pieces = []
        for par in range(per):
            total = acc[0][m * per + par]
            for other in acc[1:]:
                total = total + other[m * per + par]
            for jp in range(per):
                pieces.append(total[jp * kvec:(jp + 1) * kvec])
        a = jnp.concatenate(pieces, axis=1)
        hi = a.astype(jnp.bfloat16).astype(jnp.float32)
        both = jnp.concatenate([hi, a - hi], axis=0).astype(jnp.bfloat16)
        picked[pl.ds(pl.multiple_of(m * 2 * kvec, 2 * kvec), 2 * kvec), :] = both
        return carry

    lax.fori_loop(0, pairs, pick, 0)

    spread = jnp.dot(picked[...], select[...], preferred_element_type=jnp.float32)
    for m in range(pairs):
        at = m * 2 * kvec
        row = spread[at:at + kvec] + spread[at + kvec:at + 2 * kvec]
        c, lane0 = divmod(m * LANES, own)
        part[c, :, lane0:lane0 + LANES] = row

    copies[2].wait()
    own_ref[...] = part[my_col] + ener[...] * gath[0][my_far].astype(jnp.float32)
    for s in range(1, n_col):
        share = part[lax.rem(my_col + s, n_col)]
        send_ref[s - 1] = share.astype(jnp.bfloat16)
        rest_ref[s - 1] = share


def tile_work(rows, cols, count, gath, n_col, ener, tiles):
    n_core = len(gath)
    n_far, kvec, own = gath[0].shape
    slots, area = tiles.shape
    side = math.isqrt(area)
    per = LANES // side
    blk_own = own // side
    n_seg = n_col * blk_own
    width = area // LANES * SUB
    vmem = pl.BlockSpec(memory_space=pltpu.VMEM)
    far_away = pl.BlockSpec(memory_space=pltpu.HBM)
    return pl.pallas_call(
        functools.partial(tile_kernel, n_core, n_col, side),
        out_shape=(
            jax.ShapeDtypeStruct((kvec, own), jnp.float32),
            jax.ShapeDtypeStruct((n_col - 1, kvec, own), jnp.bfloat16),
            jax.ShapeDtypeStruct((n_col - 1, kvec, own), jnp.float32),
        ),
        in_specs=[pl.BlockSpec(memory_space=pltpu.SMEM)] + [far_away] * 4 + [vmem] * n_core,
        out_specs=(vmem, vmem, vmem),
        scratch_shapes=[
            pltpu.SMEM((slots,), jnp.int32),
            pltpu.SMEM((slots,), jnp.int32),
            pltpu.VMEM((1, own), jnp.float32),
            pltpu.VMEM((slots, area), jnp.bfloat16),
            pltpu.VMEM((n_far * n_core * blk_own + 1, kvec, LANES), jnp.float32),
            pltpu.VMEM((n_seg // per * 2 * kvec, per * per * width), jnp.bfloat16),
            pltpu.VMEM((per * per * width, LANES), jnp.bfloat16),
            pltpu.VMEM((n_col, kvec, own), jnp.float32),
            pltpu.SemaphoreType.DMA((slots // CHUNK,)),
            pltpu.SemaphoreType.DMA((3,)),
        ] + [pltpu.VMEM((n_seg, per * kvec, width), jnp.float32)] * SUMS,
        compiler_params=pltpu.CompilerParams(vmem_limit_bytes=48 * 2**20),
        cost_estimate=pl.CostEstimate(
            flops=2 * slots * area * kvec, bytes_accessed=2 * slots * area, transcendentals=0
        ),
        name="tile_work",
    )(count, *[pltpu.with_memory_space_constraint(x, pltpu.HBM) for x in (rows, cols, ener, tiles)],
      *gath)


def terms_kernel(own, rest, vec, *refs):
    others, (terms_ref, wide) = refs[:-2], refs[-2:]
    n_col = len(others) + 1
    kvec = vec.shape[0]

    def outer(share, seg):
        return lax.dot_general(
            share, seg[...].astype(jnp.float32), NT,
            precision=lax.Precision.HIGHEST, preferred_element_type=jnp.float32,
        )

    terms = outer(own[...], vec)
    for s in range(1, n_col):
        terms = terms + outer(rest[s - 1], others[n_col - s - 1])
    wide[...] = jnp.zeros(wide.shape, jnp.float32)
    wide[:, :kvec] = terms
    spaced = pltpu.roll(wide[...], 0, 1, stride=kvec, stride_axis=0)
    terms_ref[...] = jnp.sum(spaced, axis=0, keepdims=True)


def gram_terms(own, rest, vectors, others):
    vmem = pl.BlockSpec(memory_space=pltpu.VMEM)
    return pl.pallas_call(
        terms_kernel,
        out_shape=jax.ShapeDtypeStruct((1, LANES), jnp.float32),
        in_specs=[vmem] * (3 + len(others)),
        out_specs=vmem,
        scratch_shapes=[pltpu.VMEM((vectors.shape[0], LANES), jnp.float32)],
        compiler_params=pltpu.CompilerParams(vmem_limit_bytes=4 * 2**20),
        name="gram_terms",
    )(own, rest, vectors, *others)


def finish_kernel(scale, base, gram_parts, vec, *refs):
    got, (product, residual) = refs[:-2], refs[-2:]
    whole = base[...]
    for piece in got:
        whole = whole + piece[...].astype(jnp.float32)
    product[...] = whole.astype(jnp.bfloat16)
    flat = gram_parts[0]
    for i in range(1, gram_parts.shape[0]):
        flat = flat + gram_parts[i]
    kvec = vec.shape[0]
    lane = lax.broadcasted_iota(jnp.int32, (kvec, LANES), 1)
    first = kvec * lax.broadcasted_iota(jnp.int32, (kvec, LANES), 0)
    wide = jnp.broadcast_to(flat * scale, (kvec, LANES))
    vec32 = vec[...].astype(jnp.float32)
    for a in range(kvec):
        column = jnp.sum(jnp.where(lane == first + a, wide, 0.0), axis=1, keepdims=True)
        whole = whole - column * vec32[a:a + 1, :]
    residual[...] = whole


def finish(scale, base, gram_parts, vectors, got):
    vmem = pl.BlockSpec(memory_space=pltpu.VMEM)
    return pl.pallas_call(
        functools.partial(finish_kernel, scale),
        out_shape=(
            jax.ShapeDtypeStruct(vectors.shape, jnp.bfloat16),
            jax.ShapeDtypeStruct(vectors.shape, jnp.float32),
        ),
        in_specs=[vmem] * (3 + len(got)),
        out_specs=(vmem, vmem),
        compiler_params=pltpu.CompilerParams(vmem_limit_bytes=4 * 2**20),
        name="finish",
    )(base, gram_parts, vectors, *got)


def from_all(x, axis):
    size = lax.axis_size(axis)
    got = [x]
    for s in range(1, size):
        got.append(lax.ppermute(x, axis, [(i, (i + s) % size) for i in range(size)]))
    return got


def per_device(vectors, energies, tiles, tile_rows, tile_cols, tile_count):
    kvec, own = vectors.shape
    n_col = lax.axis_size("col")
    copies = jnp.broadcast_to(vectors[None], (lax.axis_size("far"), kvec, own))
    gath = lax.all_to_all(copies, "far", 0, 0)
    gath = from_all(gath, "core")
    base, send, rest = tile_work(
        tile_rows, tile_cols, tile_count, gath, n_col, energies[None, :], tiles
    )
    got = [
        lax.ppermute(send[s - 1], "col", [(c, (c + s) % n_col) for c in range(n_col)])
        for s in range(1, n_col)
    ]
    others = from_all(vectors, "col")[1:]
    members = lax.axis_size(("far", "core", "col"))
    terms = gram_terms(base, rest, vectors, others)
    terms = jnp.broadcast_to(terms[None], (members,) + terms.shape)
    gram_parts = lax.all_to_all(terms, ("far", "core", "col"), 0, 0)
    return finish(1.0 / (members * own), base, gram_parts, vectors, got)


def solution(mesh):
    n_row, n_col = mesh.devices.shape
    n_core = 2 if n_row % 2 == 0 else 1
    split = ("far", "core", "col")
    chips = Mesh(mesh.devices.reshape(n_row // n_core, n_core, n_col), split)
    in_specs = (P(None, split), P(split), P(split, None), P(split), P(split), P(split))
    out_specs = (P(None, split), P(None, split))
    return jax.shard_map(
        per_device, mesh=chips, in_specs=in_specs, out_specs=out_specs, check_vma=False
    )
```

```python
import functools
import math

import jax
import jax.numpy as jnp
from jax import lax
from jax.experimental import pallas as pl
from jax.experimental.pallas import tpu as pltpu
from jax.sharding import Mesh, PartitionSpec as P

LANES = 128
SUB = 8
CHUNK = 64
STEP = 256
SUMS = 4

NT = (((1,), (1,)), ((), ()))


def tile_kernel(
    n_core, n_col, side, count_s, rows_h, cols_h, ener_h, tiles, *refs,
):
    gath, refs = refs[:n_core], refs[n_core:]
    (own_ref, send_ref, rest_ref, rows_s, cols_s, ener,
     buf, table, picked, select, part, sems, small, *acc) = refs
    n_far, kvec, own = gath[0].shape
    slots = tiles.shape[0]
    blk_own = own // side
    per = LANES // side
    n_chunk = tiles.shape[1] // LANES
    my_far, my_core, my_col = (lax.axis_index(name) for name in ("far", "core", "col"))

    copies = [
        pltpu.make_async_copy(src, dst, small.at[i])
        for i, (src, dst) in enumerate(
            ((cols_h, cols_s), (rows_h, rows_s), (ener_h, ener))
        )
    ]
    for copy in copies:
        copy.start()

    def tile_copy(ch):
        span = pl.ds(pl.multiple_of(ch * CHUNK, CHUNK), CHUNK)
        return pltpu.make_async_copy(tiles.at[span], buf.at[span], sems.at[ch])

    count = count_s[0]
    used = (count + CHUNK - 1) // CHUNK

    def ask(ch):
        @pl.when(ch < used)
        def _():
            tile_copy(ch).start()

    ahead = STEP // CHUNK
    for ch in range(ahead):
        ask(ch)

    lane = lax.broadcasted_iota(jnp.int32, (kvec, LANES), 1)
    low = lane < side
    zero = jnp.zeros((kvec, LANES), jnp.float32)

    for s in range(n_core):
        core = lax.rem(my_core + (n_core - s), n_core)
        for f in range(n_far):
            for p in range(own // LANES):
                x = gath[s][f, :, p * LANES:(p + 1) * LANES].astype(jnp.float32)
                y = pltpu.roll(x, side, 1)
                at = (f * n_core + core) * blk_own + p * per
                table[at] = jnp.where(low, x, y)
                table[at + 1] = jnp.where(low, y, x)
    n_blocks = n_far * n_core * blk_own
    table[n_blocks] = zero

    n_seg = acc[0].shape[0]
    width = n_chunk * SUB

    def clear(r, carry):
        for a in acc:
            a[r] = jnp.zeros(a.shape[1:], jnp.float32)
        return carry

    lax.fori_loop(0, n_seg, clear, 0)

    k_id = lax.broadcasted_iota(jnp.int32, (width, LANES), 0)
    n_id = lax.broadcasted_iota(jnp.int32, (width, LANES), 1)
    base_id = n_id - per * (k_id // SUB)
    for par in range(per):
        for jp in range(per):
            at = (par * per + jp) * width
            hit = (base_id == side * par + jp).astype(jnp.float32)
            select[at:at + width, :] = hit.astype(jnp.bfloat16)

    rows_of = per * kvec

    def product(base, half, x, check):
        xh = x[half * SUB:(half + 1) * SUB]
        w = jnp.concatenate(
            [xh[:, c * LANES:(c + 1) * LANES] for c in range(n_chunk)], axis=0
        ).astype(jnp.bfloat16)
        entries = []
        for t in range(SUB):
            slot = base + half * SUB + t
            at = cols_s[slot]
            entry = table[jnp.where(slot < count, at, n_blocks) if check else at]
            entries.append(jnp.where(low, entry, zero))
            entries.append(jnp.where(low, zero, entry))
        left = jnp.concatenate(entries, axis=0).astype(jnp.bfloat16)
        return lax.dot_general(left, w, NT, preferred_element_type=jnp.float32)

    lane_w = lax.broadcasted_iota(jnp.int32, (rows_of, width), 1) % SUB

    def accumulate(at, out):
        for t in range(SUB):
            r = rows_s[at + t]
            mine = jnp.where(lane_w == t, out[t * rows_of:(t + 1) * rows_of], 0.0)
            acc[t % len(acc)][r] += mine

    def step(first, slots_in, check):
        waiting = None
        for q in range(slots_in // (2 * SUB)):
            if q * 2 * SUB % CHUNK == 0:
                tile_copy(first // CHUNK + q * 2 * SUB // CHUNK).wait()
            base = pl.multiple_of(first + q * 2 * SUB, 2 * SUB)
            x = buf[pl.ds(base, 2 * SUB), :].astype(jnp.float32)
            for half in range(2):
                out = product(base, half, x, check)
                if waiting is not None:
                    accumulate(*waiting)
                waiting = (base + half * SUB, out)
        accumulate(*waiting)

    def full_step(i, carry):
        for ch in range(ahead):
            ask((i + 2) * ahead + ch)
        step(i * STEP, STEP, False)
        return carry

    def last_step(ch, carry):
        step(ch * CHUNK, CHUNK, True)
        return carry

    for ch in range(ahead, 2 * ahead):
        ask(ch)
    for copy in copies[:2]:
        copy.wait()
    full = count // STEP
    lax.fori_loop(0, full, full_step, 0)
    lax.fori_loop(full * (STEP // CHUNK), used, last_step, 0)

    pairs = n_seg // per

    def pick(m, carry):
        pieces = []
        for par in range(per):
            total = acc[0][m * per + par]
            for other in acc[1:]:
                total = total + other[m * per + par]
            for jp in range(per):
                pieces.append(total[jp * kvec:(jp + 1) * kvec])
        a = jnp.concatenate(pieces, axis=1)
        hi = a.astype(jnp.bfloat16).astype(jnp.float32)
        both = jnp.concatenate([hi, a - hi], axis=0).astype(jnp.bfloat16)
        picked[pl.ds(pl.multiple_of(m * 2 * kvec, 2 * kvec), 2 * kvec), :] = both
        return carry

    lax.fori_loop(0, pairs, pick, 0)

    spread = jnp.dot(picked[...], select[...], preferred_element_type=jnp.float32)
    for m in range(pairs):
        at = m * 2 * kvec
        row = spread[at:at + kvec] + spread[at + kvec:at + 2 * kvec]
        c, lane0 = divmod(m * LANES, own)
        part[c, :, lane0:lane0 + LANES] = row

    copies[2].wait()
    own_ref[...] = part[my_col] + ener[...] * gath[0][my_far].astype(jnp.float32)
    for s in range(1, n_col):
        share = part[lax.rem(my_col + s, n_col)]
        send_ref[s - 1] = share.astype(jnp.bfloat16)
        rest_ref[s - 1] = share


def tile_work(rows, cols, count, gath, n_col, ener, tiles):
    n_core = len(gath)
    n_far, kvec, own = gath[0].shape
    slots, area = tiles.shape
    side = math.isqrt(area)
    per = LANES // side
    blk_own = own // side
    n_seg = n_col * blk_own
    width = area // LANES * SUB
    vmem = pl.BlockSpec(memory_space=pltpu.VMEM)
    far_away = pl.BlockSpec(memory_space=pltpu.HBM)
    return pl.pallas_call(
        functools.partial(tile_kernel, n_core, n_col, side),
        out_shape=(
            jax.ShapeDtypeStruct((kvec, own), jnp.float32),
            jax.ShapeDtypeStruct((n_col - 1, kvec, own), jnp.bfloat16),
            jax.ShapeDtypeStruct((n_col - 1, kvec, own), jnp.float32),
        ),
        in_specs=[pl.BlockSpec(memory_space=pltpu.SMEM)] + [far_away] * 4 + [vmem] * n_core,
        out_specs=(vmem, vmem, vmem),
        scratch_shapes=[
            pltpu.SMEM((slots,), jnp.int32),
            pltpu.SMEM((slots,), jnp.int32),
            pltpu.VMEM((1, own), jnp.float32),
            pltpu.VMEM((slots, area), jnp.bfloat16),
            pltpu.VMEM((n_far * n_core * blk_own + 1, kvec, LANES), jnp.float32),
            pltpu.VMEM((n_seg // per * 2 * kvec, per * per * width), jnp.bfloat16),
            pltpu.VMEM((per * per * width, LANES), jnp.bfloat16),
            pltpu.VMEM((n_col, kvec, own), jnp.float32),
            pltpu.SemaphoreType.DMA((slots // CHUNK,)),
            pltpu.SemaphoreType.DMA((3,)),
        ] + [pltpu.VMEM((n_seg, per * kvec, width), jnp.float32)] * SUMS,
        compiler_params=pltpu.CompilerParams(vmem_limit_bytes=48 * 2**20),
        cost_estimate=pl.CostEstimate(
            flops=2 * slots * area * kvec, bytes_accessed=2 * slots * area, transcendentals=0
        ),
        name="tile_work",
    )(count, *[pltpu.with_memory_space_constraint(x, pltpu.HBM) for x in (rows, cols, ener, tiles)],
      *gath)


def terms_kernel(own, rest, vec, *refs):
    others, (terms_ref, wide) = refs[:-2], refs[-2:]
    n_col = len(others) + 1
    kvec = vec.shape[0]

    def outer(share, seg):
        return lax.dot_general(
            share, seg[...].astype(jnp.float32), NT,
            precision=lax.Precision.HIGHEST, preferred_element_type=jnp.float32,
        )

    terms = outer(own[...], vec)
    for s in range(1, n_col):
        terms = terms + outer(rest[s - 1], others[n_col - s - 1])
    wide[...] = jnp.zeros(wide.shape, jnp.float32)
    wide[:, :kvec] = terms
    spaced = pltpu.roll(wide[...], 0, 1, stride=kvec, stride_axis=0)
    terms_ref[...] = jnp.sum(spaced, axis=0, keepdims=True)


def gram_terms(own, rest, vectors, others):
    vmem = pl.BlockSpec(memory_space=pltpu.VMEM)
    return pl.pallas_call(
        terms_kernel,
        out_shape=jax.ShapeDtypeStruct((1, LANES), jnp.float32),
        in_specs=[vmem] * (3 + len(others)),
        out_specs=vmem,
        scratch_shapes=[pltpu.VMEM((vectors.shape[0], LANES), jnp.float32)],
        compiler_params=pltpu.CompilerParams(vmem_limit_bytes=4 * 2**20),
        name="gram_terms",
    )(own, rest, vectors, *others)


def finish_kernel(scale, base, gram_parts, vec, *refs):
    got, (product, residual) = refs[:-2], refs[-2:]
    whole = base[...]
    for piece in got:
        whole = whole + piece[...].astype(jnp.float32)
    product[...] = whole.astype(jnp.bfloat16)
    flat = gram_parts[0]
    for i in range(1, gram_parts.shape[0]):
        flat = flat + gram_parts[i]
    kvec = vec.shape[0]
    lane = lax.broadcasted_iota(jnp.int32, (kvec, LANES), 1)
    first = kvec * lax.broadcasted_iota(jnp.int32, (kvec, LANES), 0)
    wide = jnp.broadcast_to(flat * scale, (kvec, LANES))
    vec32 = vec[...].astype(jnp.float32)
    for a in range(kvec):
        column = jnp.sum(jnp.where(lane == first + a, wide, 0.0), axis=1, keepdims=True)
        whole = whole - column * vec32[a:a + 1, :]
    residual[...] = whole


def finish(scale, base, gram_parts, vectors, got):
    vmem = pl.BlockSpec(memory_space=pltpu.VMEM)
    return pl.pallas_call(
        functools.partial(finish_kernel, scale),
        out_shape=(
            jax.ShapeDtypeStruct(vectors.shape, jnp.bfloat16),
            jax.ShapeDtypeStruct(vectors.shape, jnp.float32),
        ),
        in_specs=[vmem] * (3 + len(got)),
        out_specs=(vmem, vmem),
        compiler_params=pltpu.CompilerParams(vmem_limit_bytes=4 * 2**20),
        name="finish",
    )(base, gram_parts, vectors, *got)


def from_all(x, axis):
    size = lax.axis_size(axis)
    got = [x]
    for s in range(1, size):
        got.append(lax.ppermute(x, axis, [(i, (i + s) % size) for i in range(size)]))
    return got


def per_device(vectors, energies, tiles, tile_rows, tile_cols, tile_count):
    kvec, own = vectors.shape
    n_col = lax.axis_size("col")
    copies = jnp.broadcast_to(vectors[None], (lax.axis_size("far"), kvec, own))
    gath = lax.all_to_all(copies, "far", 0, 0)
    gath = from_all(gath, "core")
    base, send, rest = tile_work(
        tile_rows, tile_cols, tile_count, gath, n_col, energies[None, :], tiles
    )
    got = [
        lax.ppermute(send[s - 1], "col", [(c, (c + s) % n_col) for c in range(n_col)])
        for s in range(1, n_col)
    ]
    others = from_all(vectors, "col")[1:]
    members = lax.axis_size(("far", "core", "col"))
    terms = gram_terms(base, rest, vectors, others)
    terms = jnp.broadcast_to(terms[None], (members,) + terms.shape)
    gram_parts = lax.all_to_all(terms, ("far", "core", "col"), 0, 0)
    return finish(1.0 / (members * own), base, gram_parts, vectors, got)


def solution(mesh):
    n_row, n_col = mesh.devices.shape
    n_core = 2 if n_row % 2 == 0 else 1
    split = ("far", "core", "col")
    chips = Mesh(mesh.devices.reshape(n_row // n_core, n_core, n_col), split)
    in_specs = (P(None, split), P(split), P(split, None), P(split), P(split), P(split))
    out_specs = (P(None, split), P(None, split))
    return jax.shard_map(
        per_device, mesh=chips, in_specs=in_specs, out_specs=out_specs, check_vma=False
    )
```

```python
import functools
import math

import jax
import jax.numpy as jnp
from jax import lax
from jax.experimental import pallas as pl
from jax.experimental.pallas import tpu as pltpu
from jax.sharding import Mesh, PartitionSpec as P

LANES = 128
SUB = 8
CHUNK = 128
STEP = 256
SUMS = 4

NT = (((1,), (1,)), ((), ()))


def tile_kernel(
    n_core, n_col, side, count_s, rows_h, cols_h, ener_h, tiles, *refs,
):
    gath, refs = refs[:n_core], refs[n_core:]
    (own_ref, send_ref, rest_ref, rows_s, cols_s, ener,
     buf, table, picked, select, part, sems, small, *acc) = refs
    n_far, kvec, own = gath[0].shape
    slots = tiles.shape[0]
    blk_own = own // side
    per = LANES // side
    n_chunk = tiles.shape[1] // LANES
    my_far, my_core, my_col = (lax.axis_index(name) for name in ("far", "core", "col"))

    copies = [
        pltpu.make_async_copy(src, dst, small.at[i])
        for i, (src, dst) in enumerate(
            ((cols_h, cols_s), (rows_h, rows_s), (ener_h, ener))
        )
    ]
    for copy in copies:
        copy.start()

    def tile_copy(ch):
        span = pl.ds(pl.multiple_of(ch * CHUNK, CHUNK), CHUNK)
        return pltpu.make_async_copy(tiles.at[span], buf.at[span], sems.at[ch])

    count = count_s[0]
    used = (count + CHUNK - 1) // CHUNK

    def ask(ch):
        @pl.when(ch < used)
        def _():
            tile_copy(ch).start()

    ahead = STEP // CHUNK
    for ch in range(ahead):
        ask(ch)

    lane = lax.broadcasted_iota(jnp.int32, (kvec, LANES), 1)
    low = lane < side
    zero = jnp.zeros((kvec, LANES), jnp.float32)

    for s in range(n_core):
        core = lax.rem(my_core + (n_core - s), n_core)
        for f in range(n_far):
            for p in range(own // LANES):
                x = gath[s][f, :, p * LANES:(p + 1) * LANES].astype(jnp.float32)
                y = pltpu.roll(x, side, 1)
                at = (f * n_core + core) * blk_own + p * per
                table[at] = jnp.where(low, x, y)
                table[at + 1] = jnp.where(low, y, x)
    n_blocks = n_far * n_core * blk_own
    table[n_blocks] = zero

    n_seg = acc[0].shape[0]
    width = n_chunk * SUB

    def clear(r, carry):
        for a in acc:
            a[r] = jnp.zeros(a.shape[1:], jnp.float32)
        return carry

    lax.fori_loop(0, n_seg, clear, 0)

    k_id = lax.broadcasted_iota(jnp.int32, (width, LANES), 0)
    n_id = lax.broadcasted_iota(jnp.int32, (width, LANES), 1)
    base_id = n_id - per * (k_id // SUB)
    for par in range(per):
        for jp in range(per):
            at = (par * per + jp) * width
            hit = (base_id == side * par + jp).astype(jnp.float32)
            select[at:at + width, :] = hit.astype(jnp.bfloat16)

    rows_of = per * kvec

    def product(base, half, x, check):
        xh = x[half * SUB:(half + 1) * SUB]
        w = jnp.concatenate(
            [xh[:, c * LANES:(c + 1) * LANES] for c in range(n_chunk)], axis=0
        ).astype(jnp.bfloat16)
        entries = []
        for t in range(SUB):
            slot = base + half * SUB + t
            at = cols_s[slot]
            entry = table[jnp.where(slot < count, at, n_blocks) if check else at]
            entries.append(jnp.where(low, entry, zero))
            entries.append(jnp.where(low, zero, entry))
        left = jnp.concatenate(entries, axis=0).astype(jnp.bfloat16)
        return jnp.dot(left, w.T, preferred_element_type=jnp.float32)

    lane_w = lax.broadcasted_iota(jnp.int32, (rows_of, width), 1) % SUB

    def accumulate(at, out):
        for t in range(SUB):
            r = rows_s[at + t]
            mine = jnp.where(lane_w == t, out[t * rows_of:(t + 1) * rows_of], 0.0)
            acc[t % len(acc)][r] += mine

    def step(first, slots_in, check):
        for i in range(slots_in // CHUNK):
            tile_copy(first // CHUNK + i).wait()
        waiting = None
        for q in range(slots_in // (2 * SUB)):
            base = pl.multiple_of(first + q * 2 * SUB, 2 * SUB)
            x = buf[pl.ds(base, 2 * SUB), :].astype(jnp.float32)
            for half in range(2):
                out = product(base, half, x, check)
                if waiting is not None:
                    accumulate(*waiting)
                waiting = (base + half * SUB, out)
        accumulate(*waiting)

    def full_step(i, carry):
        for ch in range(ahead):
            ask((i + 2) * ahead + ch)
        step(i * STEP, STEP, False)
        return carry

    def last_step(ch, carry):
        step(ch * CHUNK, CHUNK, True)
        return carry

    for ch in range(ahead, 2 * ahead):
        ask(ch)
    for copy in copies[:2]:
        copy.wait()
    full = count // STEP
    lax.fori_loop(0, full, full_step, 0)
    lax.fori_loop(full * (STEP // CHUNK), used, last_step, 0)

    pairs = n_seg // per

    def pick(m, carry):
        pieces = []
        for par in range(per):
            total = acc[0][m * per + par]
            for other in acc[1:]:
                total = total + other[m * per + par]
            for jp in range(per):
                pieces.append(total[jp * kvec:(jp + 1) * kvec])
        a = jnp.concatenate(pieces, axis=1)
        hi = a.astype(jnp.bfloat16).astype(jnp.float32)
        both = jnp.concatenate([hi, a - hi], axis=0).astype(jnp.bfloat16)
        picked[pl.ds(pl.multiple_of(m * 2 * kvec, 2 * kvec), 2 * kvec), :] = both
        return carry

    lax.fori_loop(0, pairs, pick, 0)

    spread = jnp.dot(picked[...], select[...], preferred_element_type=jnp.float32)
    for m in range(pairs):
        at = m * 2 * kvec
        row = spread[at:at + kvec] + spread[at + kvec:at + 2 * kvec]
        c, lane0 = divmod(m * LANES, own)
        part[c, :, lane0:lane0 + LANES] = row

    copies[2].wait()
    own_ref[...] = part[my_col] + ener[...] * gath[0][my_far].astype(jnp.float32)
    for s in range(1, n_col):
        share = part[lax.rem(my_col + s, n_col)]
        send_ref[s - 1] = share.astype(jnp.bfloat16)
        rest_ref[s - 1] = share


def tile_work(rows, cols, count, gath, n_col, ener, tiles):
    n_core = len(gath)
    n_far, kvec, own = gath[0].shape
    slots, area = tiles.shape
    side = math.isqrt(area)
    per = LANES // side
    blk_own = own // side
    n_seg = n_col * blk_own
    width = area // LANES * SUB
    vmem = pl.BlockSpec(memory_space=pltpu.VMEM)
    far_away = pl.BlockSpec(memory_space=pltpu.HBM)
    return pl.pallas_call(
        functools.partial(tile_kernel, n_core, n_col, side),
        out_shape=(
            jax.ShapeDtypeStruct((kvec, own), jnp.float32),
            jax.ShapeDtypeStruct((n_col - 1, kvec, own), jnp.bfloat16),
            jax.ShapeDtypeStruct((n_col - 1, kvec, own), jnp.float32),
        ),
        in_specs=[pl.BlockSpec(memory_space=pltpu.SMEM)] + [far_away] * 4 + [vmem] * n_core,
        out_specs=(vmem, vmem, vmem),
        scratch_shapes=[
            pltpu.SMEM((slots,), jnp.int32),
            pltpu.SMEM((slots,), jnp.int32),
            pltpu.VMEM((1, own), jnp.float32),
            pltpu.VMEM((slots, area), jnp.bfloat16),
            pltpu.VMEM((n_far * n_core * blk_own + 1, kvec, LANES), jnp.float32),
            pltpu.VMEM((n_seg // per * 2 * kvec, per * per * width), jnp.bfloat16),
            pltpu.VMEM((per * per * width, LANES), jnp.bfloat16),
            pltpu.VMEM((n_col, kvec, own), jnp.float32),
            pltpu.SemaphoreType.DMA((slots // CHUNK,)),
            pltpu.SemaphoreType.DMA((3,)),
        ] + [pltpu.VMEM((n_seg, per * kvec, width), jnp.float32)] * SUMS,
        compiler_params=pltpu.CompilerParams(vmem_limit_bytes=48 * 2**20),
        cost_estimate=pl.CostEstimate(
            flops=2 * slots * area * kvec, bytes_accessed=2 * slots * area, transcendentals=0
        ),
        name="tile_work",
    )(count, *[pltpu.with_memory_space_constraint(x, pltpu.HBM) for x in (rows, cols, ener, tiles)],
      *gath)


def terms_kernel(own, rest, vec, *refs):
    others, (terms_ref, wide) = refs[:-2], refs[-2:]
    n_col = len(others) + 1
    kvec = vec.shape[0]

    def outer(share, seg):
        return lax.dot_general(
            share, seg[...].astype(jnp.float32), NT,
            precision=lax.Precision.HIGHEST, preferred_element_type=jnp.float32,
        )

    terms = outer(own[...], vec)
    for s in range(1, n_col):
        terms = terms + outer(rest[s - 1], others[n_col - s - 1])
    wide[...] = jnp.zeros(wide.shape, jnp.float32)
    wide[:, :kvec] = terms
    spaced = pltpu.roll(wide[...], 0, 1, stride=kvec, stride_axis=0)
    terms_ref[...] = jnp.sum(spaced, axis=0, keepdims=True)


def gram_terms(own, rest, vectors, others):
    vmem = pl.BlockSpec(memory_space=pltpu.VMEM)
    return pl.pallas_call(
        terms_kernel,
        out_shape=jax.ShapeDtypeStruct((1, LANES), jnp.float32),
        in_specs=[vmem] * (3 + len(others)),
        out_specs=vmem,
        scratch_shapes=[pltpu.VMEM((vectors.shape[0], LANES), jnp.float32)],
        compiler_params=pltpu.CompilerParams(vmem_limit_bytes=4 * 2**20),
        name="gram_terms",
    )(own, rest, vectors, *others)


def finish_kernel(scale, base, gram_parts, vec, *refs):
    got, (product, residual) = refs[:-2], refs[-2:]
    whole = base[...]
    for piece in got:
        whole = whole + piece[...].astype(jnp.float32)
    product[...] = whole.astype(jnp.bfloat16)
    flat = gram_parts[0]
    for i in range(1, gram_parts.shape[0]):
        flat = flat + gram_parts[i]
    kvec = vec.shape[0]
    lane = lax.broadcasted_iota(jnp.int32, (kvec, LANES), 1)
    first = kvec * lax.broadcasted_iota(jnp.int32, (kvec, LANES), 0)
    wide = jnp.broadcast_to(flat * scale, (kvec, LANES))
    vec32 = vec[...].astype(jnp.float32)
    for a in range(kvec):
        column = jnp.sum(jnp.where(lane == first + a, wide, 0.0), axis=1, keepdims=True)
        whole = whole - column * vec32[a:a + 1, :]
    residual[...] = whole


def finish(scale, base, gram_parts, vectors, got):
    vmem = pl.BlockSpec(memory_space=pltpu.VMEM)
    return pl.pallas_call(
        functools.partial(finish_kernel, scale),
        out_shape=(
            jax.ShapeDtypeStruct(vectors.shape, jnp.bfloat16),
            jax.ShapeDtypeStruct(vectors.shape, jnp.float32),
        ),
        in_specs=[vmem] * (3 + len(got)),
        out_specs=(vmem, vmem),
        compiler_params=pltpu.CompilerParams(vmem_limit_bytes=4 * 2**20),
        name="finish",
    )(base, gram_parts, vectors, *got)


def from_all(x, axis):
    size = lax.axis_size(axis)
    got = [x]
    for s in range(1, size):
        got.append(lax.ppermute(x, axis, [(i, (i + s) % size) for i in range(size)]))
    return got


def per_device(vectors, energies, tiles, tile_rows, tile_cols, tile_count):
    kvec, own = vectors.shape
    n_col = lax.axis_size("col")
    copies = jnp.broadcast_to(vectors[None], (lax.axis_size("far"), kvec, own))
    gath = lax.all_to_all(copies, "far", 0, 0)
    gath = from_all(gath, "core")
    base, send, rest = tile_work(
        tile_rows, tile_cols, tile_count, gath, n_col, energies[None, :], tiles
    )
    got = [
        lax.ppermute(send[s - 1], "col", [(c, (c + s) % n_col) for c in range(n_col)])
        for s in range(1, n_col)
    ]
    others = from_all(vectors, "col")[1:]
    members = lax.axis_size(("far", "core", "col"))
    terms = gram_terms(base, rest, vectors, others)
    terms = jnp.broadcast_to(terms[None], (members,) + terms.shape)
    gram_parts = lax.all_to_all(terms, ("far", "core", "col"), 0, 0)
    return finish(1.0 / (members * own), base, gram_parts, vectors, got)


def solution(mesh):
    n_row, n_col = mesh.devices.shape
    n_core = 2 if n_row % 2 == 0 else 1
    split = ("far", "core", "col")
    chips = Mesh(mesh.devices.reshape(n_row // n_core, n_core, n_col), split)
    in_specs = (P(None, split), P(split), P(split, None), P(split), P(split), P(split))
    out_specs = (P(None, split), P(None, split))
    return jax.shard_map(
        per_device, mesh=chips, in_specs=in_specs, out_specs=out_specs, check_vma=False
    )
```

```python
import functools
import math

import jax
import jax.numpy as jnp
from jax import lax
from jax.experimental import pallas as pl
from jax.experimental.pallas import tpu as pltpu
from jax.sharding import Mesh, PartitionSpec as P

LANES = 128
SUB = 8
CHUNK = 128
STEP = 256
SUMS = 4

NT = (((1,), (1,)), ((), ()))


def tile_kernel(
    n_core, n_col, side, count_s, rows_h, cols_h, ener_h, tiles, *refs,
):
    gath, refs = refs[:n_core], refs[n_core:]
    (own_ref, send_ref, rest_ref, rows_s, cols_s, ener,
     buf, table, picked, select, part, sems, small, *acc) = refs
    n_far, kvec, own = gath[0].shape
    slots = tiles.shape[0]
    blk_own = own // side
    per = LANES // side
    n_chunk = tiles.shape[1] // LANES
    my_far, my_core, my_col = (lax.axis_index(name) for name in ("far", "core", "col"))

    copies = [
        pltpu.make_async_copy(src, dst, small.at[i])
        for i, (src, dst) in enumerate(
            ((cols_h, cols_s), (rows_h, rows_s), (ener_h, ener))
        )
    ]
    for copy in copies:
        copy.start()

    def tile_copy(ch):
        span = pl.ds(pl.multiple_of(ch * CHUNK, CHUNK), CHUNK)
        return pltpu.make_async_copy(tiles.at[span], buf.at[span], sems.at[ch])

    count = count_s[0]
    used = (count + CHUNK - 1) // CHUNK

    def ask(ch):
        @pl.when(ch < used)
        def _():
            tile_copy(ch).start()

    ahead = STEP // CHUNK
    for ch in range(ahead):
        ask(ch)

    lane = lax.broadcasted_iota(jnp.int32, (kvec, LANES), 1)
    low = lane < side
    zero = jnp.zeros((kvec, LANES), jnp.float32)

    for s in range(n_core):
        core = lax.rem(my_core + (n_core - s), n_core)
        for f in range(n_far):
            for p in range(own // LANES):
                x = gath[s][f, :, p * LANES:(p + 1) * LANES].astype(jnp.float32)
                y = pltpu.roll(x, side, 1)
                at = (f * n_core + core) * blk_own + p * per
                table[at] = jnp.where(low, x, y)
                table[at + 1] = jnp.where(low, y, x)
    n_blocks = n_far * n_core * blk_own
    table[n_blocks] = zero

    n_seg = acc[0].shape[0]
    width = n_chunk * SUB

    def clear(r, carry):
        for a in acc:
            a[r] = jnp.zeros(a.shape[1:], jnp.float32)
        return carry

    lax.fori_loop(0, n_seg, clear, 0)

    k_id = lax.broadcasted_iota(jnp.int32, (width, LANES), 0)
    n_id = lax.broadcasted_iota(jnp.int32, (width, LANES), 1)
    base_id = n_id - per * (k_id // SUB)
    for par in range(per):
        for jp in range(per):
            at = (par * per + jp) * width
            hit = (base_id == side * par + jp).astype(jnp.float32)
            select[at:at + width, :] = hit.astype(jnp.bfloat16)

    rows_of = per * kvec

    def product(base, half, x, check):
        xh = x[half * SUB:(half + 1) * SUB]
        w = jnp.concatenate(
            [xh[:, c * LANES:(c + 1) * LANES] for c in range(n_chunk)], axis=0
        ).astype(jnp.bfloat16)
        entries = []
        for t in range(SUB):
            slot = base + half * SUB + t
            at = cols_s[slot]
            entry = table[jnp.where(slot < count, at, n_blocks) if check else at]
            entries.append(jnp.where(low, entry, zero))
            entries.append(jnp.where(low, zero, entry))
        left = jnp.concatenate(entries, axis=0).astype(jnp.bfloat16)
        return jnp.dot(left, w.T, preferred_element_type=jnp.float32)

    lane_w = lax.broadcasted_iota(jnp.int32, (rows_of, width), 1) % SUB

    def accumulate(at, out):
        for t in range(SUB):
            r = rows_s[at + t]
            mine = jnp.where(lane_w == t, out[t * rows_of:(t + 1) * rows_of], 0.0)
            acc[t % len(acc)][r] += mine

    def step(first, slots_in, check):
        for i in range(slots_in // CHUNK):
            tile_copy(first // CHUNK + i).wait()
        waiting = None
        for q in range(slots_in // (2 * SUB)):
            base = pl.multiple_of(first + q * 2 * SUB, 2 * SUB)
            x = buf[pl.ds(base, 2 * SUB), :].astype(jnp.float32)
            for half in range(2):
                out = product(base, half, x, check)
                if waiting is not None:
                    accumulate(*waiting)
                waiting = (base + half * SUB, out)
        accumulate(*waiting)

    def full_step(i, carry):
        for ch in range(ahead):
            ask((i + 2) * ahead + ch)
        step(i * STEP, STEP, False)
        return carry

    def last_step(ch, carry):
        step(ch * CHUNK, CHUNK, True)
        return carry

    for ch in range(ahead, 2 * ahead):
        ask(ch)
    for copy in copies[:2]:
        copy.wait()
    full = count // STEP
    lax.fori_loop(0, full, full_step, 0)
    lax.fori_loop(full * (STEP // CHUNK), used, last_step, 0)

    pairs = n_seg // per

    def pick(m, carry):
        pieces = []
        for par in range(per):
            total = acc[0][m * per + par]
            for other in acc[1:]:
                total = total + other[m * per + par]
            for jp in range(per):
                pieces.append(total[jp * kvec:(jp + 1) * kvec])
        a = jnp.concatenate(pieces, axis=1)
        hi = a.astype(jnp.bfloat16).astype(jnp.float32)
        both = jnp.concatenate([hi, a - hi], axis=0).astype(jnp.bfloat16)
        picked[pl.ds(pl.multiple_of(m * 2 * kvec, 2 * kvec), 2 * kvec), :] = both
        return carry

    lax.fori_loop(0, pairs, pick, 0)

    spread = jnp.dot(picked[...], select[...], preferred_element_type=jnp.float32)
    for m in range(pairs):
        at = m * 2 * kvec
        row = spread[at:at + kvec] + spread[at + kvec:at + 2 * kvec]
        c, lane0 = divmod(m * LANES, own)
        part[c, :, lane0:lane0 + LANES] = row

    copies[2].wait()
    own_ref[...] = part[my_col] + ener[...] * gath[0][my_far].astype(jnp.float32)
    for s in range(1, n_col):
        share = part[lax.rem(my_col + s, n_col)]
        send_ref[s - 1] = share.astype(jnp.bfloat16)
        rest_ref[s - 1] = share


def tile_work(rows, cols, count, gath, n_col, ener, tiles):
    n_core = len(gath)
    n_far, kvec, own = gath[0].shape
    slots, area = tiles.shape
    side = math.isqrt(area)
    per = LANES // side
    blk_own = own // side
    n_seg = n_col * blk_own
    width = area // LANES * SUB
    vmem = pl.BlockSpec(memory_space=pltpu.VMEM)
    far_away = pl.BlockSpec(memory_space=pltpu.HBM)
    return pl.pallas_call(
        functools.partial(tile_kernel, n_core, n_col, side),
        out_shape=(
            jax.ShapeDtypeStruct((kvec, own), jnp.float32),
            jax.ShapeDtypeStruct((n_col - 1, kvec, own), jnp.bfloat16),
            jax.ShapeDtypeStruct((n_col - 1, kvec, own), jnp.float32),
        ),
        in_specs=[pl.BlockSpec(memory_space=pltpu.SMEM)] + [far_away] * 4 + [vmem] * n_core,
        out_specs=(vmem, vmem, vmem),
        scratch_shapes=[
            pltpu.SMEM((slots,), jnp.int32),
            pltpu.SMEM((slots,), jnp.int32),
            pltpu.VMEM((1, own), jnp.float32),
            pltpu.VMEM((slots, area), jnp.bfloat16),
            pltpu.VMEM((n_far * n_core * blk_own + 1, kvec, LANES), jnp.float32),
            pltpu.VMEM((n_seg // per * 2 * kvec, per * per * width), jnp.bfloat16),
            pltpu.VMEM((per * per * width, LANES), jnp.bfloat16),
            pltpu.VMEM((n_col, kvec, own), jnp.float32),
            pltpu.SemaphoreType.DMA((slots // CHUNK,)),
            pltpu.SemaphoreType.DMA((3,)),
        ] + [pltpu.VMEM((n_seg, per * kvec, width), jnp.float32)] * SUMS,
        compiler_params=pltpu.CompilerParams(vmem_limit_bytes=48 * 2**20),
        cost_estimate=pl.CostEstimate(
            flops=2 * slots * area * kvec, bytes_accessed=2 * slots * area, transcendentals=0
        ),
        name="tile_work",
    )(count, *[pltpu.with_memory_space_constraint(x, pltpu.HBM) for x in (rows, cols, ener, tiles)],
      *gath)


def terms_kernel(own, rest, vec, *refs):
    others, (terms_ref, wide) = refs[:-2], refs[-2:]
    n_col = len(others) + 1
    kvec = vec.shape[0]

    def outer(share, seg):
        return lax.dot_general(
            share, seg[...].astype(jnp.float32), NT,
            precision=lax.Precision.HIGHEST, preferred_element_type=jnp.float32,
        )

    terms = outer(own[...], vec)
    for s in range(1, n_col):
        terms = terms + outer(rest[s - 1], others[n_col - s - 1])
    wide[...] = jnp.zeros(wide.shape, jnp.float32)
    wide[:, :kvec] = terms
    spaced = pltpu.roll(wide[...], 0, 1, stride=kvec, stride_axis=0)
    terms_ref[...] = jnp.sum(spaced, axis=0, keepdims=True)


def gram_terms(own, rest, vectors, others):
    vmem = pl.BlockSpec(memory_space=pltpu.VMEM)
    return pl.pallas_call(
        terms_kernel,
        out_shape=jax.ShapeDtypeStruct((1, LANES), jnp.float32),
        in_specs=[vmem] * (3 + len(others)),
        out_specs=vmem,
        scratch_shapes=[pltpu.VMEM((vectors.shape[0], LANES), jnp.float32)],
        compiler_params=pltpu.CompilerParams(vmem_limit_bytes=4 * 2**20),
        name="gram_terms",
    )(own, rest, vectors, *others)


def finish_kernel(scale, base, gram_parts, vec, *refs):
    got, (product, residual) = refs[:-2], refs[-2:]
    whole = base[...]
    for piece in got:
        whole = whole + piece[...].astype(jnp.float32)
    product[...] = whole.astype(jnp.bfloat16)
    flat = gram_parts[0]
    for i in range(1, gram_parts.shape[0]):
        flat = flat + gram_parts[i]
    kvec = vec.shape[0]
    lane = lax.broadcasted_iota(jnp.int32, (kvec, LANES), 1)
    first = kvec * lax.broadcasted_iota(jnp.int32, (kvec, LANES), 0)
    wide = jnp.broadcast_to(flat * scale, (kvec, LANES))
    vec32 = vec[...].astype(jnp.float32)
    for a in range(kvec):
        column = jnp.sum(jnp.where(lane == first + a, wide, 0.0), axis=1, keepdims=True)
        whole = whole - column * vec32[a:a + 1, :]
    residual[...] = whole


def finish(scale, base, gram_parts, vectors, got):
    vmem = pl.BlockSpec(memory_space=pltpu.VMEM)
    return pl.pallas_call(
        functools.partial(finish_kernel, scale),
        out_shape=(
            jax.ShapeDtypeStruct(vectors.shape, jnp.bfloat16),
            jax.ShapeDtypeStruct(vectors.shape, jnp.float32),
        ),
        in_specs=[vmem] * (3 + len(got)),
        out_specs=(vmem, vmem),
        compiler_params=pltpu.CompilerParams(vmem_limit_bytes=4 * 2**20),
        name="finish",
    )(base, gram_parts, vectors, *got)


def from_all(x, axis):
    size = lax.axis_size(axis)
    got = [x]
    for s in range(1, size):
        got.append(lax.ppermute(x, axis, [(i, (i + s) % size) for i in range(size)]))
    return got


def per_device(vectors, energies, tiles, tile_rows, tile_cols, tile_count):
    kvec, own = vectors.shape
    n_col = lax.axis_size("col")
    copies = jnp.broadcast_to(vectors[None], (lax.axis_size("far"), kvec, own))
    gath = lax.all_to_all(copies, "far", 0, 0)
    gath = from_all(gath, "core")
    late, gath[-1] = lax.optimization_barrier((vectors, gath[-1]))
    others = from_all(late, "col")[1:]
    base, send, rest = tile_work(
        tile_rows, tile_cols, tile_count, gath, n_col, energies[None, :], tiles
    )
    got = [
        lax.ppermute(send[s - 1], "col", [(c, (c + s) % n_col) for c in range(n_col)])
        for s in range(1, n_col)
    ]
    members = lax.axis_size(("far", "core", "col"))
    terms = gram_terms(base, rest, vectors, others)
    terms = jnp.broadcast_to(terms[None], (members,) + terms.shape)
    gram_parts = lax.all_to_all(terms, ("far", "core", "col"), 0, 0)
    return finish(1.0 / (members * own), base, gram_parts, vectors, got)


def solution(mesh):
    n_row, n_col = mesh.devices.shape
    n_core = 2 if n_row % 2 == 0 else 1
    split = ("far", "core", "col")
    chips = Mesh(mesh.devices.reshape(n_row // n_core, n_core, n_col), split)
    in_specs = (P(None, split), P(split), P(split, None), P(split), P(split), P(split))
    out_specs = (P(None, split), P(None, split))
    return jax.shard_map(
        per_device, mesh=chips, in_specs=in_specs, out_specs=out_specs, check_vma=False
    )
```

```python
import functools
import math

import jax
import jax.numpy as jnp
from jax import lax
from jax.experimental import pallas as pl
from jax.experimental.pallas import tpu as pltpu
from jax.sharding import Mesh, PartitionSpec as P

LANES = 128
SUB = 8
CHUNK = 128
STEP = 256
SUMS = 4

NT = (((1,), (1,)), ((), ()))


def tile_kernel(
    n_core, n_col, side, count_s, rows_h, cols_h, ener_h, tiles, *refs,
):
    gath, refs = refs[:n_core], refs[n_core:]
    (own_ref, send_ref, rest_ref, rows_s, cols_s, ener,
     buf, table, picked, select, part, sems, small, *acc) = refs
    n_far, kvec, own = gath[0].shape
    slots = tiles.shape[0]
    blk_own = own // side
    per = LANES // side
    n_chunk = tiles.shape[1] // LANES
    my_far, my_core, my_col = (lax.axis_index(name) for name in ("far", "core", "col"))

    copies = [
        pltpu.make_async_copy(src, dst, small.at[i])
        for i, (src, dst) in enumerate(
            ((cols_h, cols_s), (rows_h, rows_s), (ener_h, ener))
        )
    ]
    for copy in copies:
        copy.start()

    def tile_copy(ch):
        span = pl.ds(pl.multiple_of(ch * CHUNK, CHUNK), CHUNK)
        return pltpu.make_async_copy(tiles.at[span], buf.at[span], sems.at[ch])

    count = count_s[0]
    used = (count + CHUNK - 1) // CHUNK

    def ask(ch):
        @pl.when(ch < used)
        def _():
            tile_copy(ch).start()

    ahead = STEP // CHUNK
    for ch in range(ahead):
        ask(ch)

    lane = lax.broadcasted_iota(jnp.int32, (kvec, LANES), 1)
    low = lane < side
    zero = jnp.zeros((kvec, LANES), jnp.float32)

    for s in range(n_core):
        core = lax.rem(my_core + (n_core - s), n_core)
        for f in range(n_far):
            for p in range(own // LANES):
                x = gath[s][f, :, p * LANES:(p + 1) * LANES].astype(jnp.float32)
                y = pltpu.roll(x, side, 1)
                at = (f * n_core + core) * blk_own + p * per
                table[at] = jnp.where(low, x, y)
                table[at + 1] = jnp.where(low, y, x)
    n_blocks = n_far * n_core * blk_own
    table[n_blocks] = zero

    n_seg = acc[0].shape[0]
    width = n_chunk * SUB

    def clear(r, carry):
        for a in acc:
            a[r] = jnp.zeros(a.shape[1:], jnp.float32)
        return carry

    lax.fori_loop(0, n_seg, clear, 0)

    k_id = lax.broadcasted_iota(jnp.int32, (width, LANES), 0)
    n_id = lax.broadcasted_iota(jnp.int32, (width, LANES), 1)
    base_id = n_id - per * (k_id // SUB)
    for par in range(per):
        for jp in range(per):
            at = (par * per + jp) * width
            hit = (base_id == side * par + jp).astype(jnp.float32)
            select[at:at + width, :] = hit.astype(jnp.bfloat16)

    rows_of = per * kvec

    def product(base, half, x, check):
        xh = x[half * SUB:(half + 1) * SUB]
        w = jnp.concatenate(
            [xh[:, c * LANES:(c + 1) * LANES] for c in range(n_chunk)], axis=0
        ).astype(jnp.bfloat16)
        entries = []
        for t in range(SUB):
            slot = base + half * SUB + t
            at = cols_s[slot]
            entry = table[jnp.where(slot < count, at, n_blocks) if check else at]
            entries.append(jnp.where(low, entry, zero))
            entries.append(jnp.where(low, zero, entry))
        left = jnp.concatenate(entries, axis=0).astype(jnp.bfloat16)
        return jnp.dot(left, w.T, preferred_element_type=jnp.float32)

    lane_w = lax.broadcasted_iota(jnp.int32, (rows_of, width), 1) % SUB

    def accumulate(at, out):
        for t in range(SUB):
            r = rows_s[at + t]
            mine = jnp.where(lane_w == t, out[t * rows_of:(t + 1) * rows_of], 0.0)
            acc[t % len(acc)][r] += mine

    def step(first, slots_in, check):
        for i in range(slots_in // CHUNK):
            tile_copy(first // CHUNK + i).wait()
        waiting = None
        for q in range(slots_in // (2 * SUB)):
            base = pl.multiple_of(first + q * 2 * SUB, 2 * SUB)
            x = buf[pl.ds(base, 2 * SUB), :].astype(jnp.float32)
            for half in range(2):
                out = product(base, half, x, check)
                if waiting is not None:
                    accumulate(*waiting)
                waiting = (base + half * SUB, out)
        accumulate(*waiting)

    def full_step(i, carry):
        for ch in range(ahead):
            ask(1 + (i + 2) * ahead + ch)
        step(CHUNK + i * STEP, STEP, False)
        return carry

    def last_step(ch, carry):
        step(ch * CHUNK, CHUNK, True)
        return carry

    for ch in range(ahead, 1 + 2 * ahead):
        ask(ch)
    for copy in copies[:2]:
        copy.wait()
    head = (count >= CHUNK).astype(jnp.int32)

    @pl.when(head == 1)
    def _():
        step(0, CHUNK, False)

    full = jnp.maximum(count - CHUNK, 0) // STEP
    lax.fori_loop(0, full, full_step, 0)
    lax.fori_loop(head + full * ahead, used, last_step, 0)

    pairs = n_seg // per

    def pick(m, carry):
        pieces = []
        for par in range(per):
            total = acc[0][m * per + par]
            for other in acc[1:]:
                total = total + other[m * per + par]
            for jp in range(per):
                pieces.append(total[jp * kvec:(jp + 1) * kvec])
        a = jnp.concatenate(pieces, axis=1)
        hi = a.astype(jnp.bfloat16).astype(jnp.float32)
        both = jnp.concatenate([hi, a - hi], axis=0).astype(jnp.bfloat16)
        picked[pl.ds(pl.multiple_of(m * 2 * kvec, 2 * kvec), 2 * kvec), :] = both
        return carry

    lax.fori_loop(0, pairs, pick, 0)

    spread = jnp.dot(picked[...], select[...], preferred_element_type=jnp.float32)
    for m in range(pairs):
        at = m * 2 * kvec
        row = spread[at:at + kvec] + spread[at + kvec:at + 2 * kvec]
        c, lane0 = divmod(m * LANES, own)
        part[c, :, lane0:lane0 + LANES] = row

    copies[2].wait()
    own_ref[...] = part[my_col] + ener[...] * gath[0][my_far].astype(jnp.float32)
    for s in range(1, n_col):
        share = part[lax.rem(my_col + s, n_col)]
        send_ref[s - 1] = share.astype(jnp.bfloat16)
        rest_ref[s - 1] = share


def tile_work(rows, cols, count, gath, n_col, ener, tiles):
    n_core = len(gath)
    n_far, kvec, own = gath[0].shape
    slots, area = tiles.shape
    side = math.isqrt(area)
    per = LANES // side
    blk_own = own // side
    n_seg = n_col * blk_own
    width = area // LANES * SUB
    vmem = pl.BlockSpec(memory_space=pltpu.VMEM)
    far_away = pl.BlockSpec(memory_space=pltpu.HBM)
    return pl.pallas_call(
        functools.partial(tile_kernel, n_core, n_col, side),
        out_shape=(
            jax.ShapeDtypeStruct((kvec, own), jnp.float32),
            jax.ShapeDtypeStruct((n_col - 1, kvec, own), jnp.bfloat16),
            jax.ShapeDtypeStruct((n_col - 1, kvec, own), jnp.float32),
        ),
        in_specs=[pl.BlockSpec(memory_space=pltpu.SMEM)] + [far_away] * 4 + [vmem] * n_core,
        out_specs=(vmem, vmem, vmem),
        scratch_shapes=[
            pltpu.SMEM((slots,), jnp.int32),
            pltpu.SMEM((slots,), jnp.int32),
            pltpu.VMEM((1, own), jnp.float32),
            pltpu.VMEM((slots, area), jnp.bfloat16),
            pltpu.VMEM((n_far * n_core * blk_own + 1, kvec, LANES), jnp.float32),
            pltpu.VMEM((n_seg // per * 2 * kvec, per * per * width), jnp.bfloat16),
            pltpu.VMEM((per * per * width, LANES), jnp.bfloat16),
            pltpu.VMEM((n_col, kvec, own), jnp.float32),
            pltpu.SemaphoreType.DMA((slots // CHUNK,)),
            pltpu.SemaphoreType.DMA((3,)),
        ] + [pltpu.VMEM((n_seg, per * kvec, width), jnp.float32)] * SUMS,
        compiler_params=pltpu.CompilerParams(vmem_limit_bytes=48 * 2**20),
        cost_estimate=pl.CostEstimate(
            flops=2 * slots * area * kvec, bytes_accessed=2 * slots * area, transcendentals=0
        ),
        name="tile_work",
    )(count, *[pltpu.with_memory_space_constraint(x, pltpu.HBM) for x in (rows, cols, ener, tiles)],
      *gath)


def terms_kernel(own, rest, vec, *refs):
    others, (terms_ref, wide) = refs[:-2], refs[-2:]
    n_col = len(others) + 1
    kvec = vec.shape[0]

    def outer(share, seg):
        return lax.dot_general(
            share, seg[...].astype(jnp.float32), NT,
            precision=lax.Precision.HIGHEST, preferred_element_type=jnp.float32,
        )

    terms = outer(own[...], vec)
    for s in range(1, n_col):
        terms = terms + outer(rest[s - 1], others[n_col - s - 1])
    wide[...] = jnp.zeros(wide.shape, jnp.float32)
    wide[:, :kvec] = terms
    spaced = pltpu.roll(wide[...], 0, 1, stride=kvec, stride_axis=0)
    terms_ref[...] = jnp.sum(spaced, axis=0, keepdims=True)


def gram_terms(own, rest, vectors, others):
    vmem = pl.BlockSpec(memory_space=pltpu.VMEM)
    return pl.pallas_call(
        terms_kernel,
        out_shape=jax.ShapeDtypeStruct((1, LANES), jnp.float32),
        in_specs=[vmem] * (3 + len(others)),
        out_specs=vmem,
        scratch_shapes=[pltpu.VMEM((vectors.shape[0], LANES), jnp.float32)],
        compiler_params=pltpu.CompilerParams(vmem_limit_bytes=4 * 2**20),
        name="gram_terms",
    )(own, rest, vectors, *others)


def finish_kernel(scale, base, gram_parts, vec, *refs):
    got, (product, residual) = refs[:-2], refs[-2:]
    whole = base[...]
    for piece in got:
        whole = whole + piece[...].astype(jnp.float32)
    product[...] = whole.astype(jnp.bfloat16)
    flat = gram_parts[0]
    for i in range(1, gram_parts.shape[0]):
        flat = flat + gram_parts[i]
    kvec = vec.shape[0]
    lane = lax.broadcasted_iota(jnp.int32, (kvec, LANES), 1)
    first = kvec * lax.broadcasted_iota(jnp.int32, (kvec, LANES), 0)
    wide = jnp.broadcast_to(flat * scale, (kvec, LANES))
    vec32 = vec[...].astype(jnp.float32)
    for a in range(kvec):
        column = jnp.sum(jnp.where(lane == first + a, wide, 0.0), axis=1, keepdims=True)
        whole = whole - column * vec32[a:a + 1, :]
    residual[...] = whole


def finish(scale, base, gram_parts, vectors, got):
    vmem = pl.BlockSpec(memory_space=pltpu.VMEM)
    return pl.pallas_call(
        functools.partial(finish_kernel, scale),
        out_shape=(
            jax.ShapeDtypeStruct(vectors.shape, jnp.bfloat16),
            jax.ShapeDtypeStruct(vectors.shape, jnp.float32),
        ),
        in_specs=[vmem] * (3 + len(got)),
        out_specs=(vmem, vmem),
        compiler_params=pltpu.CompilerParams(vmem_limit_bytes=4 * 2**20),
        name="finish",
    )(base, gram_parts, vectors, *got)


def from_all(x, axis):
    size = lax.axis_size(axis)
    got = [x]
    for s in range(1, size):
        got.append(lax.ppermute(x, axis, [(i, (i + s) % size) for i in range(size)]))
    return got


def per_device(vectors, energies, tiles, tile_rows, tile_cols, tile_count):
    kvec, own = vectors.shape
    n_col = lax.axis_size("col")
    copies = jnp.broadcast_to(vectors[None], (lax.axis_size("far"), kvec, own))
    gath = lax.all_to_all(copies, "far", 0, 0)
    gath = from_all(gath, "core")
    base, send, rest = tile_work(
        tile_rows, tile_cols, tile_count, gath, n_col, energies[None, :], tiles
    )
    got = [
        lax.ppermute(send[s - 1], "col", [(c, (c + s) % n_col) for c in range(n_col)])
        for s in range(1, n_col)
    ]
    others = from_all(vectors, "col")[1:]
    members = lax.axis_size(("far", "core", "col"))
    terms = gram_terms(base, rest, vectors, others)
    terms = jnp.broadcast_to(terms[None], (members,) + terms.shape)
    gram_parts = lax.all_to_all(terms, ("far", "core", "col"), 0, 0)
    return finish(1.0 / (members * own), base, gram_parts, vectors, got)


def solution(mesh):
    n_row, n_col = mesh.devices.shape
    n_core = 2 if n_row % 2 == 0 else 1
    split = ("far", "core", "col")
    chips = Mesh(mesh.devices.reshape(n_row // n_core, n_core, n_col), split)
    in_specs = (P(None, split), P(split), P(split, None), P(split), P(split), P(split))
    out_specs = (P(None, split), P(None, split))
    return jax.shard_map(
        per_device, mesh=chips, in_specs=in_specs, out_specs=out_specs, check_vma=False
    )
```

```python
import functools
import math

import jax
import jax.numpy as jnp
from jax import lax
from jax.experimental import pallas as pl
from jax.experimental.pallas import tpu as pltpu
from jax.sharding import Mesh, PartitionSpec as P

LANES = 128
SUB = 8
CHUNK = 128
STEP = 256
SUMS = 4

NT = (((1,), (1,)), ((), ()))


def tile_kernel(
    n_core, n_col, side, count_s, rows_h, cols_h, ener_h, tiles, *refs,
):
    gath, refs = refs[:n_core], refs[n_core:]
    (own_ref, send_ref, rest_ref, rows_s, cols_s, ener,
     buf, table, picked, select, part, sems, small, *acc) = refs
    n_far, kvec, own = gath[0].shape
    slots = tiles.shape[0]
    blk_own = own // side
    per = LANES // side
    n_chunk = tiles.shape[1] // LANES
    my_far, my_core, my_col = (lax.axis_index(name) for name in ("far", "core", "col"))

    copies = [
        pltpu.make_async_copy(src, dst, small.at[i])
        for i, (src, dst) in enumerate(
            ((cols_h, cols_s), (rows_h, rows_s), (ener_h, ener))
        )
    ]
    for copy in copies:
        copy.start()

    def tile_copy(ch):
        span = pl.ds(pl.multiple_of(ch * CHUNK, CHUNK), CHUNK)
        return pltpu.make_async_copy(tiles.at[span], buf.at[span], sems.at[ch])

    count = count_s[0]
    used = (count + CHUNK - 1) // CHUNK

    def ask(ch):
        @pl.when(ch < used)
        def _():
            tile_copy(ch).start()

    ahead = STEP // CHUNK
    for ch in range(ahead):
        ask(ch)

    lane = lax.broadcasted_iota(jnp.int32, (kvec, LANES), 1)
    low = lane < side
    zero = jnp.zeros((kvec, LANES), jnp.float32)

    for s in range(n_core):
        core = lax.rem(my_core + (n_core - s), n_core)
        for f in range(n_far):
            for p in range(own // LANES):
                x = gath[s][f, :, p * LANES:(p + 1) * LANES].astype(jnp.float32)
                y = pltpu.roll(x, side, 1)
                at = (f * n_core + core) * blk_own + p * per
                table[at] = jnp.where(low, x, y)
                table[at + 1] = jnp.where(low, y, x)
    n_blocks = n_far * n_core * blk_own
    table[n_blocks] = zero

    n_seg = acc[0].shape[0]
    width = n_chunk * SUB

    def clear(r, carry):
        for a in acc:
            a[r] = jnp.zeros(a.shape[1:], jnp.float32)
        return carry

    lax.fori_loop(0, n_seg, clear, 0)

    k_id = lax.broadcasted_iota(jnp.int32, (width, LANES), 0)
    n_id = lax.broadcasted_iota(jnp.int32, (width, LANES), 1)
    base_id = n_id - per * (k_id // SUB)
    for par in range(per):
        for jp in range(per):
            at = (par * per + jp) * width
            hit = (base_id == side * par + jp).astype(jnp.float32)
            select[at:at + width, :] = hit.astype(jnp.bfloat16)

    rows_of = per * kvec

    def product(base, half, x, check):
        xh = x[half * SUB:(half + 1) * SUB]
        w = jnp.concatenate([xh[:, c * LANES:(c + 1) * LANES] for c in range(n_chunk)], axis=0)
        entries = []
        for t in range(SUB):
            slot = base + half * SUB + t
            at = cols_s[slot]
            entry = table[jnp.where(slot < count, at, n_blocks) if check else at]
            entries.append(jnp.where(low, entry, zero))
            entries.append(jnp.where(low, zero, entry))
        left = jnp.concatenate(entries, axis=0).astype(jnp.bfloat16)
        return jnp.dot(left, w.T, preferred_element_type=jnp.float32)

    lane_w = lax.broadcasted_iota(jnp.int32, (rows_of, width), 1) % SUB

    def accumulate(at, out):
        for t in range(SUB):
            r = rows_s[at + t]
            mine = jnp.where(lane_w == t, out[t * rows_of:(t + 1) * rows_of], 0.0)
            acc[t % len(acc)][r] += mine

    def step(first, slots_in, check):
        for i in range(slots_in // CHUNK):
            tile_copy(first // CHUNK + i).wait()
        waiting = None
        for q in range(slots_in // (2 * SUB)):
            base = pl.multiple_of(first + q * 2 * SUB, 2 * SUB)
            x = buf[pl.ds(base, 2 * SUB), :]
            for half in range(2):
                out = product(base, half, x, check)
                if waiting is not None:
                    accumulate(*waiting)
                waiting = (base + half * SUB, out)
        accumulate(*waiting)

    def full_step(i, carry):
        for ch in range(ahead):
            ask(1 + (i + 2) * ahead + ch)
        step(CHUNK + i * STEP, STEP, False)
        return carry

    def last_step(ch, carry):
        step(ch * CHUNK, CHUNK, True)
        return carry

    for ch in range(ahead, 1 + 2 * ahead):
        ask(ch)
    for copy in copies[:2]:
        copy.wait()
    head = (count >= CHUNK).astype(jnp.int32)

    @pl.when(head == 1)
    def _():
        step(0, CHUNK, False)

    full = jnp.maximum(count - CHUNK, 0) // STEP
    lax.fori_loop(0, full, full_step, 0)
    lax.fori_loop(head + full * ahead, used, last_step, 0)

    pairs = n_seg // per

    def pick(m, carry):
        pieces = []
        for par in range(per):
            total = acc[0][m * per + par]
            for other in acc[1:]:
                total = total + other[m * per + par]
            for jp in range(per):
                pieces.append(total[jp * kvec:(jp + 1) * kvec])
        a = jnp.concatenate(pieces, axis=1)
        hi = a.astype(jnp.bfloat16).astype(jnp.float32)
        both = jnp.concatenate([hi, a - hi], axis=0).astype(jnp.bfloat16)
        picked[pl.ds(pl.multiple_of(m * 2 * kvec, 2 * kvec), 2 * kvec), :] = both
        return carry

    lax.fori_loop(0, pairs, pick, 0)

    spread = jnp.dot(picked[...], select[...], preferred_element_type=jnp.float32)
    for m in range(pairs):
        at = m * 2 * kvec
        row = spread[at:at + kvec] + spread[at + kvec:at + 2 * kvec]
        c, lane0 = divmod(m * LANES, own)
        part[c, :, lane0:lane0 + LANES] = row

    copies[2].wait()
    own_ref[...] = part[my_col] + ener[...] * gath[0][my_far].astype(jnp.float32)
    for s in range(1, n_col):
        share = part[lax.rem(my_col + s, n_col)]
        send_ref[s - 1] = share.astype(jnp.bfloat16)
        rest_ref[s - 1] = share


def tile_work(rows, cols, count, gath, n_col, ener, tiles):
    n_core = len(gath)
    n_far, kvec, own = gath[0].shape
    slots, area = tiles.shape
    side = math.isqrt(area)
    per = LANES // side
    blk_own = own // side
    n_seg = n_col * blk_own
    width = area // LANES * SUB
    vmem = pl.BlockSpec(memory_space=pltpu.VMEM)
    far_away = pl.BlockSpec(memory_space=pltpu.HBM)
    return pl.pallas_call(
        functools.partial(tile_kernel, n_core, n_col, side),
        out_shape=(
            jax.ShapeDtypeStruct((kvec, own), jnp.float32),
            jax.ShapeDtypeStruct((n_col - 1, kvec, own), jnp.bfloat16),
            jax.ShapeDtypeStruct((n_col - 1, kvec, own), jnp.float32),
        ),
        in_specs=[pl.BlockSpec(memory_space=pltpu.SMEM)] + [far_away] * 4 + [vmem] * n_core,
        out_specs=(vmem, vmem, vmem),
        scratch_shapes=[
            pltpu.SMEM((slots,), jnp.int32),
            pltpu.SMEM((slots,), jnp.int32),
            pltpu.VMEM((1, own), jnp.float32),
            pltpu.VMEM((slots, area), jnp.bfloat16),
            pltpu.VMEM((n_far * n_core * blk_own + 1, kvec, LANES), jnp.float32),
            pltpu.VMEM((n_seg // per * 2 * kvec, per * per * width), jnp.bfloat16),
            pltpu.VMEM((per * per * width, LANES), jnp.bfloat16),
            pltpu.VMEM((n_col, kvec, own), jnp.float32),
            pltpu.SemaphoreType.DMA((slots // CHUNK,)),
            pltpu.SemaphoreType.DMA((3,)),
        ] + [pltpu.VMEM((n_seg, per * kvec, width), jnp.float32)] * SUMS,
        compiler_params=pltpu.CompilerParams(vmem_limit_bytes=48 * 2**20),
        cost_estimate=pl.CostEstimate(
            flops=2 * slots * area * kvec, bytes_accessed=2 * slots * area, transcendentals=0
        ),
        name="tile_work",
    )(count, *[pltpu.with_memory_space_constraint(x, pltpu.HBM) for x in (rows, cols, ener, tiles)],
      *gath)


def terms_kernel(own, rest, vec, *refs):
    others, (terms_ref, wide) = refs[:-2], refs[-2:]
    n_col = len(others) + 1
    kvec = vec.shape[0]

    def outer(share, seg):
        return lax.dot_general(
            share, seg[...].astype(jnp.float32), NT,
            precision=lax.Precision.HIGHEST, preferred_element_type=jnp.float32,
        )

    terms = outer(own[...], vec)
    for s in range(1, n_col):
        terms = terms + outer(rest[s - 1], others[n_col - s - 1])
    wide[...] = jnp.zeros(wide.shape, jnp.float32)
    wide[:, :kvec] = terms
    spaced = pltpu.roll(wide[...], 0, 1, stride=kvec, stride_axis=0)
    terms_ref[...] = jnp.sum(spaced, axis=0, keepdims=True)


def gram_terms(own, rest, vectors, others):
    vmem = pl.BlockSpec(memory_space=pltpu.VMEM)
    return pl.pallas_call(
        terms_kernel,
        out_shape=jax.ShapeDtypeStruct((1, LANES), jnp.float32),
        in_specs=[vmem] * (3 + len(others)),
        out_specs=vmem,
        scratch_shapes=[pltpu.VMEM((vectors.shape[0], LANES), jnp.float32)],
        compiler_params=pltpu.CompilerParams(vmem_limit_bytes=4 * 2**20),
        name="gram_terms",
    )(own, rest, vectors, *others)


def finish_kernel(scale, base, gram_parts, vec, *refs):
    got, (product, residual) = refs[:-2], refs[-2:]
    whole = base[...]
    for piece in got:
        whole = whole + piece[...].astype(jnp.float32)
    product[...] = whole.astype(jnp.bfloat16)
    flat = gram_parts[0]
    for i in range(1, gram_parts.shape[0]):
        flat = flat + gram_parts[i]
    kvec = vec.shape[0]
    lane = lax.broadcasted_iota(jnp.int32, (kvec, LANES), 1)
    first = kvec * lax.broadcasted_iota(jnp.int32, (kvec, LANES), 0)
    wide = jnp.broadcast_to(flat * scale, (kvec, LANES))
    vec32 = vec[...].astype(jnp.float32)
    for a in range(kvec):
        column = jnp.sum(jnp.where(lane == first + a, wide, 0.0), axis=1, keepdims=True)
        whole = whole - column * vec32[a:a + 1, :]
    residual[...] = whole


def finish(scale, base, gram_parts, vectors, got):
    vmem = pl.BlockSpec(memory_space=pltpu.VMEM)
    return pl.pallas_call(
        functools.partial(finish_kernel, scale),
        out_shape=(
            jax.ShapeDtypeStruct(vectors.shape, jnp.bfloat16),
            jax.ShapeDtypeStruct(vectors.shape, jnp.float32),
        ),
        in_specs=[vmem] * (3 + len(got)),
        out_specs=(vmem, vmem),
        compiler_params=pltpu.CompilerParams(vmem_limit_bytes=4 * 2**20),
        name="finish",
    )(base, gram_parts, vectors, *got)


def from_all(x, axis):
    size = lax.axis_size(axis)
    got = [x]
    for s in range(1, size):
        got.append(lax.ppermute(x, axis, [(i, (i + s) % size) for i in range(size)]))
    return got


def per_device(vectors, energies, tiles, tile_rows, tile_cols, tile_count):
    kvec, own = vectors.shape
    n_col = lax.axis_size("col")
    copies = jnp.broadcast_to(vectors[None], (lax.axis_size("far"), kvec, own))
    gath = lax.all_to_all(copies, "far", 0, 0)
    gath = from_all(gath, "core")
    base, send, rest = tile_work(
        tile_rows, tile_cols, tile_count, gath, n_col, energies[None, :], tiles
    )
    got = [
        lax.ppermute(send[s - 1], "col", [(c, (c + s) % n_col) for c in range(n_col)])
        for s in range(1, n_col)
    ]
    others = from_all(vectors, "col")[1:]
    members = lax.axis_size(("far", "core", "col"))
    terms = gram_terms(base, rest, vectors, others)
    terms = jnp.broadcast_to(terms[None], (members,) + terms.shape)
    gram_parts = lax.all_to_all(terms, ("far", "core", "col"), 0, 0)
    return finish(1.0 / (members * own), base, gram_parts, vectors, got)


def solution(mesh):
    n_row, n_col = mesh.devices.shape
    n_core = 2 if n_row % 2 == 0 else 1
    split = ("far", "core", "col")
    chips = Mesh(mesh.devices.reshape(n_row // n_core, n_core, n_col), split)
    in_specs = (P(None, split), P(split), P(split, None), P(split), P(split), P(split))
    out_specs = (P(None, split), P(None, split))
    return jax.shard_map(
        per_device, mesh=chips, in_specs=in_specs, out_specs=out_specs, check_vma=False
    )
```

```python
import functools
import math

import jax
import jax.numpy as jnp
from jax import lax
from jax.experimental import pallas as pl
from jax.experimental.pallas import tpu as pltpu
from jax.sharding import Mesh, PartitionSpec as P

LANES = 128
SUB = 8
CHUNK = 128
STEP = 256
SUMS = 4

NT = (((1,), (1,)), ((), ()))


def tile_kernel(
    n_core, n_col, side, count_s, rows_h, cols_h, ener_h, tiles, *refs,
):
    gath, refs = refs[:n_core], refs[n_core:]
    (own_ref, send_ref, rest_ref, rows_s, cols_s, ener,
     buf, table, picked, select, part, sems, small, *acc) = refs
    n_far, kvec, own = gath[0].shape
    slots = tiles.shape[0]
    blk_own = own // side
    per = LANES // side
    n_chunk = tiles.shape[1] // LANES
    my_far, my_core, my_col = (lax.axis_index(name) for name in ("far", "core", "col"))

    copies = [
        pltpu.make_async_copy(src, dst, small.at[i])
        for i, (src, dst) in enumerate(
            ((cols_h, cols_s), (rows_h, rows_s), (ener_h, ener))
        )
    ]
    for copy in copies:
        copy.start()

    def tile_copy(ch):
        span = pl.ds(pl.multiple_of(ch * CHUNK, CHUNK), CHUNK)
        return pltpu.make_async_copy(tiles.at[span], buf.at[span], sems.at[ch])

    count = count_s[0]
    used = (count + CHUNK - 1) // CHUNK

    def ask(ch):
        @pl.when(ch < used)
        def _():
            tile_copy(ch).start()

    ahead = STEP // CHUNK
    for ch in range(ahead):
        ask(ch)

    lane = lax.broadcasted_iota(jnp.int32, (kvec, LANES), 1)
    low = lane < side
    zero = jnp.zeros((kvec, LANES), jnp.float32)

    for s in range(n_core):
        core = lax.rem(my_core + (n_core - s), n_core)
        for f in range(n_far):
            for p in range(own // LANES):
                x = gath[s][f, :, p * LANES:(p + 1) * LANES].astype(jnp.float32)
                y = pltpu.roll(x, side, 1)
                at = (f * n_core + core) * blk_own + p * per
                table[at] = jnp.where(low, x, y)
                table[at + 1] = jnp.where(low, y, x)
    n_blocks = n_far * n_core * blk_own
    table[n_blocks] = zero

    n_seg = acc[0].shape[0]
    width = n_chunk * SUB

    def clear(r, carry):
        for a in acc:
            a[r] = jnp.zeros(a.shape[1:], jnp.float32)
        return carry

    lax.fori_loop(0, n_seg, clear, 0)

    k_id = lax.broadcasted_iota(jnp.int32, (width, LANES), 0)
    n_id = lax.broadcasted_iota(jnp.int32, (width, LANES), 1)
    base_id = n_id - per * (k_id // SUB)
    for par in range(per):
        for jp in range(per):
            at = (par * per + jp) * width
            hit = (base_id == side * par + jp).astype(jnp.float32)
            select[at:at + width, :] = hit.astype(jnp.bfloat16)

    rows_of = per * kvec

    def product(base, half, x, check):
        xh = x[half * SUB:(half + 1) * SUB]
        w = jnp.concatenate(
            [xh[:, c * LANES:(c + 1) * LANES] for c in range(n_chunk)], axis=0
        ).astype(jnp.bfloat16)
        entries = []
        for t in range(SUB):
            slot = base + half * SUB + t
            at = cols_s[slot]
            entry = table[jnp.where(slot < count, at, n_blocks) if check else at]
            entries.append(jnp.where(low, entry, zero))
            entries.append(jnp.where(low, zero, entry))
        left = jnp.concatenate(entries, axis=0).astype(jnp.bfloat16)
        return jnp.dot(left, w.T, preferred_element_type=jnp.float32)

    lane_w = lax.broadcasted_iota(jnp.int32, (rows_of, width), 1) % SUB

    def accumulate(at, out):
        for t in range(SUB):
            r = rows_s[at + t]
            mine = jnp.where(lane_w == t, out[t * rows_of:(t + 1) * rows_of], 0.0)
            acc[t % len(acc)][r] += mine

    def step(first, slots_in, check):
        for i in range(slots_in // CHUNK):
            tile_copy(first // CHUNK + i).wait()
        waiting = None
        for q in range(slots_in // (2 * SUB)):
            base = pl.multiple_of(first + q * 2 * SUB, 2 * SUB)
            x = buf[pl.ds(base, 2 * SUB), :].astype(jnp.float32)
            for half in range(2):
                out = product(base, half, x, check)
                if waiting is not None:
                    accumulate(*waiting)
                waiting = (base + half * SUB, out)
        accumulate(*waiting)

    def full_step(i, carry):
        for ch in range(ahead):
            ask(1 + (i + 2) * ahead + ch)
        step(CHUNK + i * STEP, STEP, False)
        return carry

    def last_step(ch, carry):
        step(ch * CHUNK, CHUNK, True)
        return carry

    for ch in range(ahead, 1 + 2 * ahead):
        ask(ch)
    for copy in copies[:2]:
        copy.wait()
    head = (count >= CHUNK).astype(jnp.int32)

    @pl.when(head == 1)
    def _():
        step(0, CHUNK, False)

    full = jnp.maximum(count - CHUNK, 0) // STEP
    lax.fori_loop(0, full, full_step, 0)
    lax.fori_loop(head + full * ahead, used, last_step, 0)

    pairs = n_seg // per

    def pick(m, carry):
        pieces = []
        for par in range(per):
            total = acc[0][m * per + par]
            for other in acc[1:]:
                total = total + other[m * per + par]
            for jp in range(per):
                pieces.append(total[jp * kvec:(jp + 1) * kvec])
        a = jnp.concatenate(pieces, axis=1)
        hi = a.astype(jnp.bfloat16).astype(jnp.float32)
        both = jnp.concatenate([hi, a - hi], axis=0).astype(jnp.bfloat16)
        picked[pl.ds(pl.multiple_of(m * 2 * kvec, 2 * kvec), 2 * kvec), :] = both
        return carry

    lax.fori_loop(0, pairs, pick, 0)

    spread = jnp.dot(picked[...], select[...], preferred_element_type=jnp.float32)
    for m in range(pairs):
        at = m * 2 * kvec
        row = spread[at:at + kvec] + spread[at + kvec:at + 2 * kvec]
        c, lane0 = divmod(m * LANES, own)
        part[c, :, lane0:lane0 + LANES] = row

    copies[2].wait()
    own_ref[...] = part[my_col] + ener[...] * gath[0][my_far].astype(jnp.float32)
    for s in range(1, n_col):
        share = part[lax.rem(my_col + s, n_col)]
        send_ref[s - 1] = share.astype(jnp.bfloat16)
        rest_ref[s - 1] = share


def tile_work(rows, cols, count, gath, n_col, ener, tiles):
    n_core = len(gath)
    n_far, kvec, own = gath[0].shape
    slots, area = tiles.shape
    side = math.isqrt(area)
    per = LANES // side
    blk_own = own // side
    n_seg = n_col * blk_own
    width = area // LANES * SUB
    vmem = pl.BlockSpec(memory_space=pltpu.VMEM)
    far_away = pl.BlockSpec(memory_space=pltpu.HBM)
    return pl.pallas_call(
        functools.partial(tile_kernel, n_core, n_col, side),
        out_shape=(
            jax.ShapeDtypeStruct((kvec, own), jnp.float32),
            jax.ShapeDtypeStruct((n_col - 1, kvec, own), jnp.bfloat16),
            jax.ShapeDtypeStruct((n_col - 1, kvec, own), jnp.float32),
        ),
        in_specs=[pl.BlockSpec(memory_space=pltpu.SMEM)] + [far_away] * 4 + [vmem] * n_core,
        out_specs=(vmem, vmem, vmem),
        scratch_shapes=[
            pltpu.SMEM((slots,), jnp.int32),
            pltpu.SMEM((slots,), jnp.int32),
            pltpu.VMEM((1, own), jnp.float32),
            pltpu.VMEM((slots, area), jnp.bfloat16),
            pltpu.VMEM((n_far * n_core * blk_own + 1, kvec, LANES), jnp.float32),
            pltpu.VMEM((n_seg // per * 2 * kvec, per * per * width), jnp.bfloat16),
            pltpu.VMEM((per * per * width, LANES), jnp.bfloat16),
            pltpu.VMEM((n_col, kvec, own), jnp.float32),
            pltpu.SemaphoreType.DMA((slots // CHUNK,)),
            pltpu.SemaphoreType.DMA((3,)),
        ] + [pltpu.VMEM((n_seg, per * kvec, width), jnp.float32)] * SUMS,
        compiler_params=pltpu.CompilerParams(vmem_limit_bytes=48 * 2**20),
        cost_estimate=pl.CostEstimate(
            flops=2 * slots * area * kvec, bytes_accessed=2 * slots * area, transcendentals=0
        ),
        name="tile_work",
    )(count, *[pltpu.with_memory_space_constraint(x, pltpu.HBM) for x in (rows, cols, ener, tiles)],
      *gath)


def terms_kernel(own, rest, vec, *refs):
    others, (terms_ref, wide) = refs[:-2], refs[-2:]
    n_col = len(others) + 1
    kvec = vec.shape[0]

    def outer(share, seg):
        return lax.dot_general(
            share, seg[...].astype(jnp.float32), NT,
            precision=lax.Precision.HIGHEST, preferred_element_type=jnp.float32,
        )

    terms = outer(own[...], vec)
    for s in range(1, n_col):
        terms = terms + outer(rest[s - 1], others[n_col - s - 1])
    wide[...] = jnp.zeros(wide.shape, jnp.float32)
    wide[:, :kvec] = terms
    spaced = pltpu.roll(wide[...], 0, 1, stride=kvec, stride_axis=0)
    terms_ref[...] = jnp.sum(spaced, axis=0, keepdims=True)


def gram_terms(own, rest, vectors, others):
    vmem = pl.BlockSpec(memory_space=pltpu.VMEM)
    return pl.pallas_call(
        terms_kernel,
        out_shape=jax.ShapeDtypeStruct((1, LANES), jnp.float32),
        in_specs=[vmem] * (3 + len(others)),
        out_specs=vmem,
        scratch_shapes=[pltpu.VMEM((vectors.shape[0], LANES), jnp.float32)],
        compiler_params=pltpu.CompilerParams(vmem_limit_bytes=4 * 2**20),
        name="gram_terms",
    )(own, rest, vectors, *others)


def finish_kernel(scale, base, gram_parts, vec, *refs):
    got, (product, residual) = refs[:-2], refs[-2:]
    whole = base[...]
    for piece in got:
        whole = whole + piece[...].astype(jnp.float32)
    product[...] = whole.astype(jnp.bfloat16)
    flat = gram_parts[0]
    for i in range(1, gram_parts.shape[0]):
        flat = flat + gram_parts[i]
    kvec = vec.shape[0]
    lane = lax.broadcasted_iota(jnp.int32, (kvec, LANES), 1)
    first = kvec * lax.broadcasted_iota(jnp.int32, (kvec, LANES), 0)
    wide = jnp.broadcast_to(flat * scale, (kvec, LANES))
    vec32 = vec[...].astype(jnp.float32)
    for a in range(kvec):
        column = jnp.sum(jnp.where(lane == first + a, wide, 0.0), axis=1, keepdims=True)
        whole = whole - column * vec32[a:a + 1, :]
    residual[...] = whole


def finish(scale, base, gram_parts, vectors, got):
    vmem = pl.BlockSpec(memory_space=pltpu.VMEM)
    return pl.pallas_call(
        functools.partial(finish_kernel, scale),
        out_shape=(
            jax.ShapeDtypeStruct(vectors.shape, jnp.bfloat16),
            jax.ShapeDtypeStruct(vectors.shape, jnp.float32),
        ),
        in_specs=[vmem] * (3 + len(got)),
        out_specs=(vmem, vmem),
        compiler_params=pltpu.CompilerParams(vmem_limit_bytes=4 * 2**20),
        name="finish",
    )(base, gram_parts, vectors, *got)


def from_all(x, axis):
    size = lax.axis_size(axis)
    got = [x]
    for s in range(1, size):
        got.append(lax.ppermute(x, axis, [(i, (i + s) % size) for i in range(size)]))
    return got


def per_device(vectors, energies, tiles, tile_rows, tile_cols, tile_count):
    kvec, own = vectors.shape
    n_col = lax.axis_size("col")
    copies = jnp.broadcast_to(vectors[None], (lax.axis_size("far"), kvec, own))
    gath = lax.all_to_all(copies, "far", 0, 0)
    gath = from_all(gath, "core")
    base, send, rest = tile_work(
        tile_rows, tile_cols, tile_count, gath, n_col, energies[None, :], tiles
    )
    got = [
        lax.ppermute(send[s - 1], "col", [(c, (c + s) % n_col) for c in range(n_col)])
        for s in range(1, n_col)
    ]
    others = from_all(vectors, "col")[1:]
    members = lax.axis_size(("far", "core", "col"))
    terms = gram_terms(base, rest, vectors, others)
    terms = jnp.broadcast_to(terms[None], (members,) + terms.shape)
    gram_parts = lax.all_to_all(terms, ("col", "core", "far"), 0, 0)
    return finish(1.0 / (members * own), base, gram_parts, vectors, got)


def solution(mesh):
    n_row, n_col = mesh.devices.shape
    n_core = 2 if n_row % 2 == 0 else 1
    split = ("far", "core", "col")
    chips = Mesh(mesh.devices.reshape(n_row // n_core, n_core, n_col), split)
    in_specs = (P(None, split), P(split), P(split, None), P(split), P(split), P(split))
    out_specs = (P(None, split), P(None, split))
    return jax.shard_map(
        per_device, mesh=chips, in_specs=in_specs, out_specs=out_specs, check_vma=False
    )
```

```python
import functools
import math

import jax
import jax.numpy as jnp
from jax import lax
from jax.experimental import pallas as pl
from jax.experimental.pallas import tpu as pltpu
from jax.sharding import Mesh, PartitionSpec as P

LANES = 128
SUB = 8
CHUNK = 128
STEP = 256
SUMS = 2

NT = (((1,), (1,)), ((), ()))


def tile_kernel(
    n_core, n_col, side, count_s, rows_h, cols_h, ener_h, tiles, *refs,
):
    gath, refs = refs[:n_core], refs[n_core:]
    (own_ref, send_ref, rest_ref, rows_s, cols_s, ener,
     buf, table, picked, select, part, sems, small, *acc) = refs
    n_far, kvec, own = gath[0].shape
    slots = tiles.shape[0]
    blk_own = own // side
    per = LANES // side
    n_chunk = tiles.shape[1] // LANES
    my_far, my_core, my_col = (lax.axis_index(name) for name in ("far", "core", "col"))

    copies = [
        pltpu.make_async_copy(src, dst, small.at[i])
        for i, (src, dst) in enumerate(
            ((cols_h, cols_s), (rows_h, rows_s), (ener_h, ener))
        )
    ]
    for copy in copies:
        copy.start()

    def tile_copy(ch):
        span = pl.ds(pl.multiple_of(ch * CHUNK, CHUNK), CHUNK)
        return pltpu.make_async_copy(tiles.at[span], buf.at[span], sems.at[ch])

    count = count_s[0]
    used = (count + CHUNK - 1) // CHUNK

    def ask(ch):
        @pl.when(ch < used)
        def _():
            tile_copy(ch).start()

    ahead = STEP // CHUNK
    for ch in range(ahead):
        ask(ch)

    lane = lax.broadcasted_iota(jnp.int32, (kvec, LANES), 1)
    low = lane < side
    zero = jnp.zeros((kvec, LANES), jnp.float32)

    for s in range(n_core):
        core = lax.rem(my_core + (n_core - s), n_core)
        for f in range(n_far):
            for p in range(own // LANES):
                x = gath[s][f, :, p * LANES:(p + 1) * LANES].astype(jnp.float32)
                y = pltpu.roll(x, side, 1)
                at = (f * n_core + core) * blk_own + p * per
                table[at] = jnp.where(low, x, y)
                table[at + 1] = jnp.where(low, y, x)
    n_blocks = n_far * n_core * blk_own
    table[n_blocks] = zero

    n_seg = acc[0].shape[0]
    width = n_chunk * SUB

    def clear(r, carry):
        for a in acc:
            a[r] = jnp.zeros(a.shape[1:], jnp.float32)
        return carry

    lax.fori_loop(0, n_seg, clear, 0)

    k_id = lax.broadcasted_iota(jnp.int32, (width, LANES), 0)
    n_id = lax.broadcasted_iota(jnp.int32, (width, LANES), 1)
    base_id = n_id - per * (k_id // SUB)
    for par in range(per):
        for jp in range(per):
            at = (par * per + jp) * width
            hit = (base_id == side * par + jp).astype(jnp.float32)
            select[at:at + width, :] = hit.astype(jnp.bfloat16)

    rows_of = per * kvec

    def product(base, half, x, check):
        xh = x[half * SUB:(half + 1) * SUB]
        w = jnp.concatenate(
            [xh[:, c * LANES:(c + 1) * LANES] for c in range(n_chunk)], axis=0
        ).astype(jnp.bfloat16)
        entries = []
        for t in range(SUB):
            slot = base + half * SUB + t
            at = cols_s[slot]
            entry = table[jnp.where(slot < count, at, n_blocks) if check else at]
            entries.append(jnp.where(low, entry, zero))
            entries.append(jnp.where(low, zero, entry))
        left = jnp.concatenate(entries, axis=0).astype(jnp.bfloat16)
        return jnp.dot(left, w.T, preferred_element_type=jnp.float32)

    lane_w = lax.broadcasted_iota(jnp.int32, (rows_of, width), 1) % SUB

    def accumulate(at, out):
        for t in range(SUB):
            r = rows_s[at + t]
            mine = jnp.where(lane_w == t, out[t * rows_of:(t + 1) * rows_of], 0.0)
            acc[t % len(acc)][r] += mine

    def step(first, slots_in, check):
        for i in range(slots_in // CHUNK):
            tile_copy(first // CHUNK + i).wait()
        waiting = None
        for q in range(slots_in // (2 * SUB)):
            base = pl.multiple_of(first + q * 2 * SUB, 2 * SUB)
            x = buf[pl.ds(base, 2 * SUB), :].astype(jnp.float32)
            for half in range(2):
                out = product(base, half, x, check)
                if waiting is not None:
                    accumulate(*waiting)
                waiting = (base + half * SUB, out)
        accumulate(*waiting)

    def full_step(i, carry):
        for ch in range(ahead):
            ask(1 + (i + 2) * ahead + ch)
        step(CHUNK + i * STEP, STEP, False)
        return carry

    def last_step(ch, carry):
        step(ch * CHUNK, CHUNK, True)
        return carry

    for ch in range(ahead, 1 + 2 * ahead):
        ask(ch)
    for copy in copies[:2]:
        copy.wait()
    head = (count >= CHUNK).astype(jnp.int32)

    @pl.when(head == 1)
    def _():
        step(0, CHUNK, False)

    full = jnp.maximum(count - CHUNK, 0) // STEP
    lax.fori_loop(0, full, full_step, 0)
    lax.fori_loop(head + full * ahead, used, last_step, 0)

    pairs = n_seg // per

    def pick(m, carry):
        pieces = []
        for par in range(per):
            total = acc[0][m * per + par]
            for other in acc[1:]:
                total = total + other[m * per + par]
            for jp in range(per):
                pieces.append(total[jp * kvec:(jp + 1) * kvec])
        a = jnp.concatenate(pieces, axis=1)
        hi = a.astype(jnp.bfloat16).astype(jnp.float32)
        both = jnp.concatenate([hi, a - hi], axis=0).astype(jnp.bfloat16)
        picked[pl.ds(pl.multiple_of(m * 2 * kvec, 2 * kvec), 2 * kvec), :] = both
        return carry

    lax.fori_loop(0, pairs, pick, 0)

    spread = jnp.dot(picked[...], select[...], preferred_element_type=jnp.float32)
    for m in range(pairs):
        at = m * 2 * kvec
        row = spread[at:at + kvec] + spread[at + kvec:at + 2 * kvec]
        c, lane0 = divmod(m * LANES, own)
        part[c, :, lane0:lane0 + LANES] = row

    copies[2].wait()
    own_ref[...] = part[my_col] + ener[...] * gath[0][my_far].astype(jnp.float32)
    for s in range(1, n_col):
        share = part[lax.rem(my_col + s, n_col)]
        send_ref[s - 1] = share.astype(jnp.bfloat16)
        rest_ref[s - 1] = share


def tile_work(rows, cols, count, gath, n_col, ener, tiles):
    n_core = len(gath)
    n_far, kvec, own = gath[0].shape
    slots, area = tiles.shape
    side = math.isqrt(area)
    per = LANES // side
    blk_own = own // side
    n_seg = n_col * blk_own
    width = area // LANES * SUB
    vmem = pl.BlockSpec(memory_space=pltpu.VMEM)
    far_away = pl.BlockSpec(memory_space=pltpu.HBM)
    return pl.pallas_call(
        functools.partial(tile_kernel, n_core, n_col, side),
        out_shape=(
            jax.ShapeDtypeStruct((kvec, own), jnp.float32),
            jax.ShapeDtypeStruct((n_col - 1, kvec, own), jnp.bfloat16),
            jax.ShapeDtypeStruct((n_col - 1, kvec, own), jnp.float32),
        ),
        in_specs=[pl.BlockSpec(memory_space=pltpu.SMEM)] + [far_away] * 4 + [vmem] * n_core,
        out_specs=(vmem, vmem, vmem),
        scratch_shapes=[
            pltpu.SMEM((slots,), jnp.int32),
            pltpu.SMEM((slots,), jnp.int32),
            pltpu.VMEM((1, own), jnp.float32),
            pltpu.VMEM((slots, area), jnp.bfloat16),
            pltpu.VMEM((n_far * n_core * blk_own + 1, kvec, LANES), jnp.float32),
            pltpu.VMEM((n_seg // per * 2 * kvec, per * per * width), jnp.bfloat16),
            pltpu.VMEM((per * per * width, LANES), jnp.bfloat16),
            pltpu.VMEM((n_col, kvec, own), jnp.float32),
            pltpu.SemaphoreType.DMA((slots // CHUNK,)),
            pltpu.SemaphoreType.DMA((3,)),
        ] + [pltpu.VMEM((n_seg, per * kvec, width), jnp.float32)] * SUMS,
        compiler_params=pltpu.CompilerParams(vmem_limit_bytes=48 * 2**20),
        cost_estimate=pl.CostEstimate(
            flops=2 * slots * area * kvec, bytes_accessed=2 * slots * area, transcendentals=0
        ),
        name="tile_work",
    )(count, *[pltpu.with_memory_space_constraint(x, pltpu.HBM) for x in (rows, cols, ener, tiles)],
      *gath)


def terms_kernel(own, rest, vec, *refs):
    others, (terms_ref, wide) = refs[:-2], refs[-2:]
    n_col = len(others) + 1
    kvec = vec.shape[0]

    def outer(share, seg):
        return lax.dot_general(
            share, seg[...].astype(jnp.float32), NT,
            precision=lax.Precision.HIGHEST, preferred_element_type=jnp.float32,
        )

    terms = outer(own[...], vec)
    for s in range(1, n_col):
        terms = terms + outer(rest[s - 1], others[n_col - s - 1])
    wide[...] = jnp.zeros(wide.shape, jnp.float32)
    wide[:, :kvec] = terms
    spaced = pltpu.roll(wide[...], 0, 1, stride=kvec, stride_axis=0)
    terms_ref[...] = jnp.sum(spaced, axis=0, keepdims=True)


def gram_terms(own, rest, vectors, others):
    vmem = pl.BlockSpec(memory_space=pltpu.VMEM)
    return pl.pallas_call(
        terms_kernel,
        out_shape=jax.ShapeDtypeStruct((1, LANES), jnp.float32),
        in_specs=[vmem] * (3 + len(others)),
        out_specs=vmem,
        scratch_shapes=[pltpu.VMEM((vectors.shape[0], LANES), jnp.float32)],
        compiler_params=pltpu.CompilerParams(vmem_limit_bytes=4 * 2**20),
        name="gram_terms",
    )(own, rest, vectors, *others)


def finish_kernel(scale, base, gram_parts, vec, *refs):
    got, (product, residual) = refs[:-2], refs[-2:]
    whole = base[...]
    for piece in got:
        whole = whole + piece[...].astype(jnp.float32)
    product[...] = whole.astype(jnp.bfloat16)
    flat = gram_parts[0]
    for i in range(1, gram_parts.shape[0]):
        flat = flat + gram_parts[i]
    kvec = vec.shape[0]
    lane = lax.broadcasted_iota(jnp.int32, (kvec, LANES), 1)
    first = kvec * lax.broadcasted_iota(jnp.int32, (kvec, LANES), 0)
    wide = jnp.broadcast_to(flat * scale, (kvec, LANES))
    vec32 = vec[...].astype(jnp.float32)
    for a in range(kvec):
        column = jnp.sum(jnp.where(lane == first + a, wide, 0.0), axis=1, keepdims=True)
        whole = whole - column * vec32[a:a + 1, :]
    residual[...] = whole


def finish(scale, base, gram_parts, vectors, got):
    vmem = pl.BlockSpec(memory_space=pltpu.VMEM)
    return pl.pallas_call(
        functools.partial(finish_kernel, scale),
        out_shape=(
            jax.ShapeDtypeStruct(vectors.shape, jnp.bfloat16),
            jax.ShapeDtypeStruct(vectors.shape, jnp.float32),
        ),
        in_specs=[vmem] * (3 + len(got)),
        out_specs=(vmem, vmem),
        compiler_params=pltpu.CompilerParams(vmem_limit_bytes=4 * 2**20),
        name="finish",
    )(base, gram_parts, vectors, *got)


def from_all(x, axis):
    size = lax.axis_size(axis)
    got = [x]
    for s in range(1, size):
        got.append(lax.ppermute(x, axis, [(i, (i + s) % size) for i in range(size)]))
    return got


def per_device(vectors, energies, tiles, tile_rows, tile_cols, tile_count):
    kvec, own = vectors.shape
    n_col = lax.axis_size("col")
    copies = jnp.broadcast_to(vectors[None], (lax.axis_size("far"), kvec, own))
    gath = lax.all_to_all(copies, "far", 0, 0)
    gath = from_all(gath, "core")
    base, send, rest = tile_work(
        tile_rows, tile_cols, tile_count, gath, n_col, energies[None, :], tiles
    )
    got = [
        lax.ppermute(send[s - 1], "col", [(c, (c + s) % n_col) for c in range(n_col)])
        for s in range(1, n_col)
    ]
    others = from_all(vectors, "col")[1:]
    members = lax.axis_size(("far", "core", "col"))
    terms = gram_terms(base, rest, vectors, others)
    terms = jnp.broadcast_to(terms[None], (members,) + terms.shape)
    gram_parts = lax.all_to_all(terms, ("far", "core", "col"), 0, 0)
    return finish(1.0 / (members * own), base, gram_parts, vectors, got)


def solution(mesh):
    n_row, n_col = mesh.devices.shape
    n_core = 2 if n_row % 2 == 0 else 1
    split = ("far", "core", "col")
    chips = Mesh(mesh.devices.reshape(n_row // n_core, n_core, n_col), split)
    in_specs = (P(None, split), P(split), P(split, None), P(split), P(split), P(split))
    out_specs = (P(None, split), P(None, split))
    return jax.shard_map(
        per_device, mesh=chips, in_specs=in_specs, out_specs=out_specs, check_vma=False
    )
```
